32 devices in a mesh: dp: 8 (over z, x), head: 4 (over y, core).
Axes of the slice: x: 2, y: 2, z: 4, core: 2. Of those that a mesh axis runs over, the one named last changes fastest.
Arguments:
- tokens: bfloat16 [32, 2048, 512], P('dp', 'head'), may hold values from -6 to 6
- cotangent: bfloat16 [32, 2048, 512], P('dp', 'head'), may hold values from -6 to 6
- carry_state: float32 [32, 8, 256, 64], P('dp', 'head'), may hold values from -6 to 6
- carry_norm: float32 [32, 8, 256], P('dp', 'head'), may hold values from -6 to 6
- random_maps: float32 [8, 64, 128], P('head'), may hold values from -9 to 9
- query_weight: bfloat16 [512, 512], P(None, 'head'), may hold values from -0.25 to 0.25
- key_weight: bfloat16 [512, 512], P(None, 'head'), may hold values from -0.25 to 0.25
- value_weight: bfloat16 [512, 512], P(None, 'head'), may hold values from -0.25 to 0.25
- gate_weight: bfloat16 [512, 8], P(None, 'head'), may hold values from -0.25 to 0.25
- gate_bias: float32 [8], P('head'), may hold values from 3 to 8
- mixing_weight: bfloat16 [512, 512], P('head'), may hold values from -0.75 to 0.75
- mixing_bias: float32 [512], replicated, may hold values from -3 to 3
- norm_gain: float32 [512], replicated, may hold values from 0.5 to 1.5
- norm_bias: float32 [512], replicated, may hold values from -3 to 3
- up_weight: bfloat16 [512, 2048], replicated, may hold values from -0.25 to 0.25
- up_bias: float32 [2048], replicated, may hold values from -3 to 3
- down_weight: bfloat16 [2048, 512], replicated, may hold values from -0.125 to 0.125
- down_bias: float32 [512], replicated, may hold values from -3 to 3
Outputs:
- layer_out: bfloat16 [32, 2048, 512], P('dp', 'head')
- tokens_grad: float32 [32, 2048, 512], P('dp', 'head')
- penalty: float32 [], replicated
- query_grad: float32 [512, 512], P(None, 'head')
- key_grad: float32 [512, 512], P(None, 'head')
- value_grad: float32 [512, 512], P(None, 'head')
- gate_grad: float32 [512, 8], P(None, 'head')
- gate_bias_grad: float32 [8], P('head')
- mixing_grad: float32 [512, 512], P('head')
- mixing_bias_grad: float32 [512], replicated
- gain_grad: float32 [512], replicated
- norm_bias_grad: float32 [512], replicated
- up_grad: float32 [512, 2048], replicated
- up_bias_grad: float32 [2048], replicated
- down_grad: float32 [2048, 512], replicated
- down_bias_grad: float32 [512], replicated
The draws below stay inside these ranges and needn't reach their ends.
All inputs are finite; a program needn't handle non-finite values.
Results may differ from the reference program's by a relative error of at most 0.02.
Values may be sent and summed in bfloat16 or wider, within the bound.
No kernel may reach another device: no remote copies, remote signals or barrier semaphores. Data moves between devices by JAX's collectives and lax.ppermute only.
A program may use at most 320 MiB of HBM per device.

```python
import math
import jax
import jax.numpy as jnp
from jax import lax

D = 512
HEADS = 8
HD = 64
NF = 128
FF = 2048
LEN = 2048
CH = 256
ROWS = 32


def steps_of(stream_key, shape, cuts, low, largest):
    def one(axis_at, parts):
        heights = jax.random.uniform(jax.random.fold_in(jax.random.fold_in(stream_key, 6), axis_at), (parts,), jnp.float32, low / len(cuts), largest / len(cuts))
        return jnp.repeat(jnp.exp(heights), shape[axis_at] // parts).reshape((-1,) + (1,) * (len(shape) - axis_at - 1))

    level = one(*cuts[0])
    for cut in cuts[1:]:
        level = level * one(*cut)
    return level


def scatter_about(key, shape, deviation, most, cuts=(), kind=jnp.bfloat16):
    values = jax.random.normal(key, shape, jnp.float32) * deviation
    if len(cuts) > 0:
        values = steps_of(key, shape, cuts, -0.22, 0.18) * values
    return jnp.clip(values, min=-most, max=most).astype(kind)


def setup_inputs(seed: int = 0) -> dict:
    splits = jax.random.split(jax.random.key(seed), 19)
    return {
        "tokens": scatter_about(splits[0], (ROWS, LEN, D), 1.0, 6.0, ((0, 8), (1, 4))),
        "cotangent": scatter_about(splits[1], (ROWS, LEN, D), 1.0, 6.0, ((0, 8), (1, 4))),
        "carry_state": scatter_about(splits[2], (ROWS, HEADS, 2 * NF, HD), 1.0, 6.0, ((0, 8), (1, 4)), jnp.float32),
        "carry_norm": scatter_about(splits[3], (ROWS, HEADS, 2 * NF), 1.0, 6.0, ((0, 8), (1, 4)), jnp.float32),
        "random_maps": scatter_about(splits[4], (HEADS, HD, NF), 1.5, 9.0, ((0, 4),), jnp.float32),
        "query_weight": scatter_about(splits[5], (D, HEADS * HD), D ** -0.5, 0.25, ((1, 4),)),
        "key_weight": scatter_about(splits[6], (D, HEADS * HD), D ** -0.5, 0.25, ((1, 4),)),
        "value_weight": scatter_about(splits[7], (D, HEADS * HD), D ** -0.5, 0.25, ((1, 4),)),
        "gate_weight": scatter_about(splits[8], (D, HEADS), D ** -0.5, 0.25, ((1, 4),)),
        "gate_bias": jnp.clip(3.0 + 5.0 * jax.random.uniform(splits[9], (HEADS,), jnp.float32) ** steps_of(splits[9], (HEADS,), ((0, 4),), -0.2, 0.2), 3.0, 8.0),
        "mixing_weight": scatter_about(splits[10], (HEADS * HD, D), HD ** -0.5, 0.75, ((0, 4),)),
        "mixing_bias": scatter_about(splits[11], (D,), 0.5, 3.0, (), jnp.float32),
        "norm_gain": jnp.clip(1.0 + 0.1 * jax.random.normal(splits[12], (D,), jnp.float32), 0.5, 1.5),
        "norm_bias": scatter_about(splits[13], (D,), 0.5, 3.0, (), jnp.float32),
        "up_weight": scatter_about(splits[14], (D, FF), D ** -0.5, 0.25),
        "up_bias": scatter_about(splits[15], (FF,), 0.5, 3.0, (), jnp.float32),
        "down_weight": scatter_about(splits[16], (FF, D), FF ** -0.5, 0.125),
        "down_bias": scatter_about(splits[17], (D,), 0.5, 3.0, (), jnp.float32),
    }


HIGHEST = lax.Precision.HIGHEST
penalty_weight = 32.0
target_gate = 0.9

@jax.custom_vjp
def low(v):
    return lax.optimization_barrier(v.astype(jnp.bfloat16)).astype(jnp.float32)

@jax.custom_vjp
def low_back(v):
    return v

def low_keep(v):
    return (low(v), None)

def low_pass(kept, grad):
    return (grad,)

def back_keep(v):
    return (v, None)

def back_low(kept, grad):
    return (low(grad),)
low.defvjp(low_keep, low_pass)
low_back.defvjp(back_keep, back_low)

def rounded(values):
    return low_back(low(values))

def featurize(vectors, maps):
    scaled = vectors * lax.rsqrt(lax.optimization_barrier(jnp.sum(vectors * vectors, -1, keepdims=True)) + 1e-06)
    angles = jnp.einsum('bhtd,hdf->bhtf', scaled, maps, precision=HIGHEST)
    return jnp.concatenate([jnp.sin(angles), jnp.cos(angles)], -1) * (1.0 / math.sqrt(maps.shape[-1]))

def block_step(carry, inputs):
    state, normer = carry
    feat_query, feat_key, values, gate_pre = inputs
    size = gate_pre.shape[-1]
    place = jnp.arange(size)
    lower = place[:, None] >= place[None, :]
    cumul = jnp.cumsum(jax.nn.log_sigmoid(gate_pre), -1)
    keep = jax.nn.sigmoid(-gate_pre)
    differ = cumul[..., :, None] - cumul[..., None, :]
    decay = jnp.where(lower, jnp.exp(jnp.where(lower, differ, 0.0)), 0.0) * keep[..., None, :]
    scores = jnp.einsum('bhtf,bhsf->bhts', feat_query, feat_key, precision=HIGHEST) * decay
    carried = jnp.exp(cumul)
    numer = jnp.einsum('bhts,bhsd->bhtd', rounded(scores), values, precision=HIGHEST)
    numer = numer + carried[..., None] * jnp.einsum('bhtf,bhfd->bhtd', feat_query, rounded(state), precision=HIGHEST)
    inner = lax.optimization_barrier(jnp.sum(scores, -1)) + carried * jnp.einsum('bhtf,bhf->bht', feat_query, normer, precision=HIGHEST)
    output = numer * lax.rsqrt(inner * inner + 1.0)[..., None]
    tail = jnp.exp(cumul[..., -1:] - cumul) * keep
    weighted = feat_key * tail[..., None]
    last = carried[..., -1]
    state_next = last[..., None, None] * state + jnp.einsum('bhsf,bhsd->bhfd', rounded(weighted), values, precision=HIGHEST)
    normer_next = last[..., None] * normer + lax.optimization_barrier(jnp.sum(weighted, -2))
    return ((state_next, normer_next), output)

def attend(query, keys, values, gate_pre, start_state, start_norm, maps, block):
    batch, heads, length, head_size = query.shape
    feat_query = rounded(featurize(query, maps))
    feat_key = rounded(featurize(keys, maps))
    values = rounded(values)
    number = length // block

    def split(array):
        return jnp.moveaxis(array.reshape((batch, heads, number, block) + array.shape[3:]), 2, 0)
    _, outputs = lax.scan(jax.checkpoint(block_step), (start_state, start_norm), (split(feat_query), split(feat_key), split(values), split(gate_pre)))
    return jnp.moveaxis(outputs, 0, 2).reshape(batch, heads, length, head_size)

def layer_norm(values):
    center = values - lax.optimization_barrier(jnp.mean(values, -1, keepdims=True))
    spread = lax.optimization_barrier(jnp.mean(center * center, -1, keepdims=True))
    return center * lax.rsqrt(spread + 1e-05)

def layer(params, inputs, start_state, start_norm, maps):
    query_weight, key_weight, value_weight, gate_weight, gate_bias, mixing_weight, mixing_bias, norm_gain, norm_bias, up_weight, up_bias, down_weight, down_bias = params
    batch = inputs.shape[0]

    def heads_first(matrix):
        return matrix.reshape(batch, LEN, HEADS, HD).transpose(0, 2, 1, 3)
    query = low_back(heads_first(jnp.einsum('bld,de->ble', inputs, query_weight, precision=HIGHEST)))
    keys = low_back(heads_first(jnp.einsum('bld,de->ble', inputs, key_weight, precision=HIGHEST)))
    values = low_back(heads_first(jnp.einsum('bld,de->ble', inputs, value_weight, precision=HIGHEST)))
    gate_pre = low_back(jnp.einsum('bld,dh->blh', inputs, gate_weight, precision=HIGHEST) + gate_bias)
    gate_pre = gate_pre.transpose(0, 2, 1)
    heads_out = attend(query, keys, values, gate_pre, start_state, start_norm, maps, CH)
    heads_out = low(heads_out).transpose(0, 2, 1, 3).reshape(batch, LEN, HEADS * HD)
    mixed = low_back(jnp.einsum('ble,ed->bld', heads_out, mixing_weight, precision=HIGHEST))
    residual = inputs + mixed + mixing_bias
    normal = low(layer_norm(residual) * norm_gain + norm_bias)
    hidden = low_back(jnp.einsum('bld,df->blf', normal, up_weight, precision=HIGHEST) + up_bias)
    activated = low(jax.nn.gelu(hidden))
    result = residual + jnp.einsum('blf,fd->bld', activated, down_weight, precision=HIGHEST) + down_bias
    gate_sum = jnp.sum(jax.nn.sigmoid(gate_pre))
    return (result, gate_sum)

def reference(tokens, cotangent, carry_state, carry_norm, random_maps, query_weight, key_weight, value_weight, gate_weight, gate_bias, mixing_weight, mixing_bias, norm_gain, norm_bias, up_weight, up_bias, down_weight, down_bias):
    params = tuple((item.astype(jnp.float32) for item in (query_weight, key_weight, value_weight, gate_weight, gate_bias, mixing_weight, mixing_bias, norm_gain, norm_bias, up_weight, up_bias, down_weight, down_bias)))
    inputs = tokens.astype(jnp.float32)
    upstream = cotangent.astype(jnp.float32)

    def gate_mean(weight, bias):
        pre_all = jnp.einsum('rld,dh->rlh', inputs, weight, precision=HIGHEST) + bias
        return jnp.mean(jax.nn.sigmoid(pre_all))
    mean_gate, unused_back = jax.vjp(gate_mean, params[3], params[4])
    factor = 2.0 * penalty_weight * (mean_gate - target_gate) / HEADS
    pair = math.gcd(ROWS, 2)
    number = ROWS // pair

    def regroup(array):
        return array.reshape((number, pair) + array.shape[1:])

    def one_group(total, group):
        inputs_group, upstream_group, state_group, norm_group = group

        def run(weights, values):
            return layer(weights, values, state_group, norm_group, random_maps)
        (result, gate_sum), back = jax.vjp(run, params, inputs_group)
        weight_grads, input_grads = back((upstream_group, factor.astype(gate_sum.dtype)))
        total = jax.tree.map(jnp.add, total, weight_grads)
        return (total, (result, input_grads))
    zeros = jax.tree.map(jnp.zeros_like, params)
    totals, (results, input_grads) = lax.scan(one_group, zeros, (regroup(inputs), regroup(upstream), regroup(carry_state), regroup(carry_norm)))
    layer_out = results.reshape(ROWS, LEN, D).astype(jnp.bfloat16)
    tokens_grad = input_grads.reshape(ROWS, LEN, D)
    penalty = penalty_weight * (mean_gate - target_gate) * (mean_gate - target_gate)
    query_grad, key_grad, value_grad, gate_grad, gate_bias_grad, mixing_grad, mixing_bias_grad, gain_grad, norm_bias_grad, up_grad, up_bias_grad, down_grad, down_bias_grad = totals
    return (layer_out, tokens_grad, penalty, query_grad, key_grad, value_grad, gate_grad, gate_bias_grad, mixing_grad, mixing_bias_grad, gain_grad, norm_bias_grad, up_grad, up_bias_grad, down_grad, down_bias_grad)
```

```python
import functools
import math

import jax
import jax.numpy as jnp
import numpy as np
from jax import lax
from jax.experimental import pallas as pl
from jax.experimental.pallas import tpu as pltpu
from jax.sharding import PartitionSpec as P

CH = 256
HD = 64
NF = 128
FW = 2 * NF
SR = 80
GR = 16
TILE = 512

penalty_weight = 32.0
target_gate = 0.9
LOG2E = 1.4426950408889634
SIN_POLY = (
    3.1415925800446116,
    -5.16770687892007,
    2.5500313771889287,
    -0.5980451736320438,
    0.07722012807955428,
)
COS_POLY = (
    0.9999999534665498,
    -4.934792858660313,
    4.058411913867723,
    -1.3318801593312537,
    0.2196967947670672,
)
GELU_A = 0.7978845608028654
GELU_B = 0.044715

f32 = jnp.float32
bf16 = jnp.bfloat16


def dot(a, b):
    return lax.dot_general(a, b, (((1,), (0,)), ((), ())), preferred_element_type=f32)


def dot_nt(a, b):
    return lax.dot_general(a, b, (((1,), (1,)), ((), ())), preferred_element_type=f32)


def dot_tn(a, b):
    return lax.dot_general(a, b, (((0,), (0,)), ((), ())), preferred_element_type=f32)


def split2(x):
    high = x.astype(bf16)
    return high, (x - high.astype(f32)).astype(bf16)


def split2_cat(x):
    return jnp.concatenate(split2(x), 1)


def split3_cat(x):
    high = x.astype(bf16)
    rest = x - high.astype(f32)
    mid = rest.astype(bf16)
    return jnp.concatenate([high, mid, (rest - mid.astype(f32)).astype(bf16)], 1)


def low_lanes(rows):
    return lax.broadcasted_iota(jnp.int32, (rows, 128), 1) < HD


def unit(u, ones2):
    inverse = lax.rsqrt(dot(split2_cat(u * u), ones2) + 1e-06)
    return u * inverse, inverse


def sin_cos(n, maps):
    high, rest = split2(n)
    turns = dot(jnp.concatenate([high, rest, high], 1), maps)
    r = turns - jnp.round(turns)
    u = r * r
    scale = math.sqrt(2.0 / math.sqrt(NF))
    s = SIN_POLY[4] * scale
    c = COS_POLY[4] * scale
    for i in (3, 2, 1, 0):
        s = s * u + SIN_POLY[i] * scale
        c = c * u + COS_POLY[i] * scale
    s = s * r
    return s * c, 1.0 / math.sqrt(NF) - s * s


def feature_back(n, inverse, angle_grad, maps_back, ones2):
    high, rest = split2(angle_grad)
    dn = dot(jnp.concatenate([high, rest, high], 1), maps_back)
    radial = dot(split2_cat(n * dn), ones2)
    return (dn - n * radial) * inverse


def expand(block, odd):
    state, norm = block[:HD], block[HD:SR]
    parts = [norm] * (HD // (SR - HD))
    return jnp.concatenate(parts + [state] if odd else [state] + parts, 0)


def shrink(block, odd):
    if odd:
        return jnp.concatenate([block[HD:], block[HD - (SR - HD) : HD]], 0)
    return block[:SR]


def clear(refs):
    for ref in refs:
        ref[...] = jnp.zeros_like(ref)


def collect(held, parts, index):
    for k, part in enumerate(parts):
        held[index ^ k] = part[...]


def block_pair(even, odd):
    none = jnp.zeros_like(even)
    return jnp.concatenate(
        [jnp.concatenate([even, none], 1), jnp.concatenate([none, odd], 1)], 0
    )


def keys_setup(held, here, wkv_ref, wvt, maps_ref, back_ref, gw_ref, gb):
    size = held.shape[0]
    width = wkv_ref.shape[0]
    inner = wvt.shape[0]
    at = width * here
    high, rest, gates, biases = [], [], [], []
    for d in range(size):
        if here == 2:
            lanes = slice(128 * d, 128 * d + 128)
            wkv_ref[:, lanes] = held[d, :width]
            wkv_ref[:, inner + 128 * d : inner + 128 * d + 128] = held[d, width : 2 * width]
            wvt[lanes, :] = held[d, width : 2 * width].T
        elif d % 2:
            lanes = slice(64 * d - 64, 64 * d + 64)
            one, two = held[d - 1, :width], held[d, :width]
            wkv_ref[:, lanes] = jnp.concatenate([one[:, :HD], two[:, :HD]], 1)
            values = jnp.concatenate([one[:, HD:], two[:, HD:]], 1)
            wkv_ref[:, inner + 64 * d - 64 : inner + 64 * d + 64] = values
            wvt[lanes, :] = values.T
        for i in range(here):
            first = at + HD * i
            high.append(held[d, first : first + HD])
            rest.append(held[d, first + HD * here : first + HD * here + HD])
        tail = held[d, at + 2 * HD * here :].astype(f32)
        for i in range(here):
            gates.append(
                jnp.concatenate([tail[4 * i + j : 4 * i + j + 1] for j in range(width // 128)], 1)
            )
            bias = sum(tail[4 * here + j : 4 * here + j + 1, i : i + 1] for j in range(3))
            biases.append(jnp.broadcast_to(bias, (1, CH)))
    for pair in range(len(high) // 2):
        top = block_pair(high[2 * pair], high[2 * pair + 1])
        low = block_pair(rest[2 * pair], rest[2 * pair + 1])
        maps_ref[pair] = jnp.concatenate([top, top, low], 0)
        back = ((top.astype(f32) + low.astype(f32)) * (2.0 * math.pi)).T
        top, low = split2(back)
        back_ref[pair] = jnp.concatenate([top, top, low], 0)
    heads = len(gates)
    gw_ref[...] = jnp.concatenate(gates + [jnp.zeros((GR - heads, width), f32)], 0).astype(bf16)
    gb[...] = jnp.concatenate(biases + [jnp.zeros((GR - heads, CH), f32)], 0)


def keys_body(*refs, size, here):
    parts = refs[:size]
    (
        index_ref,
        x_ref,
        ones_ref,
        tri_ref,
        phik_ref,
        v_ref,
        row_ref,
        col_ref,
        u_ref,
        end_ref,
        tot_ref,
        gsum_ref,
        wkv_ref,
        maps_ref,
        back_ref,
        gw_ref,
        acc,
        held,
        wvt_ref,
        gb_ref,
    ) = refs[size:]
    b, c = pl.program_id(0), pl.program_id(1)

    @pl.when(jnp.logical_and(b == 0, c == 0))
    def _():
        collect(held, parts, index_ref[0])
        keys_setup(held, here, wkv_ref, wvt_ref, maps_ref, back_ref, gw_ref, gb_ref)

    x = x_ref[...]
    kv = dot(x, wkv_ref[...])
    width = kv.shape[1] // 2
    keys = kv[:, :width]
    v_ref[...] = kv[:, width:].astype(bf16)
    vt = dot_nt(wvt_ref[...], x).astype(bf16)
    pre = dot_nt(gw_ref[...], x) + gb_ref[...]
    soft = jnp.log1p(jnp.exp(-jnp.abs(pre)))
    log_gate = -(jnp.maximum(-pre, 0.0) + soft)
    log_keep = -(jnp.maximum(pre, 0.0) + soft)
    gate = jnp.exp(log_gate)
    keep = jnp.exp(log_keep)
    cumul = dot(split3_cat(log_gate * LOG2E), tri_ref[...])
    shifted = cumul - log_keep * LOG2E
    total = cumul[:, CH - 1 : CH]
    tail = jnp.exp2(total - shifted)
    row_ref[...] = jnp.concatenate([cumul, shifted, gate, keep], 0)
    stack = jnp.concatenate(
        [cumul, shifted, tail, gate, jnp.exp2(cumul), keep, keep, keep], 0
    )
    col_ref[...] = stack.T

    @pl.when(jnp.logical_and(b == 0, c == 0))
    def _():
        gsum_ref[...] = jnp.zeros_like(gsum_ref)

    gsum_ref[...] += gate

    @pl.when(c == 0)
    def _():
        acc[...] = jnp.zeros_like(acc)
        tot_ref[0] = jnp.zeros_like(tot_ref[0])

    tot_ref[0] += jnp.broadcast_to(total, tot_ref.shape[1:])
    ones2 = ones_ref[...]
    block_ones = jnp.ones((SR - HD, CH), f32)
    for pair in range(width // 128):
        n, _ = unit(keys[:, 128 * pair : 128 * pair + 128], ones2)
        sine, cosine = sin_cos(n, maps_ref[pair])
        for i in range(2):
            h = 2 * pair + i
            phi = jnp.concatenate(
                [sine[:, NF * i : NF * i + NF], cosine[:, NF * i : NF * i + NF]], 1
            ).astype(bf16)
            phik_ref[:, FW * h : FW * h + FW] = phi
            weighted = jnp.concatenate([vt[HD * h : HD * h + HD].astype(f32), block_ones], 0)
            weighted = (weighted * tail[h : h + 1]).astype(bf16)
            update = dot(weighted, phi)
            u_ref[0, 0, h] = update
            acc[h] = jnp.exp2(total[h : h + 1]) * acc[h] + update

    @pl.when(c == pl.num_programs(1) - 1)
    def _():
        end_ref[0] = acc[...]


def lower_mask(flip):
    rows = lax.broadcasted_iota(jnp.int32, (CH, CH), 0)
    columns = lax.broadcasted_iota(jnp.int32, (CH, CH), 1)
    return rows <= columns if flip else rows >= columns


def queries_setup(held, here, wq_ref, mix_ref):
    size = held.shape[0]
    width = wq_ref.shape[0]
    for d in range(size):
        at = width * here // 2
        rows = HD * here
        if here == 2:
            wq_ref[:, 128 * d : 128 * d + 128] = held[d, :width]
        elif d % 2:
            one, two = held[d - 1, :at], held[d, :at]
            lanes = slice(64 * d - 64, 64 * d + 64)
            wq_ref[:at, lanes] = jnp.concatenate([one[:, :HD], two[:, :HD]], 1)
            wq_ref[at:, lanes] = jnp.concatenate([one[:, HD:], two[:, HD:]], 1)
        for j in range(width // 128):
            mix_ref[rows * d : rows * d + rows, 128 * j : 128 * j + 128] = held[
                d, at + rows * j : at + rows * j + rows
            ]


def queries_body(*refs, size, here, skipped):
    parts, refs = refs[:size], refs[size:]
    if size:
        index_ref, refs = refs[0], refs[1:]
        held, refs = refs[-1], refs[:-1]
        wq_ref, mix_ref = refs[-2:]
        refs = refs[:-2]

        @pl.when(jnp.logical_and(pl.program_id(0) == 0, pl.program_id(1) == 0))
        def _():
            collect(held, parts, index_ref[0])
            queries_setup(held, here, wq_ref, mix_ref)

    else:
        wq_ref, refs = refs[0], refs[1:]
    x_ref, maps_ref, ones_ref, phik_ref, v_ref, row_ref, col_ref = refs[:7]
    phiq_ref, intra_ref, *ticks = refs[7 + skipped :]
    clear(ticks)
    query = dot(x_ref[...], wq_ref[...])
    width = query.shape[1]
    ones2 = ones_ref[...]
    lower = lower_mask(False)
    low = low_lanes(CH)
    for pair in range(width // 128):
        n, _ = unit(query[:, 128 * pair : 128 * pair + 128], ones2)
        sine, cosine = sin_cos(n, maps_ref[pair])
        values = v_ref[:, 128 * pair : 128 * pair + 128]
        for i in range(2):
            h = 2 * pair + i
            phi = jnp.concatenate(
                [sine[:, NF * i : NF * i + NF], cosine[:, NF * i : NF * i + NF]], 1
            ).astype(bf16)
            phiq_ref[:, FW * h : FW * h + FW] = phi
            raw = dot_nt(phi, phik_ref[:, FW * h : FW * h + FW])
            differ = col_ref[:, h : h + 1] - row_ref[GR + h : GR + h + 1, :]
            decay = jnp.exp2(jnp.where(lower, differ, -jnp.inf))
            scores = (raw * decay).astype(bf16)
            one = jnp.ones_like(values)
            augmented = jnp.where(low, one, values) if i else jnp.where(low, values, one)
            intra_ref[:, 128 * h : 128 * h + 128] = dot(scores, augmented)


def tokens_body(
    start_refs,
    x_ref,
    c_ref,
    phiq_ref,
    intra_ref,
    row_ref,
    col_ref,
    u_ref,
    mix_ref,
    up_ref,
    down_ref,
    vec_ref,
    upb_ref,
    ones_ref,
    select_ref,
    *refs,
    chunks,
    size,
):
    (
    out_ref,
    dr_ref,
    dn_ref,
    qside_ref,
    states_ref,
    vloc_ref,
    vdev_ref,
    sent_ref,
    packed_ref,
    state,
    heads_low,
    numer_all,
    inner_all,
    up_acc,
    down_acc,
    mix_acc,
    vec_acc,
    ) = refs
    b = pl.program_id(0)
    heads = state.shape[0]
    pairs = heads // 2

    @pl.when(b == 0)
    def _():
        mix_acc[...] = jnp.zeros_like(mix_acc)
        vec_acc[...] = jnp.zeros_like(vec_acc)
        up_acc[...] = jnp.zeros_like(up_acc)
        down_acc[...] = jnp.zeros_like(down_acc)

    low = low_lanes(CH)
    state[...] = sum(start_ref[0].astype(f32) for start_ref in start_refs)
    for c in range(chunks):
        rows = slice(CH * c, CH * c + CH)
        for pair in range(pairs):
            both = []
            for i in range(2):
                h = 2 * pair + i
                block = state[h].astype(bf16)
                states_ref[0, c, h] = block
                carry = dot_nt(phiq_ref[rows, FW * h : FW * h + FW], expand(block, i))
                carried = col_ref[rows, 4 * GR + h : 4 * GR + h + 1]
                both.append(intra_ref[rows, 128 * h : 128 * h + 128] + carried * carry)
                last = jnp.exp2(row_ref[c, h : h + 1, CH - 1 : CH])
                state[h] = last * state[h] + u_ref[0, c, h]
            lanes = slice(128 * pair, 128 * pair + 128)
            numer = jnp.where(low, both[0], both[1])
            inner = pltpu.roll(jnp.where(low, both[1], both[0]), HD, 1)
            numer_all[rows, lanes] = numer
            inner_all[rows, lanes] = inner
            heads_low[rows, lanes] = (numer * lax.rsqrt(inner * inner + 1.0)).astype(bf16)
    for h in range(heads):
        states_ref[0, chunks, h] = state[h].astype(bf16)

    mix = mix_ref[...]
    rest = heads_low[...]
    mixing_bias, gain, shift, down_bias = (vec_ref[i : i + 1, :] for i in range(4))
    residual = x_ref[...].astype(f32) + dot(rest, mix) + mixing_bias
    center = residual - jnp.mean(residual, -1, keepdims=True)
    scale = lax.rsqrt(jnp.mean(center * center, -1, keepdims=True) + 1e-05)
    normal = center * scale
    normal_low = (normal * gain + shift).astype(bf16)
    normal_t = normal_low.T
    upstream = c_ref[...]
    upstream_t = upstream.T
    result = residual + down_bias
    grad_normal = jnp.zeros_like(residual)
    for j in range(up_ref.shape[1] // TILE):
        part = slice(TILE * j, TILE * j + TILE)
        up = up_ref[:, part]
        down = down_ref[part, :]
        hidden = dot(normal_low, up) + upb_ref[:, part]
        square = hidden * hidden
        th = jnp.tanh(hidden * (GELU_A + (GELU_A * GELU_B) * square))
        half = 0.5 + 0.5 * th
        active = (hidden * half).astype(bf16)
        slope = half + hidden * (0.5 - 0.5 * th * th) * (
            GELU_A + (3.0 * GELU_A * GELU_B) * square
        )
        result += dot(active, down)
        grad_hidden = slope * dot_nt(upstream, down)
        grad_hidden = grad_hidden.astype(bf16)
        vec_acc[4 + j : 5 + j, :] += jnp.sum(grad_hidden.astype(f32), 0, keepdims=True)
        grad_normal += dot_nt(grad_hidden, up)
        up_acc[:, part] += dot(normal_t, grad_hidden)
        down_acc[:, part] += dot(upstream_t, active)
    out_ref[...] = result.astype(bf16)
    upstream = upstream.astype(f32)
    dn = grad_normal * gain
    grad_residual = upstream + scale * (
        dn
        - jnp.mean(dn, -1, keepdims=True)
        - normal * jnp.mean(dn * normal, -1, keepdims=True)
    )
    dr_ref[...] = grad_residual
    for i, value in enumerate((grad_residual, grad_normal * normal, grad_normal, upstream)):
        vec_acc[i : i + 1, :] += jnp.sum(value, 0, keepdims=True)
    grad_low = grad_residual.astype(bf16)
    mix_acc[...] += dot_tn(rest, grad_low)
    grad_heads = dot_nt(grad_low, mix)

    ones2 = ones_ref[...]
    following = [None] * heads
    for c in reversed(range(chunks)):
        rows = slice(CH * c, CH * c + CH)
        query_sides = []
        for pair in range(pairs):
            lanes = slice(128 * pair, 128 * pair + 128)
            numer, inner, grad = numer_all[rows, lanes], inner_all[rows, lanes], grad_heads[rows, lanes]
            square = 1.0 / (inner * inner + 1.0)
            grad_numer = grad * lax.rsqrt(inner * inner + 1.0)
            query_side = dot(split2_cat(grad_numer * numer), ones2) * square
            query_sides.append(query_side)
            grad_inner = pltpu.roll(query_side * inner * (-1.0 / HD), HD, 1)
            for i in range(2):
                h = 2 * pair + i
                if i:
                    together = jnp.where(low, grad_inner, grad_numer)
                else:
                    together = jnp.where(low, grad_numer, grad_inner)
                dn_ref[rows, 128 * h : 128 * h + 128] = together.astype(bf16)
                carried = col_ref[rows, 4 * GR + h : 4 * GR + h + 1]
                sent = (carried * together).T.astype(bf16)
                own = shrink(dot(sent, phiq_ref[rows, FW * h : FW * h + FW]), i)
                vloc_ref[0, c, h] = own
                if following[h] is not None:
                    last = jnp.exp2(row_ref[c, h : h + 1, CH - 1 : CH])
                    own = own + last * following[h]
                following[h] = own
        qside_ref[rows, :] = dot(
            split2_cat(jnp.concatenate(query_sides, 1)), select_ref[...]
        )
    for h in range(heads):
        vdev_ref[0, h] = following[h]
        sent_ref[0, h] = following[h].astype(bf16)

    @pl.when(b == pl.num_programs(0) - 1)
    def _():
        width, ff = up_acc.shape
        up_rows, down_rows, mix_rows = width // size, ff // size, mix_acc.shape[0] // size
        for d in range(size):
            at = d * (packed_ref.shape[0] // size)
            for j in range(ff // TILE):
                packed_ref[at : at + up_rows, :] = up_acc[
                    up_rows * d : up_rows * d + up_rows, TILE * j : TILE * j + TILE
                ].astype(bf16)
                at += up_rows
            packed_ref[at : at + down_rows, :] = (
                down_acc[:, down_rows * d : down_rows * d + down_rows].T.astype(bf16)
            )
            at += down_rows
            packed_ref[at : at + mix_rows, :] = mix_acc[
                mix_rows * d : mix_rows * d + mix_rows, :
            ].astype(bf16)
            at += mix_rows
            rest = packed_ref.shape[0] // size * (d + 1) - at
            packed_ref[at : at + rest, :] = jnp.zeros((rest, width), bf16)
            if d == 0:
                packed_ref[at : at + GR, :] = jnp.concatenate(split2(vec_acc[...]), 0)


def query_back_body(
    x_ref,
    wq_ref,
    maps_back_ref,
    ones_ref,
    phiq_ref,
    phik_ref,
    v_ref,
    dn_ref,
    row_ref,
    col_ref,
    states_ref,
    *refs,
):
    dq_ref, dphik_ref, dv_ref, wqg_ref, *ticks = refs[-7:]
    clear(ticks)
    first = jnp.logical_and(pl.program_id(0) == 0, pl.program_id(1) == 0)

    @pl.when(first)
    def _():
        wqg_ref[...] = jnp.zeros_like(wqg_ref)

    x = x_ref[...]
    query = dot(x, wq_ref[...])
    width = query.shape[1]
    ones2 = ones_ref[...]
    mask = lower_mask(True)
    low = low_lanes(CH)
    for pair in range(width // 128):
        lanes = slice(128 * pair, 128 * pair + 128)
        n, inverse = unit(query[:, lanes], ones2)
        values = v_ref[:, lanes]
        angles = []
        for i in range(2):
            h = 2 * pair + i
            wide = slice(FW * h, FW * h + FW)
            phiq, phik = phiq_ref[:, wide], phik_ref[:, wide]
            grad = dn_ref[:, 128 * h : 128 * h + 128]
            differ = row_ref[h : h + 1, :] - col_ref[:, GR + h : GR + h + 1]
            decay = jnp.exp2(jnp.where(mask, differ, -jnp.inf))
            one = jnp.ones_like(values)
            augmented = jnp.where(low, one, values) if i else jnp.where(low, values, one)
            scores = (dot_nt(phik, phiq) * decay).astype(bf16)
            grad_raw = (dot_nt(augmented, grad) * decay).astype(bf16)
            dv_ref[:, 128 * h : 128 * h + 128] = dot(scores, grad)
            dphik_ref[:, wide] = dot(grad_raw, phiq).astype(bf16)
            carried = col_ref[:, 4 * GR + h : 4 * GR + h + 1]
            dphi = dot_tn(grad_raw, phik) + carried * dot(grad, expand(states_ref[0, 0, h], i))
            dphi = dphi.astype(bf16).astype(f32)
            phiq = phiq.astype(f32)
            angles.append(dphi[:, :NF] * phiq[:, NF:] - dphi[:, NF:] * phiq[:, :NF])
        dq = feature_back(n, inverse, jnp.concatenate(angles, 1), maps_back_ref[pair], ones2)
        dq_ref[:, lanes] = dq.astype(bf16)
    wqg_ref[...] += dot_tn(x, dq_ref[...])


def key_back_body(
    end_refs,
    x_ref,
    wq_ref,
    wkv_ref,
    maps_back_ref,
    gw_ref,
    ones_ref,
    all_ref,
    tri_ref,
    phik_ref,
    v_ref,
    dq_ref,
    dphik_ref,
    dv_ref,
    qside_ref,
    row_ref,
    col_ref,
    states_ref,
    vloc_ref,
    dr_ref,
    factor_ref,
    *refs,
):
    dx_ref, wkvg_ref, gwg_ref, gbg_ref, *ticks, grads, state_grad, sides = refs[-10:]
    clear(ticks)
    first = jnp.logical_and(pl.program_id(0) == 0, pl.program_id(1) == 0)

    @pl.when(first)
    def _():
        wkvg_ref[...] = jnp.zeros_like(wkvg_ref)
        gwg_ref[...] = jnp.zeros_like(gwg_ref)
        gbg_ref[...] = jnp.zeros_like(gbg_ref)

    @pl.when(pl.program_id(1) == 0)
    def _():
        state_grad[...] = sum(end_ref[0].astype(f32) for end_ref in end_refs)

    x = x_ref[...]
    heads = state_grad.shape[0]
    keys = dot(x, wkv_ref[:, : wq_ref.shape[1]])
    width = wq_ref.shape[1]
    ones2 = ones_ref[...]
    low = low_lanes(CH)
    weigh = jnp.where(lax.broadcasted_iota(jnp.int32, (SR, FW), 0) < HD, 1.0, 4.0)
    bounds = []
    for pair in range(heads // 2):
        lanes = slice(128 * pair, 128 * pair + 128)
        n, inverse = unit(keys[:, lanes], ones2)
        values = v_ref[:, lanes]
        angles = []
        both = []
        for i in range(2):
            h = 2 * pair + i
            wide = slice(FW * h, FW * h + FW)
            phik = phik_ref[:, wide]
            one = jnp.ones_like(values)
            augmented = jnp.where(low, one, values) if i else jnp.where(low, values, one)
            tail = col_ref[:, 2 * GR + h : 2 * GR + h + 1]
            grad_end = state_grad[h]
            bounds.append(
                jnp.sum(grad_end * weigh * states_ref[0, 0, h].astype(f32), 0, keepdims=True)
            )
            spread = expand(grad_end.astype(bf16), i)
            dv = dv_ref[:, 128 * h : 128 * h + 128] + tail * dot_nt(phik, spread)
            sides[:, 128 * h : 128 * h + 128] = dv * augmented.astype(f32)
            both.append(dv)
            dphi = dphik_ref[:, wide].astype(f32) + tail * dot(augmented, spread)
            dphi = dphi.astype(bf16).astype(f32)
            phik = phik.astype(f32)
            angles.append(dphi[:, :NF] * phik[:, NF:] - dphi[:, NF:] * phik[:, :NF])
            last = jnp.exp2(row_ref[h : h + 1, CH - 1 : CH])
            state_grad[h] = last * grad_end + vloc_ref[0, 0, h]
        dk = feature_back(n, inverse, jnp.concatenate(angles, 1), maps_back_ref[pair], ones2)
        grads[:, lanes] = dk.astype(bf16)
        grads[:, width + 128 * pair : width + 128 * pair + 128] = jnp.where(
            low, both[0], both[1]
        ).astype(bf16)
    key_side = dot(split2_cat(sides[...]), all_ref[...])
    key_row = key_side.T[:GR]
    differ = qside_ref[...].T[:GR] - key_row
    bound = jnp.sum(jnp.concatenate(bounds, 0), 1, keepdims=True)
    bound = jnp.concatenate([bound, jnp.zeros((GR - heads, 1), f32)], 0)
    grad_log = dot(split3_cat(differ), tri_ref[...]) + bound
    gate, keep = row_ref[2 * GR : 3 * GR, :], row_ref[3 * GR : 4 * GR, :]
    grad_pre = (
        grad_log * keep - gate * key_row + factor_ref[...] * gate * keep
    ).astype(bf16)
    gbg_ref[...] += grad_pre.astype(f32)
    gwg_ref[...] += dot(grad_pre, x)
    together = grads[...]
    wkvg_ref[...] += dot_tn(x, together)
    dx_ref[...] = (
        dr_ref[...]
        + dot_nt(dq_ref[...], wq_ref[...])
        + dot_nt(together, wkv_ref[...])
        + dot_tn(grad_pre, gw_ref[...])
    )


def unpack_body(index_ref, packed_ref, up_ref, down_ref, mix_ref, vec_ref):
    d = pl.program_id(0)
    rows, ff = up_ref.shape
    at = 0
    for j in range(ff // TILE):
        up_ref[:, TILE * j : TILE * j + TILE] = packed_ref[0, at : at + rows, :].astype(f32)
        at += rows
    down_ref[...] = packed_ref[0, at : at + down_ref.shape[0], :].astype(f32)
    at += down_ref.shape[0]

    @pl.when(d == index_ref[0])
    def _():
        mix_ref[...] = packed_ref[0, at : at + mix_ref.shape[0], :].astype(f32)

    at += mix_ref.shape[0]

    @pl.when(d == 0)
    def _():
        both = packed_ref[0, at : at + GR, :].astype(f32)
        vec_ref[...] = both[:8] + both[8:]


def tokens_entry(*refs, starts, **named):
    tokens_body(refs[:starts], *refs[starts:], **named)


def key_back_entry(*refs, arrivals):
    key_back_body(refs[:arrivals], *refs[arrivals:])


def whole(array):
    zeros = (0,) * len(array.shape)
    return pl.BlockSpec(array.shape, lambda *_: zeros, pipeline_mode=pl.Buffered(1))


def fixed(shape):
    zeros = (0,) * len(shape)
    return pl.BlockSpec(shape, lambda *_: zeros)


def call(body, grid, ins, outs, previous=(), after=(), scratch=(), name=None, flops=0):
    extra = list(previous) + list(after)
    specs = [spec for _, spec in ins] + [pl.BlockSpec(memory_space=pl.ANY)] * len(extra)
    return pl.pallas_call(
        body,
        grid=grid,
        in_specs=specs,
        out_specs=[spec for _, _, spec in outs],
        out_shape=[jax.ShapeDtypeStruct(shape, kind) for shape, kind, _ in outs],
        scratch_shapes=list(scratch),
        input_output_aliases={len(ins) + i: i for i in range(len(previous))},
        compiler_params=pltpu.CompilerParams(
            dimension_semantics=("arbitrary",) * len(grid), vmem_limit_bytes=62 * 1024 * 1024
        ),
        cost_estimate=pl.CostEstimate(flops=flops, bytes_accessed=4 << 20, transcendentals=0),
        name=name,
    )(*[array for array, _ in ins], *extra)


def swap(x, axis, bit):
    size = lax.axis_size(axis)
    return lax.ppermute(x, axis, [(i, i ^ bit) for i in range(size)])


def spread_head(part):
    parts = [part]
    for k in range(1, lax.axis_size("head")):
        parts.append(swap(parts[k - 1], "head", 1) if k % 2 else swap(part, "head", k))
    return parts


def side(axis, bit):
    return (lax.axis_index(axis) // bit) % 2


class HalvingSum:
    def __init__(self, array):
        self.terms = [(array, 0)]
        self.length = array.shape[0]

    def part(self, offset, tick=0.0):
        total = tick
        for array, start in self.terms:
            piece = lax.dynamic_slice_in_dim(array, start + offset, self.length, 0)
            total = total + piece.astype(f32)
        return total.astype(bf16)

    def step(self, axis, bit, tick=0.0):
        self.length //= 2
        mine = side(axis, bit)
        send = self.part((1 - mine) * self.length, tick)
        self.terms = [(array, start + mine * self.length) for array, start in self.terms]
        self.terms.append((swap(send, axis, bit), 0))
        return send


def join(array, axis, bit):
    other = swap(array, axis, bit)
    return jnp.where(
        side(axis, bit) == 0,
        jnp.concatenate([array, other], 0),
        jnp.concatenate([other, array], 0),
    )


def high_rest(x):
    high = lax.reduce_precision(x, 8, 7)
    return high, x - high


def per_device(
    tokens,
    cotangent,
    carry_state,
    carry_norm,
    random_maps,
    query_weight,
    key_weight,
    value_weight,
    gate_weight,
    gate_bias,
    mixing_weight,
    mixing_bias,
    norm_gain,
    norm_bias,
    up_weight,
    up_bias,
    down_weight,
    down_bias,
):
    seqs, length, width = tokens.shape
    here = gate_weight.shape[1]
    size = lax.axis_size("head")
    replicas = lax.axis_size("dp")
    index = lax.axis_index("head")
    heads = here * size
    chunks = length // CH
    blocks = seqs * chunks
    count = seqs * length
    inner_width = heads * HD
    own = here * HD
    ff = up_weight.shape[1]
    pairs = heads // 2
    head_bits = [1 << i for i in range(size.bit_length() - 1)]
    dp_bits = [1 << i for i in range(replicas.bit_length() - 1)]
    index_array = index.astype(jnp.int32).reshape(1)
    smem = pl.BlockSpec(memory_space=pltpu.SMEM)

    scaled = random_maps.reshape(own, NF) * (0.5 / math.pi)
    map_high, map_rest = high_rest(scaled)
    bias_high, bias_rest = high_rest(gate_bias)
    bias_mid, bias_rest = high_rest(bias_rest)
    biases = jnp.pad(jnp.stack([bias_high, bias_mid, bias_rest]), ((0, 0), (0, 128 - here)))
    tail = jnp.concatenate([gate_weight.T.reshape(-1, 128).astype(f32), biases])
    tail = jnp.pad(tail, ((0, GR - tail.shape[0]), (0, 0)))
    key_value = jnp.concatenate([key_weight, value_weight], 0 if here == 2 else 1)
    first_part = jnp.concatenate(
        [key_value]
        + [part.astype(bf16) for part in (map_high, map_rest, tail)]
    )
    half = width // 2
    query_rows = (
        query_weight
        if here == 2
        else jnp.concatenate([query_weight[:half], query_weight[half:]], 1)
    )
    second_part = jnp.concatenate(
        [query_rows] + [mixing_weight[:, 128 * j : 128 * j + 128] for j in range(width // 128)]
    )
    first_parts = spread_head(first_part)
    second_parts = [second_part] + [swap(second_part, "head", k) for k in range(1, size)]

    begin = jnp.concatenate(
        [
            carry_state.transpose(0, 1, 3, 2),
            jnp.broadcast_to(carry_norm[:, :, None, :], (seqs, here, SR - HD, FW)),
        ],
        2,
    ).astype(bf16)
    begin = jnp.concatenate(
        [jnp.where(index == 0, begin, jnp.zeros_like(begin))]
        + [lax.ppermute(begin, "head", [(k, 0)]) for k in range(1, size)],
        1,
    )

    half = np.arange(128) // HD
    ones2 = np.tile((half[:, None] == half[None, :]).astype(np.float32), (2, 1))
    ones2 = jnp.asarray(ones2, bf16)
    place = np.arange(CH)
    upto = jnp.asarray(np.tile((place[:, None] <= place[None, :]).astype(np.float32), (3, 1)), bf16)
    onward = jnp.asarray(np.tile((place[:, None] >= place[None, :]).astype(np.float32), (3, 1)), bf16)
    lane = np.arange(128)
    one_lane = np.zeros((inner_width, 128), np.float32)
    one_lane[np.arange(heads) * HD, np.arange(heads)] = 1.0
    select = jnp.asarray(np.tile(one_lane, (2, 1)), bf16)
    all_lanes = (np.arange(heads * 128) // 128)[:, None] == lane[None, :]
    all_lanes = jnp.asarray(np.tile(all_lanes.astype(np.float32), (2, 1)), bf16)

    x = tokens.reshape(count, width)
    c = cotangent.reshape(count, width)
    state_shape = (heads, SR, FW)
    tick_outs = [((1, lanes), f32, fixed((1, lanes))) for lanes in (128, FW, width)]

    def rows_of(columns, base=0, reverse=False):
        def at(b, t):
            return ((base + b) * chunks + (chunks - 1 - t if reverse else t), 0)

        return pl.BlockSpec((CH, columns), at)

    def row_spec(base=0, reverse=False):
        return pl.BlockSpec((4 * GR, CH), rows_of(0, base, reverse).index_map)

    def per_block(shape, base=0, offset=0, reverse=False):
        zeros = (0,) * len(shape)

        def at(b, t):
            return (base + b, offset + (chunks - 1 - t if reverse else t)) + zeros

        return pl.BlockSpec((1, 1) + shape, at)

    def per_seq(base=0):
        return pl.BlockSpec((1,) + state_shape, lambda b, t: (base + b, 0, 0, 0))

    held_first = (size,) + first_part.shape
    (
        phik,
        v,
        row,
        col,
        update,
        end,
        total,
        gate_sums,
        wkv,
        maps_front,
        maps_back,
        gw,
    ) = call(
        functools.partial(keys_body, size=size, here=here),
        (seqs, chunks),
        [(part, whole(part)) for part in first_parts]
        + [
            (index_array, smem),
            (x, rows_of(width)),
            (ones2, whole(ones2)),
            (upto, whole(upto)),
        ],
        [
            ((count, heads * FW), bf16, rows_of(heads * FW)),
            ((count, inner_width), bf16, rows_of(inner_width)),
            ((blocks * 4 * GR, CH), f32, row_spec()),
            ((count, 128), f32, rows_of(128)),
            ((seqs, chunks) + state_shape, f32, per_block(state_shape)),
            ((seqs,) + state_shape, f32, per_seq()),
            ((seqs, GR, 128), f32, pl.BlockSpec((1, GR, 128), lambda b, t: (b, 0, 0))),
            ((GR, CH), f32, fixed((GR, CH))),
            ((width, 2 * inner_width), bf16, fixed((width, 2 * inner_width))),
            ((pairs, 3 * 128, FW), bf16, fixed((pairs, 3 * 128, FW))),
            ((pairs, 3 * FW, 128), bf16, fixed((pairs, 3 * FW, 128))),
            ((GR, width), bf16, fixed((GR, width))),
        ],
        scratch=[
            pltpu.VMEM(state_shape, f32),
            pltpu.VMEM(held_first, bf16),
            pltpu.VMEM((inner_width, width), bf16),
            pltpu.VMEM((GR, CH), f32),
        ],
        name="keys",
        flops=20_000_000_000,
    )

    gate_sums = gate_sums[:heads, :128] + gate_sums[:heads, 128:]
    sum_steps = [("head", bit) for bit in head_bits] + [("dp", bit) for bit in dp_bits]
    last = jnp.exp2(total[:, :heads, 0])[:, :, None, None]

    sent = (end + last * begin.astype(f32)).astype(bf16)
    starts = [begin]
    ticks = (0.0, 0.0, 0.0)
    coming = gate_sums
    phiq = intra = wq = mix = None
    previous = ()
    for step, (base, number) in enumerate(((0, 1), (1, 2), (3, 1))):
        arrived = None
        if step < size - 1:
            arrived = lax.ppermute(sent, "head", [(step, step + 1)])
            starts.append(arrived)
        coming = swap(gate_sums, *sum_steps[step])
        main = [
            (x, rows_of(width, base)),
            (maps_front, whole(maps_front)),
            (ones2, whole(ones2)),
            (phik, rows_of(heads * FW, base)),
            (v, rows_of(inner_width, base)),
            (row, row_spec(base)),
            (col, rows_of(128, base)),
        ]
        outs = [
            ((count, heads * FW), bf16, rows_of(heads * FW, base)),
            ((count, heads * 128), f32, rows_of(heads * 128, base)),
        ] + tick_outs
        if step == 0:
            phiq, intra, *ticks, wq, mix = call(
                functools.partial(queries_body, size=size, here=here, skipped=2),
                (number, chunks),
                [(part, whole(part)) for part in second_parts] + [(index_array, smem)] + main,
                outs
                + [
                    ((width, inner_width), bf16, fixed((width, inner_width))),
                    ((inner_width, width), bf16, fixed((inner_width, width))),
                ],
                after=[sent, gate_sums],
                scratch=[pltpu.VMEM((size,) + second_part.shape, bf16)],
                name="queries",
                flops=5_000_000_000,
            )
        else:
            phiq, intra, *ticks = call(
                functools.partial(queries_body, size=0, here=here, skipped=4),
                (number, chunks),
                [(wq, whole(wq))] + main,
                outs,
                previous=[phiq, intra],
                after=[sent, gate_sums],
                name="queries",
                flops=5_000_000_000 * number,
            )
        gate_sums = gate_sums + coming + ticks[0]
        if step < size - 2:
            sent = (last * arrived.astype(f32) + end + ticks[1][0]).astype(bf16)
    for step in range(3, size - 1):
        arrived = lax.ppermute(sent, "head", [(step, step + 1)])
        starts.append(arrived)
        sent = (last * arrived.astype(f32) + end).astype(bf16)

    vectors = jnp.stack([mixing_bias, norm_gain, norm_bias, down_bias] * 2)

    def seq_rows(columns):
        return pl.BlockSpec((length, columns), lambda b: (b, 0))

    def seq_block(*shape):
        zeros = (0,) * len(shape)
        return pl.BlockSpec((1,) + shape, lambda b: (b,) + zeros)

    up_bias2 = up_bias.reshape(1, ff)
    slab = (width // size) * (ff // TILE) + ff // size + own + GR
    slab += -slab % replicas
    layer_out, dr, dn, qside, states, vloc, vdev, sent, packed = call(
        functools.partial(
            tokens_entry, starts=len(starts), chunks=chunks, size=size
        ),
        (seqs,),
        [(start, seq_block(*state_shape)) for start in starts]
        + [
            (x, seq_rows(width)),
            (c, seq_rows(width)),
            (phiq, seq_rows(heads * FW)),
            (intra, seq_rows(heads * 128)),
            (
                row.reshape(blocks, 4 * GR, CH),
                pl.BlockSpec((chunks, 4 * GR, CH), lambda b: (b, 0, 0)),
            ),
            (col, seq_rows(128)),
            (update, seq_block(chunks, *state_shape)),
            (mix, whole(mix)),
            (up_weight, whole(up_weight)),
            (down_weight, whole(down_weight)),
            (vectors, whole(vectors)),
            (up_bias2, whole(up_bias2)),
            (ones2, whole(ones2)),
            (select, whole(select)),
        ],
        [
            ((count, width), bf16, seq_rows(width)),
            ((count, width), f32, seq_rows(width)),
            ((count, heads * 128), bf16, seq_rows(heads * 128)),
            ((count, 128), f32, seq_rows(128)),
            ((seqs, chunks + 1) + state_shape, bf16, seq_block(chunks + 1, *state_shape)),
            ((seqs, chunks) + state_shape, f32, seq_block(chunks, *state_shape)),
            ((seqs,) + state_shape, f32, seq_block(*state_shape)),
            ((seqs,) + state_shape, bf16, seq_block(*state_shape)),
            ((size * slab, width), bf16, fixed((size * slab, width))),
        ],
        scratch=[
            pltpu.VMEM(state_shape, f32),
            pltpu.VMEM((length, inner_width), bf16),
            pltpu.VMEM((length, inner_width), f32),
            pltpu.VMEM((length, inner_width), f32),
            pltpu.VMEM((width, ff), f32),
            pltpu.VMEM((width, ff), f32),
            pltpu.VMEM((inner_width, width), f32),
            pltpu.VMEM((8, width), f32),
        ],
        name="tokens",
        flops=50_000_000_000,
    )

    stages = (
        [("head", 1)]
        + [("dp", bit) for bit in dp_bits[:1]]
        + [("head", bit) for bit in head_bits[1:]]
        + [("dp", bit) for bit in dp_bits[1:]]
    )
    waiting = list(stages)
    sums = HalvingSum(packed)
    ticks = (0.0, [0.0], 0.0)
    finishes = []
    dq = dphik = dv = None
    previous = []
    query_grads = []
    for step, (base, number) in enumerate(((0, 1), (1, 2), (3, 1))):
        after = [sums.step(*waiting.pop(0), ticks[2])]
        if step + 3 < len(sum_steps):
            after.append(gate_sums)
            coming = swap(gate_sums, *sum_steps[step + 3])
        if step < size - 1:
            arrived = lax.ppermute(sent, "head", [(size - 1 - step, size - 2 - step)])
            finishes.append(arrived)
            after.append(sent)
        dq, dphik, dv, query_grad, *ticks = call(
            query_back_body,
            (number, chunks),
            [
                (x, rows_of(width, base)),
                (wq, whole(wq)),
                (maps_back, whole(maps_back)),
                (ones2, whole(ones2)),
                (phiq, rows_of(heads * FW, base)),
                (phik, rows_of(heads * FW, base)),
                (v, rows_of(inner_width, base)),
                (dn, rows_of(heads * 128, base)),
                (row, row_spec(base)),
                (col, rows_of(128, base)),
                (states, per_block(state_shape, base)),
            ],
            [
                ((count, inner_width), bf16, rows_of(inner_width, base)),
                ((count, heads * FW), bf16, rows_of(heads * FW, base)),
                ((count, heads * 128), f32, rows_of(heads * 128, base)),
                ((width, inner_width), f32, fixed((width, inner_width))),
            ] + tick_outs,
            previous=previous,
            after=after,
            name="query_back",
            flops=8_000_000_000 * number,
        )
        previous = [dq, dphik, dv]
        query_grads.append(query_grad)
        if step + 3 < len(sum_steps):
            gate_sums = gate_sums + coming + ticks[0]
        if step < size - 2:
            sent = (last * arrived.astype(f32) + vdev + ticks[1][0]).astype(bf16)
    for step in range(3, size - 1):
        arrived = lax.ppermute(sent, "head", [(size - 1 - step, size - 2 - step)])
        finishes.append(arrived)
        sent = (last * arrived.astype(f32) + vdev).astype(bf16)

    for axis, bit in sum_steps[6:]:
        gate_sums = gate_sums + swap(gate_sums, axis, bit)
    gate_total = jnp.sum(gate_sums)
    gate_count = replicas * heads * size * count
    mean_gate = gate_total / gate_count
    factor = 2.0 * penalty_weight * (mean_gate - target_gate) / heads
    factor = jnp.broadcast_to(factor, (1, CH))

    tokens_grad = None
    previous = []
    key_value_grads, gate_grads, gate_bias_grads = [], [], []
    for base, number in ((0, 2), (2, 2)):
        after = []
        if waiting:
            after = [sums.step(*waiting.pop(0), ticks[2])]
        tokens_grad, key_value_grad, gate_grad, gate_bias_grad, *ticks = call(
            functools.partial(key_back_entry, arrivals=len(finishes)),
            (number, chunks),
            [(finish, per_seq(base)) for finish in finishes]
            + [
                (x, rows_of(width, base, True)),
                (wq, whole(wq)),
                (wkv, whole(wkv)),
                (maps_back, whole(maps_back)),
                (gw, whole(gw)),
                (ones2, whole(ones2)),
                (all_lanes, whole(all_lanes)),
                (onward, whole(onward)),
                (phik, rows_of(heads * FW, base, True)),
                (v, rows_of(inner_width, base, True)),
                (dq, rows_of(inner_width, base, True)),
                (dphik, rows_of(heads * FW, base, True)),
                (dv, rows_of(heads * 128, base, True)),
                (qside, rows_of(128, base, True)),
                (row, row_spec(base, True)),
                (col, rows_of(128, base, True)),
                (states, per_block(state_shape, base, 1, True)),
                (vloc, per_block(state_shape, base, 0, True)),
                (dr, rows_of(width, base, True)),
                (factor, whole(factor)),
            ],
            [
                ((count, width), f32, rows_of(width, base, True)),
                ((width, 2 * inner_width), f32, fixed((width, 2 * inner_width))),
                ((GR, width), f32, fixed((GR, width))),
                ((GR, CH), f32, fixed((GR, CH))),
            ] + tick_outs,
            previous=previous,
            after=after,
            scratch=[
                pltpu.VMEM((CH, 2 * inner_width), bf16),
                pltpu.VMEM(state_shape, f32),
                pltpu.VMEM((CH, heads * 128), f32),
            ],
            name="key_back",
            flops=8_000_000_000 * number,
        )
        previous = [tokens_grad]
        key_value_grads.append(key_value_grad)
        gate_grads.append(gate_grad)
        gate_bias_grads.append(gate_bias_grad)
    for axis, bit in waiting:
        sums.step(axis, bit)
    packed = sums.part(0)
    for axis, bit in reversed(stages):
        packed = join(packed, axis, bit)
    packed = packed.reshape(size, slab, width)
    block = (1, slab, width)
    up_grad, down_grad, mixing_grad, vector_grads = call(
        unpack_body,
        (size,),
        [(index_array, smem), (packed, pl.BlockSpec(block, lambda d: (d, 0, 0)))],
        [
            ((width, ff), f32, pl.BlockSpec((width // size, ff), lambda d: (d, 0))),
            ((ff, width), f32, pl.BlockSpec((ff // size, width), lambda d: (d, 0))),
            ((own, width), f32, fixed((own, width))),
            ((8, width), f32, fixed((8, width))),
        ],
        name="unpack",
        flops=1_000_000,
    )

    def by_device(matrix):
        return matrix.astype(bf16).reshape(-1, size, own).transpose(1, 0, 2)

    query_grad = sum(query_grads)
    key_value_grad = sum(key_value_grads)
    gate_grad = sum(gate_grads)[:heads].astype(bf16).reshape(size, -1, own)
    gate_bias_grad = jnp.sum(sum(gate_bias_grads)[:heads], 1).astype(bf16).reshape(size, 1, here)
    gate_bias_grad = jnp.pad(gate_bias_grad, ((0, 0), (0, 15), (0, own - here)))
    group = jnp.concatenate(
        [
            by_device(query_grad),
            by_device(key_value_grad[:, :inner_width]),
            by_device(key_value_grad[:, inner_width:]),
            gate_grad,
            gate_bias_grad,
        ],
        1,
    )
    rows = group.shape[1]
    group = jnp.pad(group, ((0, 0), (0, -rows % (replicas * 2)), (0, 0)))
    group_sums = HalvingSum(group.reshape(-1, own))
    for bit in reversed(head_bits):
        group_sums.step("head", bit)
    for bit in dp_bits:
        group_sums.step("dp", bit)
    group = group_sums.part(0)
    for bit in reversed(dp_bits):
        group = join(group, "dp", bit)
    group = group.astype(f32)
    gate_rows = here * width // own
    gate_grad = group[3 * width : 3 * width + gate_rows].reshape(here, width).T
    penalty = penalty_weight * (mean_gate - target_gate) * (mean_gate - target_gate)
    return (
        layer_out.reshape(seqs, length, width),
        tokens_grad.reshape(seqs, length, width),
        penalty,
        group[:width],
        group[width : 2 * width],
        group[2 * width : 3 * width],
        gate_grad,
        group[3 * width + gate_rows, :here],
        mixing_grad,
        vector_grads[0],
        vector_grads[1],
        vector_grads[2],
        up_grad,
        vector_grads[4:].reshape(ff),
        down_grad,
        vector_grads[3],
    )


def solution(mesh):
    placed = (
        P("dp", "head", None),
        P("dp", "head", None),
        P("dp", "head", None, None),
        P("dp", "head", None),
        P("head", None, None),
        P(None, "head"),
        P(None, "head"),
        P(None, "head"),
        P(None, "head"),
        P("head"),
        P("head", None),
        P(),
        P(),
        P(),
        P(),
        P(),
        P(),
        P(),
    )
    return jax.shard_map(
        per_device,
        mesh=mesh,
        in_specs=placed,
        out_specs=(
            P("dp", "head", None),
            P("dp", "head", None),
            P(),
            P(None, "head"),
            P(None, "head"),
            P(None, "head"),
            P(None, "head"),
            P("head"),
            P("head", None),
            P(),
            P(),
            P(),
            P(),
            P(),
            P(),
            P(),
        ),
        check_vma=False,
    )
```

```python
import functools
import math

import jax
import jax.numpy as jnp
import numpy as np
from jax import lax
from jax.experimental import pallas as pl
from jax.experimental.pallas import tpu as pltpu
from jax.sharding import PartitionSpec as P

CH = 256
HD = 64
NF = 128
FW = 2 * NF
SR = 80
GR = 16
TILE = 512

penalty_weight = 32.0
target_gate = 0.9
LOG2E = 1.4426950408889634
SIN_POLY = (
    3.1415925800446116,
    -5.16770687892007,
    2.5500313771889287,
    -0.5980451736320438,
    0.07722012807955428,
)
COS_POLY = (
    0.9999999534665498,
    -4.934792858660313,
    4.058411913867723,
    -1.3318801593312537,
    0.2196967947670672,
)
GELU_A = 0.7978845608028654
GELU_B = 0.044715

f32 = jnp.float32
bf16 = jnp.bfloat16


def dot(a, b):
    return lax.dot_general(a, b, (((1,), (0,)), ((), ())), preferred_element_type=f32)


def dot_nt(a, b):
    return lax.dot_general(a, b, (((1,), (1,)), ((), ())), preferred_element_type=f32)


def dot_tn(a, b):
    return lax.dot_general(a, b, (((0,), (0,)), ((), ())), preferred_element_type=f32)


def split2(x):
    high = x.astype(bf16)
    return high, (x - high.astype(f32)).astype(bf16)


def split2_cat(x):
    return jnp.concatenate(split2(x), 1)


def split3_cat(x):
    high = x.astype(bf16)
    rest = x - high.astype(f32)
    mid = rest.astype(bf16)
    return jnp.concatenate([high, mid, (rest - mid.astype(f32)).astype(bf16)], 1)


def low_lanes(rows):
    return lax.broadcasted_iota(jnp.int32, (rows, 128), 1) < HD


def unit(u, ones2):
    inverse = lax.rsqrt(dot(split2_cat(u * u), ones2) + 1e-06)
    return u * inverse, inverse


def sin_cos(n, maps):
    high, rest = split2(n)
    turns = dot(jnp.concatenate([high, rest, high], 1), maps)
    r = turns - jnp.round(turns)
    u = r * r
    scale = math.sqrt(2.0 / math.sqrt(NF))
    s = SIN_POLY[4] * scale
    c = COS_POLY[4] * scale
    for i in (3, 2, 1, 0):
        s = s * u + SIN_POLY[i] * scale
        c = c * u + COS_POLY[i] * scale
    s = s * r
    return s * c, 1.0 / math.sqrt(NF) - s * s


def feature_back(n, inverse, angle_grad, maps_back, ones2):
    high, rest = split2(angle_grad)
    dn = dot(jnp.concatenate([high, rest, high], 1), maps_back)
    radial = dot(split2_cat(n * dn), ones2)
    return (dn - n * radial) * inverse


def expand(block, odd):
    state, norm = block[:HD], block[HD:SR]
    parts = [norm] * (HD // (SR - HD))
    return jnp.concatenate(parts + [state] if odd else [state] + parts, 0)


def shrink(block, odd):
    if odd:
        return jnp.concatenate([block[HD:], block[HD - (SR - HD) : HD]], 0)
    return block[:SR]


def clear(refs):
    for ref in refs:
        ref[...] = jnp.zeros_like(ref)


def collect(held, parts, index):
    for k, part in enumerate(parts):
        held[index ^ k] = part[...]


def block_pair(even, odd):
    none = jnp.zeros_like(even)
    return jnp.concatenate(
        [jnp.concatenate([even, none], 1), jnp.concatenate([none, odd], 1)], 0
    )


def keys_setup(held, here, wkv_ref, wvt, maps_ref, back_ref, gw_ref, gb):
    size = held.shape[0]
    width = wkv_ref.shape[0]
    inner = wvt.shape[0]
    at = width * here
    high, rest, gates, biases = [], [], [], []
    for d in range(size):
        if here == 2:
            lanes = slice(128 * d, 128 * d + 128)
            wkv_ref[:, lanes] = held[d, :width]
            wkv_ref[:, inner + 128 * d : inner + 128 * d + 128] = held[d, width : 2 * width]
            wvt[lanes, :] = held[d, width : 2 * width].T
        elif d % 2:
            lanes = slice(64 * d - 64, 64 * d + 64)
            one, two = held[d - 1, :width], held[d, :width]
            wkv_ref[:, lanes] = jnp.concatenate([one[:, :HD], two[:, :HD]], 1)
            values = jnp.concatenate([one[:, HD:], two[:, HD:]], 1)
            wkv_ref[:, inner + 64 * d - 64 : inner + 64 * d + 64] = values
            wvt[lanes, :] = values.T
        for i in range(here):
            first = at + HD * i
            high.append(held[d, first : first + HD])
            rest.append(held[d, first + HD * here : first + HD * here + HD])
        tail = held[d, at + 2 * HD * here :].astype(f32)
        for i in range(here):
            gates.append(
                jnp.concatenate([tail[4 * i + j : 4 * i + j + 1] for j in range(width // 128)], 1)
            )
            bias = sum(tail[4 * here + j : 4 * here + j + 1, i : i + 1] for j in range(3))
            biases.append(jnp.broadcast_to(bias, (1, CH)))
    for pair in range(len(high) // 2):
        top = block_pair(high[2 * pair], high[2 * pair + 1])
        low = block_pair(rest[2 * pair], rest[2 * pair + 1])
        maps_ref[pair] = jnp.concatenate([top, top, low], 0)
        back = ((top.astype(f32) + low.astype(f32)) * (2.0 * math.pi)).T
        top, low = split2(back)
        back_ref[pair] = jnp.concatenate([top, top, low], 0)
    heads = len(gates)
    gw_ref[...] = jnp.concatenate(gates + [jnp.zeros((GR - heads, width), f32)], 0).astype(bf16)
    gb[...] = jnp.concatenate(biases + [jnp.zeros((GR - heads, CH), f32)], 0)


def keys_body(*refs, size, here, skipped):
    if size:
        parts, index_ref, refs = refs[:size], refs[size], refs[size + 1 :]
        held, refs = refs[-1], refs[:-1]
        wkv_ref, maps_ref, back_ref, gw_ref, wvt_ref, gb_ref = refs[-7:-1]
        refs = refs[:-7] + refs[-1:]
    else:
        wkv_ref, maps_ref, gw_ref, wvt_ref, gb_ref = refs[:5]
        refs = refs[5:]
    refs = refs[:3] + refs[3 + skipped :]
    (
        x_ref,
        ones_ref,
        tri_ref,
        phik_ref,
        v_ref,
        row_ref,
        col_ref,
        u_ref,
        end_ref,
        tot_ref,
        gsum_ref,
        tick_ref,
        acc,
    ) = refs
    tick_ref[...] = jnp.zeros_like(tick_ref)
    b, c = pl.program_id(0), pl.program_id(1)

    if size:

        @pl.when(jnp.logical_and(b == 0, c == 0))
        def _():
            collect(held, parts, index_ref[0])
            keys_setup(held, here, wkv_ref, wvt_ref, maps_ref, back_ref, gw_ref, gb_ref)

    x = x_ref[...]
    kv = dot(x, wkv_ref[...])
    width = kv.shape[1] // 2
    keys = kv[:, :width]
    v_ref[...] = kv[:, width:].astype(bf16)
    vt = dot_nt(wvt_ref[...], x).astype(bf16)
    pre = dot_nt(gw_ref[...], x) + gb_ref[...]
    soft = jnp.log1p(jnp.exp(-jnp.abs(pre)))
    log_gate = -(jnp.maximum(-pre, 0.0) + soft)
    log_keep = -(jnp.maximum(pre, 0.0) + soft)
    gate = jnp.exp(log_gate)
    keep = jnp.exp(log_keep)
    cumul = dot(split3_cat(log_gate * LOG2E), tri_ref[...])
    shifted = cumul - log_keep * LOG2E
    total = cumul[:, CH - 1 : CH]
    tail = jnp.exp2(total - shifted)
    row_ref[...] = jnp.concatenate([cumul, shifted, gate, keep], 0)
    stack = jnp.concatenate(
        [cumul, shifted, tail, gate, jnp.exp2(cumul), keep, keep, keep], 0
    )
    col_ref[...] = stack.T

    @pl.when(jnp.logical_and(b == 0, c == 0))
    def _():
        gsum_ref[...] = jnp.zeros_like(gsum_ref)

    gsum_ref[...] += gate

    @pl.when(c == 0)
    def _():
        acc[...] = jnp.zeros_like(acc)
        tot_ref[0] = jnp.zeros_like(tot_ref[0])

    tot_ref[0] += jnp.broadcast_to(total, tot_ref.shape[1:])
    ones2 = ones_ref[...]
    block_ones = jnp.ones((SR - HD, CH), f32)
    for pair in range(width // 128):
        n, _ = unit(keys[:, 128 * pair : 128 * pair + 128], ones2)
        sine, cosine = sin_cos(n, maps_ref[pair])
        for i in range(2):
            h = 2 * pair + i
            phi = jnp.concatenate(
                [sine[:, NF * i : NF * i + NF], cosine[:, NF * i : NF * i + NF]], 1
            ).astype(bf16)
            phik_ref[:, FW * h : FW * h + FW] = phi
            weighted = jnp.concatenate([vt[HD * h : HD * h + HD].astype(f32), block_ones], 0)
            weighted = (weighted * tail[h : h + 1]).astype(bf16)
            update = dot(weighted, phi)
            u_ref[0, 0, h] = update
            acc[h] = jnp.exp2(total[h : h + 1]) * acc[h] + update

    @pl.when(c == pl.num_programs(1) - 1)
    def _():
        end_ref[0] = acc[...]


def lower_mask(flip):
    rows = lax.broadcasted_iota(jnp.int32, (CH, CH), 0)
    columns = lax.broadcasted_iota(jnp.int32, (CH, CH), 1)
    return rows <= columns if flip else rows >= columns


def queries_setup(held, here, wq_ref, mix_ref):
    size = held.shape[0]
    width = wq_ref.shape[0]
    for d in range(size):
        at = width * here // 2
        rows = HD * here
        if here == 2:
            wq_ref[:, 128 * d : 128 * d + 128] = held[d, :width]
        elif d % 2:
            one, two = held[d - 1, :at], held[d, :at]
            lanes = slice(64 * d - 64, 64 * d + 64)
            wq_ref[:at, lanes] = jnp.concatenate([one[:, :HD], two[:, :HD]], 1)
            wq_ref[at:, lanes] = jnp.concatenate([one[:, HD:], two[:, HD:]], 1)
        for j in range(width // 128):
            mix_ref[rows * d : rows * d + rows, 128 * j : 128 * j + 128] = held[
                d, at + rows * j : at + rows * j + rows
            ]


def queries_body(*refs, size, here, skipped):
    parts, refs = refs[:size], refs[size:]
    if size:
        index_ref, refs = refs[0], refs[1:]
        held, refs = refs[-1], refs[:-1]
        wq_ref, mix_ref = refs[-2:]
        refs = refs[:-2]

        @pl.when(jnp.logical_and(pl.program_id(0) == 0, pl.program_id(1) == 0))
        def _():
            collect(held, parts, index_ref[0])
            queries_setup(held, here, wq_ref, mix_ref)

    else:
        wq_ref, refs = refs[0], refs[1:]
    x_ref, maps_ref, ones_ref, phik_ref, v_ref, row_ref, col_ref = refs[:7]
    phiq_ref, intra_ref, *ticks = refs[7 + skipped :]
    clear(ticks)
    query = dot(x_ref[...], wq_ref[...])
    width = query.shape[1]
    ones2 = ones_ref[...]
    lower = lower_mask(False)
    low = low_lanes(CH)
    for pair in range(width // 128):
        n, _ = unit(query[:, 128 * pair : 128 * pair + 128], ones2)
        sine, cosine = sin_cos(n, maps_ref[pair])
        values = v_ref[:, 128 * pair : 128 * pair + 128]
        for i in range(2):
            h = 2 * pair + i
            phi = jnp.concatenate(
                [sine[:, NF * i : NF * i + NF], cosine[:, NF * i : NF * i + NF]], 1
            ).astype(bf16)
            phiq_ref[:, FW * h : FW * h + FW] = phi
            raw = dot_nt(phi, phik_ref[:, FW * h : FW * h + FW])
            differ = col_ref[:, h : h + 1] - row_ref[GR + h : GR + h + 1, :]
            decay = jnp.exp2(jnp.where(lower, differ, -jnp.inf))
            scores = (raw * decay).astype(bf16)
            one = jnp.ones_like(values)
            augmented = jnp.where(low, one, values) if i else jnp.where(low, values, one)
            intra_ref[:, 128 * h : 128 * h + 128] = dot(scores, augmented)


def tokens_body(
    start_refs,
    x_ref,
    c_ref,
    phiq_ref,
    intra_ref,
    row_ref,
    col_ref,
    u_ref,
    mix_ref,
    up_ref,
    down_ref,
    vec_ref,
    upb_ref,
    ones_ref,
    select_ref,
    *refs,
    chunks,
    size,
):
    (
    out_ref,
    dr_ref,
    dn_ref,
    qside_ref,
    states_ref,
    vloc_ref,
    vdev_ref,
    sent_ref,
    packed_ref,
    vec_acc,
    state,
    heads_low,
    numer_all,
    inner_all,
    up_acc,
    down_acc,
    mix_acc,
    ) = refs
    b = pl.program_id(0)
    heads = state.shape[0]
    pairs = heads // 2

    @pl.when(b == 0)
    def _():
        mix_acc[...] = jnp.zeros_like(mix_acc)
        vec_acc[...] = jnp.zeros_like(vec_acc)
        up_acc[...] = jnp.zeros_like(up_acc)
        down_acc[...] = jnp.zeros_like(down_acc)

    low = low_lanes(CH)
    state[...] = sum(start_ref[0].astype(f32) for start_ref in start_refs)
    for c in range(chunks):
        rows = slice(CH * c, CH * c + CH)
        for pair in range(pairs):
            both = []
            for i in range(2):
                h = 2 * pair + i
                block = state[h].astype(bf16)
                states_ref[0, c, h] = block
                carry = dot_nt(phiq_ref[rows, FW * h : FW * h + FW], expand(block, i))
                carried = col_ref[rows, 4 * GR + h : 4 * GR + h + 1]
                both.append(intra_ref[rows, 128 * h : 128 * h + 128] + carried * carry)
                last = jnp.exp2(row_ref[c, h : h + 1, CH - 1 : CH])
                state[h] = last * state[h] + u_ref[0, c, h]
            lanes = slice(128 * pair, 128 * pair + 128)
            numer = jnp.where(low, both[0], both[1])
            inner = pltpu.roll(jnp.where(low, both[1], both[0]), HD, 1)
            numer_all[rows, lanes] = numer
            inner_all[rows, lanes] = inner
            heads_low[rows, lanes] = (numer * lax.rsqrt(inner * inner + 1.0)).astype(bf16)
    for h in range(heads):
        states_ref[0, chunks, h] = state[h].astype(bf16)

    mix = mix_ref[...]
    rest = heads_low[...]
    mixing_bias, gain, shift, down_bias = (vec_ref[i : i + 1, :] for i in range(4))
    residual = x_ref[...].astype(f32) + dot(rest, mix) + mixing_bias
    center = residual - jnp.mean(residual, -1, keepdims=True)
    scale = lax.rsqrt(jnp.mean(center * center, -1, keepdims=True) + 1e-05)
    normal = center * scale
    normal_low = (normal * gain + shift).astype(bf16)
    normal_t = normal_low.T
    upstream = c_ref[...]
    upstream_t = upstream.T
    result = residual + down_bias
    grad_normal = jnp.zeros_like(residual)
    for j in range(up_ref.shape[1] // TILE):
        part = slice(TILE * j, TILE * j + TILE)
        up = up_ref[:, part]
        down = down_ref[part, :]
        hidden = dot(normal_low, up) + upb_ref[:, part]
        square = hidden * hidden
        th = jnp.tanh(hidden * (GELU_A + (GELU_A * GELU_B) * square))
        half = 0.5 + 0.5 * th
        active = (hidden * half).astype(bf16)
        slope = half + hidden * (0.5 - 0.5 * th * th) * (
            GELU_A + (3.0 * GELU_A * GELU_B) * square
        )
        result += dot(active, down)
        grad_hidden = slope * dot_nt(upstream, down)
        grad_hidden = grad_hidden.astype(bf16)
        vec_acc[4 + j : 5 + j, :] += jnp.sum(grad_hidden.astype(f32), 0, keepdims=True)
        grad_normal += dot_nt(grad_hidden, up)
        up_acc[:, part] += dot(normal_t, grad_hidden)
        down_acc[:, part] += dot(upstream_t, active)
    out_ref[...] = result.astype(bf16)
    upstream = upstream.astype(f32)
    dn = grad_normal * gain
    grad_residual = upstream + scale * (
        dn
        - jnp.mean(dn, -1, keepdims=True)
        - normal * jnp.mean(dn * normal, -1, keepdims=True)
    )
    dr_ref[...] = grad_residual
    for i, value in enumerate((grad_residual, grad_normal * normal, grad_normal, upstream)):
        vec_acc[i : i + 1, :] += jnp.sum(value, 0, keepdims=True)
    grad_low = grad_residual.astype(bf16)
    mix_acc[...] += dot_tn(rest, grad_low)
    grad_heads = dot_nt(grad_low, mix)

    ones2 = ones_ref[...]
    following = [None] * heads
    for c in reversed(range(chunks)):
        rows = slice(CH * c, CH * c + CH)
        query_sides = []
        for pair in range(pairs):
            lanes = slice(128 * pair, 128 * pair + 128)
            numer, inner, grad = numer_all[rows, lanes], inner_all[rows, lanes], grad_heads[rows, lanes]
            square = 1.0 / (inner * inner + 1.0)
            grad_numer = grad * lax.rsqrt(inner * inner + 1.0)
            query_side = dot(split2_cat(grad_numer * numer), ones2) * square
            query_sides.append(query_side)
            grad_inner = pltpu.roll(query_side * inner * (-1.0 / HD), HD, 1)
            for i in range(2):
                h = 2 * pair + i
                if i:
                    together = jnp.where(low, grad_inner, grad_numer)
                else:
                    together = jnp.where(low, grad_numer, grad_inner)
                dn_ref[rows, 128 * h : 128 * h + 128] = together.astype(bf16)
                carried = col_ref[rows, 4 * GR + h : 4 * GR + h + 1]
                sent = (carried * together).T.astype(bf16)
                own = shrink(dot(sent, phiq_ref[rows, FW * h : FW * h + FW]), i)
                vloc_ref[0, c, h] = own
                if following[h] is not None:
                    last = jnp.exp2(row_ref[c, h : h + 1, CH - 1 : CH])
                    own = own + last * following[h]
                following[h] = own
        qside_ref[rows, :] = dot(
            split2_cat(jnp.concatenate(query_sides, 1)), select_ref[...]
        )
    for h in range(heads):
        vdev_ref[0, h] = following[h]
        sent_ref[0, h] = following[h].astype(bf16)

    @pl.when(b == pl.num_programs(0) - 1)
    def _():
        width, ff = up_acc.shape
        up_rows, down_rows, mix_rows = width // size, ff // size, mix_acc.shape[0] // size
        for d in range(size):
            at = d * (packed_ref.shape[0] // size)
            for j in range(ff // TILE):
                packed_ref[at : at + up_rows, :] = up_acc[
                    up_rows * d : up_rows * d + up_rows, TILE * j : TILE * j + TILE
                ].astype(bf16)
                at += up_rows
            packed_ref[at : at + down_rows, :] = (
                down_acc[:, down_rows * d : down_rows * d + down_rows].T.astype(bf16)
            )
            at += down_rows
            packed_ref[at : at + mix_rows, :] = mix_acc[
                mix_rows * d : mix_rows * d + mix_rows, :
            ].astype(bf16)


def query_back_body(
    x_ref,
    wq_ref,
    maps_back_ref,
    ones_ref,
    phiq_ref,
    phik_ref,
    v_ref,
    dn_ref,
    row_ref,
    col_ref,
    states_ref,
    *refs,
):
    dq_ref, dphik_ref, dv_ref, wqg_ref, *ticks = refs[-7:]
    clear(ticks)
    first = jnp.logical_and(pl.program_id(0) == 0, pl.program_id(1) == 0)

    @pl.when(first)
    def _():
        wqg_ref[...] = jnp.zeros_like(wqg_ref)

    x = x_ref[...]
    query = dot(x, wq_ref[...])
    width = query.shape[1]
    ones2 = ones_ref[...]
    mask = lower_mask(True)
    low = low_lanes(CH)
    for pair in range(width // 128):
        lanes = slice(128 * pair, 128 * pair + 128)
        n, inverse = unit(query[:, lanes], ones2)
        values = v_ref[:, lanes]
        angles = []
        for i in range(2):
            h = 2 * pair + i
            wide = slice(FW * h, FW * h + FW)
            phiq, phik = phiq_ref[:, wide], phik_ref[:, wide]
            grad = dn_ref[:, 128 * h : 128 * h + 128]
            differ = row_ref[h : h + 1, :] - col_ref[:, GR + h : GR + h + 1]
            decay = jnp.exp2(jnp.where(mask, differ, -jnp.inf))
            one = jnp.ones_like(values)
            augmented = jnp.where(low, one, values) if i else jnp.where(low, values, one)
            scores = (dot_nt(phik, phiq) * decay).astype(bf16)
            grad_raw = (dot_nt(augmented, grad) * decay).astype(bf16)
            dv_ref[:, 128 * h : 128 * h + 128] = dot(scores, grad).astype(bf16)
            dphik_ref[:, wide] = dot(grad_raw, phiq).astype(bf16)
            carried = col_ref[:, 4 * GR + h : 4 * GR + h + 1]
            dphi = dot_tn(grad_raw, phik) + carried * dot(grad, expand(states_ref[0, 0, h], i))
            dphi = dphi.astype(bf16).astype(f32)
            phiq = phiq.astype(f32)
            angles.append(dphi[:, :NF] * phiq[:, NF:] - dphi[:, NF:] * phiq[:, :NF])
        dq = feature_back(n, inverse, jnp.concatenate(angles, 1), maps_back_ref[pair], ones2)
        dq_ref[:, lanes] = dq.astype(bf16)
    wqg_ref[...] += dot_tn(x, dq_ref[...])


def key_back_body(
    end_refs,
    x_ref,
    wq_ref,
    wkv_ref,
    maps_back_ref,
    gw_ref,
    ones_ref,
    all_ref,
    tri_ref,
    phik_ref,
    v_ref,
    dq_ref,
    dphik_ref,
    dv_ref,
    qside_ref,
    row_ref,
    col_ref,
    states_ref,
    vloc_ref,
    dr_ref,
    factor_ref,
    *refs,
):
    dx_ref, wkvg_ref, gwg_ref, gbg_ref, *ticks, grads, state_grad, sides = refs[-10:]
    clear(ticks)
    first = jnp.logical_and(pl.program_id(0) == 0, pl.program_id(1) == 0)

    @pl.when(first)
    def _():
        wkvg_ref[...] = jnp.zeros_like(wkvg_ref)
        gwg_ref[...] = jnp.zeros_like(gwg_ref)
        gbg_ref[...] = jnp.zeros_like(gbg_ref)

    @pl.when(pl.program_id(1) == 0)
    def _():
        state_grad[...] = sum(end_ref[0].astype(f32) for end_ref in end_refs)

    x = x_ref[...]
    heads = state_grad.shape[0]
    keys = dot(x, wkv_ref[:, : wq_ref.shape[1]])
    width = wq_ref.shape[1]
    ones2 = ones_ref[...]
    low = low_lanes(CH)
    weigh = jnp.where(lax.broadcasted_iota(jnp.int32, (SR, FW), 0) < HD, 1.0, 4.0)
    bounds = []
    for pair in range(heads // 2):
        lanes = slice(128 * pair, 128 * pair + 128)
        n, inverse = unit(keys[:, lanes], ones2)
        values = v_ref[:, lanes]
        angles = []
        both = []
        for i in range(2):
            h = 2 * pair + i
            wide = slice(FW * h, FW * h + FW)
            phik = phik_ref[:, wide]
            one = jnp.ones_like(values)
            augmented = jnp.where(low, one, values) if i else jnp.where(low, values, one)
            tail = col_ref[:, 2 * GR + h : 2 * GR + h + 1]
            grad_end = state_grad[h]
            bounds.append(
                jnp.sum(grad_end * weigh * states_ref[0, 0, h].astype(f32), 0, keepdims=True)
            )
            spread = expand(grad_end.astype(bf16), i)
            dv = dv_ref[:, 128 * h : 128 * h + 128] + tail * dot_nt(phik, spread)
            sides[:, 128 * h : 128 * h + 128] = dv * augmented.astype(f32)
            both.append(dv)
            dphi = dphik_ref[:, wide].astype(f32) + tail * dot(augmented, spread)
            dphi = dphi.astype(bf16).astype(f32)
            phik = phik.astype(f32)
            angles.append(dphi[:, :NF] * phik[:, NF:] - dphi[:, NF:] * phik[:, :NF])
            last = jnp.exp2(row_ref[h : h + 1, CH - 1 : CH])
            state_grad[h] = last * grad_end + vloc_ref[0, 0, h]
        dk = feature_back(n, inverse, jnp.concatenate(angles, 1), maps_back_ref[pair], ones2)
        grads[:, lanes] = dk.astype(bf16)
        grads[:, width + 128 * pair : width + 128 * pair + 128] = jnp.where(
            low, both[0], both[1]
        ).astype(bf16)
    key_side = dot(split2_cat(sides[...]), all_ref[...])
    key_row = key_side.T[:GR]
    differ = qside_ref[...].T[:GR] - key_row
    bound = jnp.sum(jnp.concatenate(bounds, 0), 1, keepdims=True)
    bound = jnp.concatenate([bound, jnp.zeros((GR - heads, 1), f32)], 0)
    grad_log = dot(split3_cat(differ), tri_ref[...]) + bound
    gate, keep = row_ref[2 * GR : 3 * GR, :], row_ref[3 * GR : 4 * GR, :]
    grad_pre = (
        grad_log * keep - gate * key_row + factor_ref[...] * gate * keep
    ).astype(bf16)
    gbg_ref[...] += grad_pre.astype(f32)
    gwg_ref[...] += dot(grad_pre, x)
    together = grads[...]
    wkvg_ref[...] += dot_tn(x, together)
    dx_ref[...] = (
        dr_ref[...]
        + dot_nt(dq_ref[...], wq_ref[...])
        + dot_nt(together, wkv_ref[...])
        + dot_tn(grad_pre, gw_ref[...])
    )


def unpack_body(index_ref, every_ref, _, up_ref, down_ref, mix_ref, tick_ref, *, places):
    rows, ff = up_ref.shape
    width = down_ref.shape[1]
    depth = every_ref.shape[1]
    slab = depth * every_ref.shape[0] // pl.num_programs(0)
    tick_ref[...] = jnp.zeros_like(tick_ref)

    def copy(first, count, ref, lanes):
        done = 0
        while done < count:
            piece, at = divmod(first + done, depth)
            number = min(count - done, depth - at)
            ref[done : done + number, lanes] = every_ref[
                places[piece], at : at + number, :
            ].astype(f32)
            done += number

    for d in range(pl.num_programs(0)):

        @pl.when(pl.program_id(0) == d)
        def _(d=d):
            first = slab * d
            for j in range(ff // TILE):
                copy(first, rows, up_ref, slice(TILE * j, TILE * j + TILE))
                first += rows
            copy(first, down_ref.shape[0], down_ref, slice(0, width))
            first += down_ref.shape[0]

            @pl.when(index_ref[0] == d)
            def _():
                copy(first, mix_ref.shape[0], mix_ref, slice(0, width))


def tokens_entry(*refs, starts, **named):
    tokens_body(refs[:starts], *refs[starts:], **named)


def key_back_entry(*refs, arrivals):
    key_back_body(refs[:arrivals], *refs[arrivals:])


def whole(array):
    zeros = (0,) * len(array.shape)
    return pl.BlockSpec(array.shape, lambda *_: zeros, pipeline_mode=pl.Buffered(1))


def fixed(shape):
    zeros = (0,) * len(shape)
    return pl.BlockSpec(shape, lambda *_: zeros)


def call(body, grid, ins, outs, previous=(), after=(), scratch=(), name=None, flops=0, room=40):
    extra = list(previous) + list(after)
    specs = [spec for _, spec in ins] + [pl.BlockSpec(memory_space=pl.ANY)] * len(extra)
    return pl.pallas_call(
        body,
        grid=grid,
        in_specs=specs,
        out_specs=[spec for _, _, spec in outs],
        out_shape=[jax.ShapeDtypeStruct(shape, kind) for shape, kind, _ in outs],
        scratch_shapes=list(scratch),
        input_output_aliases={len(ins) + i: i for i in range(len(previous))},
        compiler_params=pltpu.CompilerParams(
            dimension_semantics=("arbitrary",) * len(grid), vmem_limit_bytes=room * 1024 * 1024
        ),
        cost_estimate=pl.CostEstimate(flops=flops, bytes_accessed=4 << 20, transcendentals=0),
        name=name,
    )(*[array for array, _ in ins], *extra)


def swap(x, axis, bit):
    size = lax.axis_size(axis)
    return lax.ppermute(x, axis, [(i, i ^ bit) for i in range(size)])


def spread_head(part):
    parts = [part]
    for k in range(1, lax.axis_size("head")):
        parts.append(swap(parts[k - 1], "head", 1) if k % 2 else swap(part, "head", k))
    return parts


def side(axis, bit):
    return (lax.axis_index(axis) // bit) % 2


class HalvingSum:
    def __init__(self, array):
        self.terms = [(array, 0)]
        self.length = array.shape[0]

    def part(self, offset, tick=0.0):
        total = tick
        for array, start in self.terms:
            piece = lax.dynamic_slice_in_dim(array, start + offset, self.length, 0)
            total = total + piece.astype(f32)
        return total.astype(bf16)

    def step(self, axis, bit, tick=0.0):
        self.length //= 2
        mine = side(axis, bit)
        send = self.part((1 - mine) * self.length, tick)
        self.terms = [(array, start + mine * self.length) for array, start in self.terms]
        self.terms.append((swap(send, axis, bit), 0))
        return send


def join(array, axis, bit):
    return order_halves(array, swap(array, axis, bit), side(axis, bit))


def order_halves(mine, other, upper):
    return jnp.where(
        upper == 0, jnp.concatenate([mine, other], 0), jnp.concatenate([other, mine], 0)
    )


def gather_all(piece, stages):
    every = lax.all_gather(piece, ("dp", "head"), axis=0, tiled=False)
    names = [
        (axis, 1 << i)
        for axis in ("dp", "head")
        for i in reversed(range(lax.axis_size(axis).bit_length() - 1))
    ]
    places = np.arange(1 << len(names)).reshape((2,) * len(names))
    places = places.transpose([names.index(stage) for stage in stages]).reshape(-1)
    if piece.shape[0] % GR:
        every = every[places].reshape(1, -1, piece.shape[1])
        places = places[:1] * 0
    return every, tuple(int(place) for place in places)


def high_rest(x):
    high = lax.reduce_precision(x, 8, 7)
    return high, x - high


def per_device(
    tokens,
    cotangent,
    carry_state,
    carry_norm,
    random_maps,
    query_weight,
    key_weight,
    value_weight,
    gate_weight,
    gate_bias,
    mixing_weight,
    mixing_bias,
    norm_gain,
    norm_bias,
    up_weight,
    up_bias,
    down_weight,
    down_bias,
):
    seqs, length, width = tokens.shape
    here = gate_weight.shape[1]
    size = lax.axis_size("head")
    replicas = lax.axis_size("dp")
    index = lax.axis_index("head")
    heads = here * size
    chunks = length // CH
    blocks = seqs * chunks
    count = seqs * length
    inner_width = heads * HD
    own = here * HD
    ff = up_weight.shape[1]
    pairs = heads // 2
    head_bits = [1 << i for i in range(size.bit_length() - 1)]
    dp_bits = [1 << i for i in range(replicas.bit_length() - 1)]
    index_array = index.astype(jnp.int32).reshape(1)
    smem = pl.BlockSpec(memory_space=pltpu.SMEM)

    scaled = random_maps.reshape(own, NF) * (0.5 / math.pi)
    map_high, map_rest = high_rest(scaled)
    bias_high, bias_rest = high_rest(gate_bias)
    bias_mid, bias_rest = high_rest(bias_rest)
    biases = jnp.pad(jnp.stack([bias_high, bias_mid, bias_rest]), ((0, 0), (0, 128 - here)))
    tail = jnp.concatenate([gate_weight.T.reshape(-1, 128).astype(f32), biases])
    tail = jnp.pad(tail, ((0, GR - tail.shape[0]), (0, 0)))
    key_value = jnp.concatenate([key_weight, value_weight], 0 if here == 2 else 1)
    first_part = jnp.concatenate(
        [key_value]
        + [part.astype(bf16) for part in (map_high, map_rest, tail)]
    )
    half = width // 2
    query_rows = (
        query_weight
        if here == 2
        else jnp.concatenate([query_weight[:half], query_weight[half:]], 1)
    )
    second_part = jnp.concatenate(
        [query_rows] + [mixing_weight[:, 128 * j : 128 * j + 128] for j in range(width // 128)]
    )
    first_parts = spread_head(first_part)

    begin = jnp.concatenate(
        [
            carry_state.transpose(0, 1, 3, 2),
            jnp.broadcast_to(carry_norm[:, :, None, :], (seqs, here, SR - HD, FW)),
        ],
        2,
    ).astype(bf16)

    half = np.arange(128) // HD
    ones2 = np.tile((half[:, None] == half[None, :]).astype(np.float32), (2, 1))
    ones2 = jnp.asarray(ones2, bf16)
    place = np.arange(CH)
    upto = jnp.asarray(np.tile((place[:, None] <= place[None, :]).astype(np.float32), (3, 1)), bf16)
    onward = jnp.asarray(np.tile((place[:, None] >= place[None, :]).astype(np.float32), (3, 1)), bf16)
    lane = np.arange(128)
    one_lane = np.zeros((inner_width, 128), np.float32)
    one_lane[np.arange(heads) * HD, np.arange(heads)] = 1.0
    select = jnp.asarray(np.tile(one_lane, (2, 1)), bf16)
    all_lanes = (np.arange(heads * 128) // 128)[:, None] == lane[None, :]
    all_lanes = jnp.asarray(np.tile(all_lanes.astype(np.float32), (2, 1)), bf16)

    x = tokens.reshape(count, width)
    c = cotangent.reshape(count, width)
    state_shape = (heads, SR, FW)
    tick_outs = [((1, lanes), f32, fixed((1, lanes))) for lanes in (128, FW, width)]

    def rows_of(columns, base=0, reverse=False):
        def at(b, t):
            return ((base + b) * chunks + (chunks - 1 - t if reverse else t), 0)

        return pl.BlockSpec((CH, columns), at)

    def row_spec(base=0, reverse=False):
        return pl.BlockSpec((4 * GR, CH), rows_of(0, base, reverse).index_map)

    def per_block(shape, base=0, offset=0, reverse=False):
        zeros = (0,) * len(shape)

        def at(b, t):
            return (base + b, offset + (chunks - 1 - t if reverse else t)) + zeros

        return pl.BlockSpec((1, 1) + shape, at)

    def per_seq(base=0):
        return pl.BlockSpec((1,) + state_shape, lambda b, t: (base + b, 0, 0, 0))

    weights = [
        ((width, 2 * inner_width), bf16),
        ((pairs, 3 * 128, FW), bf16),
        ((pairs, 3 * FW, 128), bf16),
        ((GR, width), bf16),
        ((inner_width, width), bf16),
        ((GR, CH), f32),
    ]
    weights = [(shape, kind, fixed(shape)) for shape, kind in weights]

    def keys_ins(base):
        return [(x, rows_of(width, base)), (ones2, whole(ones2)), (upto, whole(upto))]

    def keys_outs(base):
        total_spec = pl.BlockSpec((1, GR, 128), lambda b, t: (base + b, 0, 0))
        return [
            ((count, heads * FW), bf16, rows_of(heads * FW, base)),
            ((count, inner_width), bf16, rows_of(inner_width, base)),
            ((blocks * 4 * GR, CH), f32, row_spec(base)),
            ((count, 128), f32, rows_of(128, base)),
            ((seqs, chunks) + state_shape, f32, per_block(state_shape, base)),
            ((seqs,) + state_shape, f32, per_seq(base)),
            ((seqs, GR, 128), f32, total_spec),
            ((GR, CH), f32, fixed((GR, CH))),
            ((1, FW), f32, fixed((1, FW))),
        ]

    *previous, gate_sums, tick, wkv, maps_front, maps_back, gw, wvt, gb = call(
        functools.partial(keys_body, size=size, here=here, skipped=2),
        (2, chunks),
        [(part, whole(part)) for part in first_parts] + [(index_array, smem)] + keys_ins(0),
        keys_outs(0) + weights,
        after=[second_part, begin],
        scratch=[
            pltpu.VMEM(state_shape, f32),
            pltpu.VMEM((size,) + first_part.shape, bf16),
        ],
        name="keys",
        flops=10_000_000_000,
    )
    second_parts = [second_part] + [swap(second_part, "head", k) for k in range(1, size)]
    begins = [jnp.where(index == 0, begin, jnp.zeros_like(begin))] + [
        lax.ppermute(begin, "head", [(k, 0)]) for k in range(1, size)
    ]
    phik, v, row, col, update, end, total, more_sums, tick = call(
        functools.partial(keys_body, size=0, here=here, skipped=2 * size - 2 + len(previous)),
        (seqs - 2, chunks),
        [(part, whole(part)) for part in (wkv, maps_front, gw, wvt, gb)] + keys_ins(2),
        keys_outs(2),
        previous=previous,
        after=second_parts[1:] + begins[1:],
        scratch=[pltpu.VMEM(state_shape, f32)],
        name="keys",
        flops=10_000_000_000,
    )
    gate_sums = gate_sums[:heads] + more_sums[:heads]
    gate_sums = gate_sums[:, :128] + gate_sums[:, 128:]
    last = jnp.exp2(total[:, :heads, 0])[:, :, None, None]
    begin = jnp.concatenate(begins, 1)
    sum_steps = [("head", bit) for bit in head_bits] + [("dp", bit) for bit in dp_bits]

    sent = (end + last * begin.astype(f32)).astype(bf16)
    starts = [begin]
    ticks = (0.0, 0.0, 0.0)
    coming = gate_sums
    phiq = intra = wq = mix = None
    previous = ()
    for step, (base, number) in enumerate(((0, 1), (1, 2), (3, 1))):
        arrived = None
        if step < size - 1:
            arrived = lax.ppermute(sent, "head", [(step, step + 1)])
            starts.append(arrived)
        coming = swap(gate_sums, *sum_steps[step])
        main = [
            (x, rows_of(width, base)),
            (maps_front, whole(maps_front)),
            (ones2, whole(ones2)),
            (phik, rows_of(heads * FW, base)),
            (v, rows_of(inner_width, base)),
            (row, row_spec(base)),
            (col, rows_of(128, base)),
        ]
        outs = [
            ((count, heads * FW), bf16, rows_of(heads * FW, base)),
            ((count, heads * 128), f32, rows_of(heads * 128, base)),
        ] + tick_outs
        if step == 0:
            phiq, intra, *ticks, wq, mix = call(
                functools.partial(queries_body, size=size, here=here, skipped=2),
                (number, chunks),
                [(part, whole(part)) for part in second_parts] + [(index_array, smem)] + main,
                outs
                + [
                    ((width, inner_width), bf16, fixed((width, inner_width))),
                    ((inner_width, width), bf16, fixed((inner_width, width))),
                ],
                after=[sent, gate_sums],
                scratch=[pltpu.VMEM((size,) + second_part.shape, bf16)],
                name="queries",
                flops=5_000_000_000,
            )
        else:
            phiq, intra, *ticks = call(
                functools.partial(queries_body, size=0, here=here, skipped=4),
                (number, chunks),
                [(wq, whole(wq))] + main,
                outs,
                previous=[phiq, intra],
                after=[sent, gate_sums],
                name="queries",
                flops=5_000_000_000 * number,
            )
        gate_sums = gate_sums + coming + ticks[0]
        if step < size - 2:
            sent = (last * arrived.astype(f32) + end + ticks[1][0]).astype(bf16)
    for step in range(3, size - 1):
        arrived = lax.ppermute(sent, "head", [(step, step + 1)])
        starts.append(arrived)
        sent = (last * arrived.astype(f32) + end).astype(bf16)

    vectors = jnp.stack([mixing_bias, norm_gain, norm_bias, down_bias] * 2)

    def seq_rows(columns):
        return pl.BlockSpec((length, columns), lambda b: (b, 0))

    def seq_block(*shape):
        zeros = (0,) * len(shape)
        return pl.BlockSpec((1,) + shape, lambda b: (b,) + zeros)

    up_bias2 = up_bias.reshape(1, ff)
    slab = (width // size) * (ff // TILE) + ff // size + own
    layer_out, dr, dn, qside, states, vloc, vdev, sent, packed, vector_grads = call(
        functools.partial(
            tokens_entry, starts=len(starts), chunks=chunks, size=size
        ),
        (seqs,),
        [(start, seq_block(*state_shape)) for start in starts]
        + [
            (x, seq_rows(width)),
            (c, seq_rows(width)),
            (phiq, seq_rows(heads * FW)),
            (intra, seq_rows(heads * 128)),
            (
                row.reshape(blocks, 4 * GR, CH),
                pl.BlockSpec((chunks, 4 * GR, CH), lambda b: (b, 0, 0)),
            ),
            (col, seq_rows(128)),
            (update, seq_block(chunks, *state_shape)),
            (mix, whole(mix)),
            (up_weight, whole(up_weight)),
            (down_weight, whole(down_weight)),
            (vectors, whole(vectors)),
            (up_bias2, whole(up_bias2)),
            (ones2, whole(ones2)),
            (select, whole(select)),
        ],
        [
            ((count, width), bf16, seq_rows(width)),
            ((count, width), f32, seq_rows(width)),
            ((count, heads * 128), bf16, seq_rows(heads * 128)),
            ((count, 128), f32, seq_rows(128)),
            ((seqs, chunks + 1) + state_shape, bf16, seq_block(chunks + 1, *state_shape)),
            ((seqs, chunks) + state_shape, f32, seq_block(chunks, *state_shape)),
            ((seqs,) + state_shape, f32, seq_block(*state_shape)),
            ((seqs,) + state_shape, bf16, seq_block(*state_shape)),
            ((size * slab, width), bf16, fixed((size * slab, width))),
            ((8, width), f32, fixed((8, width))),
        ],
        scratch=[
            pltpu.VMEM(state_shape, f32),
            pltpu.VMEM((length, inner_width), bf16),
            pltpu.VMEM((length, inner_width), f32),
            pltpu.VMEM((length, inner_width), f32),
            pltpu.VMEM((width, ff), f32),
            pltpu.VMEM((width, ff), f32),
            pltpu.VMEM((inner_width, width), f32),
        ],
        name="tokens",
        room=62,
        flops=50_000_000_000,
    )

    stages = (
        [("head", 1)]
        + [("dp", bit) for bit in dp_bits[:1]]
        + [("head", bit) for bit in head_bits[1:]]
        + [("dp", bit) for bit in dp_bits[1:]]
    )
    waiting = list(stages)
    sums = HalvingSum(packed)
    ticks = (0.0, [0.0], 0.0)
    finishes = []
    dq = dphik = dv = None
    previous = []
    query_grads = []
    for step, (base, number) in enumerate(((0, 1), (1, 2), (3, 1))):
        after = [sums.step(*waiting.pop(0), ticks[2])]
        if step + 3 < len(sum_steps):
            after.append(gate_sums)
            coming = swap(gate_sums, *sum_steps[step + 3])
        if step < size - 1:
            arrived = lax.ppermute(sent, "head", [(size - 1 - step, size - 2 - step)])
            finishes.append(arrived)
            after.append(sent)
        dq, dphik, dv, query_grad, *ticks = call(
            query_back_body,
            (number, chunks),
            [
                (x, rows_of(width, base)),
                (wq, whole(wq)),
                (maps_back, whole(maps_back)),
                (ones2, whole(ones2)),
                (phiq, rows_of(heads * FW, base)),
                (phik, rows_of(heads * FW, base)),
                (v, rows_of(inner_width, base)),
                (dn, rows_of(heads * 128, base)),
                (row, row_spec(base)),
                (col, rows_of(128, base)),
                (states, per_block(state_shape, base)),
            ],
            [
                ((count, inner_width), bf16, rows_of(inner_width, base)),
                ((count, heads * FW), bf16, rows_of(heads * FW, base)),
                ((count, heads * 128), bf16, rows_of(heads * 128, base)),
                ((width, inner_width), f32, fixed((width, inner_width))),
            ] + tick_outs,
            previous=previous,
            after=after,
            name="query_back",
            flops=8_000_000_000 * number,
        )
        previous = [dq, dphik, dv]
        query_grads.append(query_grad)
        if step + 3 < len(sum_steps):
            gate_sums = gate_sums + coming + ticks[0]
        if step < size - 2:
            sent = (last * arrived.astype(f32) + vdev + ticks[1][0]).astype(bf16)
    for step in range(3, size - 1):
        arrived = lax.ppermute(sent, "head", [(size - 1 - step, size - 2 - step)])
        finishes.append(arrived)
        sent = (last * arrived.astype(f32) + vdev).astype(bf16)

    for axis, bit in sum_steps[6:]:
        gate_sums = gate_sums + swap(gate_sums, axis, bit)
    gate_total = jnp.sum(gate_sums)
    gate_count = replicas * heads * size * count
    mean_gate = gate_total / gate_count
    factor = 2.0 * penalty_weight * (mean_gate - target_gate) / heads
    factor = jnp.broadcast_to(factor, (1, CH))

    tokens_grad = None
    previous = []
    key_value_grads, gate_grads, gate_bias_grads = [], [], []
    for base, number in ((0, 1), (1, 1), (2, 2)):
        after = []
        if waiting and base < 2:
            after = [sums.step(*waiting.pop(0), ticks[2])]
        elif base == 2:
            for axis, bit in waiting:
                sums.step(axis, bit)
            piece = sums.part(0, ticks[2])
            after = [piece]
            every, places = gather_all(piece, stages)
        tokens_grad, key_value_grad, gate_grad, gate_bias_grad, *ticks = call(
            functools.partial(key_back_entry, arrivals=len(finishes)),
            (number, chunks),
            [(finish, per_seq(base)) for finish in finishes]
            + [
                (x, rows_of(width, base, True)),
                (wq, whole(wq)),
                (wkv, whole(wkv)),
                (maps_back, whole(maps_back)),
                (gw, whole(gw)),
                (ones2, whole(ones2)),
                (all_lanes, whole(all_lanes)),
                (onward, whole(onward)),
                (phik, rows_of(heads * FW, base, True)),
                (v, rows_of(inner_width, base, True)),
                (dq, rows_of(inner_width, base, True)),
                (dphik, rows_of(heads * FW, base, True)),
                (dv, rows_of(heads * 128, base, True)),
                (qside, rows_of(128, base, True)),
                (row, row_spec(base, True)),
                (col, rows_of(128, base, True)),
                (states, per_block(state_shape, base, 1, True)),
                (vloc, per_block(state_shape, base, 0, True)),
                (dr, rows_of(width, base, True)),
                (factor, whole(factor)),
            ],
            [
                ((count, width), f32, rows_of(width, base, True)),
                ((width, 2 * inner_width), f32, fixed((width, 2 * inner_width))),
                ((GR, width), f32, fixed((GR, width))),
                ((GR, CH), f32, fixed((GR, CH))),
            ] + tick_outs,
            previous=previous,
            after=after,
            scratch=[
                pltpu.VMEM((CH, 2 * inner_width), bf16),
                pltpu.VMEM(state_shape, f32),
                pltpu.VMEM((CH, heads * 128), f32),
            ],
            name="key_back",
            flops=8_000_000_000 * number,
        )
        previous = [tokens_grad]
        key_value_grads.append(key_value_grad)
        gate_grads.append(gate_grad)
        gate_bias_grads.append(gate_bias_grad)
    def by_bits(matrix):
        number = len(head_bits)
        matrix = matrix.reshape((2,) * number + matrix.shape[1:])
        matrix = matrix.transpose(tuple(reversed(range(number))) + (number, number + 1))
        return matrix.reshape((size,) + matrix.shape[number:])

    def by_device(matrix):
        matrix = matrix.astype(bf16).reshape((-1,) + (2,) * len(head_bits) + (own,))
        number = len(head_bits)
        return matrix.transpose(tuple(reversed(range(1, number + 1))) + (0, number + 1)).reshape(
            size, -1, own
        )

    query_grad = sum(query_grads)
    key_value_grad = sum(key_value_grads)
    gate_grad = sum(gate_grads)[:heads].astype(bf16).reshape(size, -1, own)
    gate_bias_grad = jnp.sum(sum(gate_bias_grads)[:heads], 1).astype(bf16).reshape(size, 1, here)
    gate_bias_grad = jnp.pad(gate_bias_grad, ((0, 0), (0, 15), (0, own - here)))
    vector_rows = vector_grads.reshape(-1, own).astype(bf16)
    group = jnp.concatenate(
        [
            by_device(query_grad),
            by_device(key_value_grad[:, :inner_width]),
            by_device(key_value_grad[:, inner_width:]),
            by_bits(gate_grad),
            by_bits(gate_bias_grad),
            jnp.broadcast_to(vector_rows, (size,) + vector_rows.shape),
        ],
        1,
    )
    rows = group.shape[1]
    group = jnp.pad(group, ((0, 0), (0, -rows % (replicas * 2)), (0, 0)))
    group_sums = HalvingSum(group.reshape(-1, own))
    for bit in head_bits:
        group_sums.step("head", bit)
    for bit in dp_bits:
        group_sums.step("dp", bit)
    group = group_sums.part(0)
    for bit in reversed(dp_bits[1:]):
        group = join(group, "dp", bit)
    other = swap(group, "dp", 1)
    up_grad, down_grad, mixing_grad, tick = call(
        functools.partial(unpack_body, places=places),
        (size,),
        [(index_array, smem), (every, whole(every))],
        [
            ((width, ff), f32, pl.BlockSpec((width // size, ff), lambda d: (d, 0))),
            ((ff, width), f32, pl.BlockSpec((ff // size, width), lambda d: (d, 0))),
            ((own, width), f32, fixed((own, width))),
            ((1, own), f32, fixed((1, own))),
        ],
        after=[group],
        name="unpack",
        flops=1_000_000_000,
    )
    group = order_halves(group + tick.astype(bf16), other, side("dp", 1))
    group = group.astype(f32)
    gate_rows = here * width // own
    gate_grad = group[3 * width : 3 * width + gate_rows].reshape(here, width).T
    vector_grads = group[3 * width + gate_rows + 16 : rows].reshape(8, width)
    penalty = penalty_weight * (mean_gate - target_gate) * (mean_gate - target_gate)
    return (
        layer_out.reshape(seqs, length, width),
        tokens_grad.reshape(seqs, length, width),
        penalty,
        group[:width],
        group[width : 2 * width],
        group[2 * width : 3 * width],
        gate_grad,
        group[3 * width + gate_rows, :here],
        mixing_grad,
        vector_grads[0],
        vector_grads[1],
        vector_grads[2],
        up_grad,
        vector_grads[4:].reshape(ff),
        down_grad,
        vector_grads[3],
    )


def solution(mesh):
    placed = (
        P("dp", "head", None),
        P("dp", "head", None),
        P("dp", "head", None, None),
        P("dp", "head", None),
        P("head", None, None),
        P(None, "head"),
        P(None, "head"),
        P(None, "head"),
        P(None, "head"),
        P("head"),
        P("head", None),
        P(),
        P(),
        P(),
        P(),
        P(),
        P(),
        P(),
    )
    return jax.shard_map(
        per_device,
        mesh=mesh,
        in_specs=placed,
        out_specs=(
            P("dp", "head", None),
            P("dp", "head", None),
            P(),
            P(None, "head"),
            P(None, "head"),
            P(None, "head"),
            P(None, "head"),
            P("head"),
            P("head", None),
            P(),
            P(),
            P(),
            P(),
            P(),
            P(),
            P(),
        ),
        check_vma=False,
    )
```

```python
import functools
import math

import jax
import jax.numpy as jnp
import numpy as np
from jax import lax
from jax.experimental import pallas as pl
from jax.experimental.pallas import tpu as pltpu
from jax.sharding import PartitionSpec as P

CH = 256
HD = 64
NF = 128
FW = 2 * NF
SR = 80
GR = 16
TILE = 512

penalty_weight = 32.0
target_gate = 0.9
LOG2E = 1.4426950408889634
SIN_POLY = (
    3.1415925800446116,
    -5.16770687892007,
    2.5500313771889287,
    -0.5980451736320438,
    0.07722012807955428,
)
COS_POLY = (
    0.9999999534665498,
    -4.934792858660313,
    4.058411913867723,
    -1.3318801593312537,
    0.2196967947670672,
)
GELU_A = 0.7978845608028654
GELU_B = 0.044715

f32 = jnp.float32
bf16 = jnp.bfloat16


def dot(a, b):
    return lax.dot_general(a, b, (((1,), (0,)), ((), ())), preferred_element_type=f32)


def dot_nt(a, b):
    return lax.dot_general(a, b, (((1,), (1,)), ((), ())), preferred_element_type=f32)


def dot_tn(a, b):
    return lax.dot_general(a, b, (((0,), (0,)), ((), ())), preferred_element_type=f32)


def split2(x):
    high = x.astype(bf16)
    return high, (x - high.astype(f32)).astype(bf16)


def split2_cat(x):
    return jnp.concatenate(split2(x), 1)


def split3_cat(x):
    high = x.astype(bf16)
    rest = x - high.astype(f32)
    mid = rest.astype(bf16)
    return jnp.concatenate([high, mid, (rest - mid.astype(f32)).astype(bf16)], 1)


def low_lanes(rows):
    return lax.broadcasted_iota(jnp.int32, (rows, 128), 1) < HD


def unit(u, ones2):
    inverse = lax.rsqrt(dot(split2_cat(u * u), ones2) + 1e-06)
    return u * inverse, inverse


def sin_cos(n, maps):
    high, rest = split2(n)
    turns = dot(jnp.concatenate([high, rest, high], 1), maps)
    r = turns - jnp.round(turns)
    u = r * r
    scale = math.sqrt(2.0 / math.sqrt(NF))
    s = SIN_POLY[4] * scale
    c = COS_POLY[4] * scale
    for i in (3, 2, 1, 0):
        s = s * u + SIN_POLY[i] * scale
        c = c * u + COS_POLY[i] * scale
    s = s * r
    return s * c, 1.0 / math.sqrt(NF) - s * s


def feature_back(n, inverse, angle_grad, maps_back, ones2):
    high, rest = split2(angle_grad)
    dn = dot(jnp.concatenate([high, rest, high], 1), maps_back)
    radial = dot(split2_cat(n * dn), ones2)
    return (dn - n * radial) * inverse


def expand(block, odd):
    state, norm = block[:HD], block[HD:SR]
    parts = [norm] * (HD // (SR - HD))
    return jnp.concatenate(parts + [state] if odd else [state] + parts, 0)


def shrink(block, odd):
    if odd:
        return jnp.concatenate([block[HD:], block[HD - (SR - HD) : HD]], 0)
    return block[:SR]


def clear(refs):
    for ref in refs:
        ref[...] = jnp.zeros_like(ref)


def collect(held, parts, index):
    for k, part in enumerate(parts):
        held[index ^ k] = part[...]


def block_pair(even, odd):
    none = jnp.zeros_like(even)
    return jnp.concatenate(
        [jnp.concatenate([even, none], 1), jnp.concatenate([none, odd], 1)], 0
    )


def keys_setup(held, here, wkv_ref, wvt, maps_ref, back_ref, gw_ref, gb):
    size = held.shape[0]
    width = wkv_ref.shape[0]
    inner = wvt.shape[0]
    at = width * here
    high, rest, gates, biases = [], [], [], []
    for d in range(size):
        if here == 2:
            lanes = slice(128 * d, 128 * d + 128)
            wkv_ref[:, lanes] = held[d, :width]
            wkv_ref[:, inner + 128 * d : inner + 128 * d + 128] = held[d, width : 2 * width]
            wvt[lanes, :] = held[d, width : 2 * width].T
        elif d % 2:
            lanes = slice(64 * d - 64, 64 * d + 64)
            one, two = held[d - 1, :width], held[d, :width]
            wkv_ref[:, lanes] = jnp.concatenate([one[:, :HD], two[:, :HD]], 1)
            values = jnp.concatenate([one[:, HD:], two[:, HD:]], 1)
            wkv_ref[:, inner + 64 * d - 64 : inner + 64 * d + 64] = values
            wvt[lanes, :] = values.T
        for i in range(here):
            first = at + HD * i
            high.append(held[d, first : first + HD])
            rest.append(held[d, first + HD * here : first + HD * here + HD])
        tail = held[d, at + 2 * HD * here :].astype(f32)
        for i in range(here):
            gates.append(
                jnp.concatenate([tail[4 * i + j : 4 * i + j + 1] for j in range(width // 128)], 1)
            )
            bias = sum(tail[4 * here + j : 4 * here + j + 1, i : i + 1] for j in range(3))
            biases.append(jnp.broadcast_to(bias, (1, CH)))
    for pair in range(len(high) // 2):
        top = block_pair(high[2 * pair], high[2 * pair + 1])
        low = block_pair(rest[2 * pair], rest[2 * pair + 1])
        maps_ref[pair] = jnp.concatenate([top, top, low], 0)
        back = ((top.astype(f32) + low.astype(f32)) * (2.0 * math.pi)).T
        top, low = split2(back)
        back_ref[pair] = jnp.concatenate([top, top, low], 0)
    heads = len(gates)
    gw_ref[...] = jnp.concatenate(gates + [jnp.zeros((GR - heads, width), f32)], 0).astype(bf16)
    gb[...] = jnp.concatenate(biases + [jnp.zeros((GR - heads, CH), f32)], 0)


def keys_body(*refs, size, here, skipped):
    if size:
        parts, index_ref, refs = refs[:size], refs[size], refs[size + 1 :]
        held, refs = refs[-1], refs[:-1]
        wkv_ref, maps_ref, back_ref, gw_ref, wvt_ref, gb_ref = refs[-7:-1]
        refs = refs[:-7] + refs[-1:]
    else:
        wkv_ref, maps_ref, gw_ref, wvt_ref, gb_ref = refs[:5]
        refs = refs[5:]
    refs = refs[:3] + refs[3 + skipped :]
    (
        x_ref,
        ones_ref,
        tri_ref,
        phik_ref,
        v_ref,
        row_ref,
        col_ref,
        u_ref,
        end_ref,
        tot_ref,
        gsum_ref,
        tick_ref,
        acc,
    ) = refs
    tick_ref[...] = jnp.zeros_like(tick_ref)
    b, c = pl.program_id(0), pl.program_id(1)

    if size:

        @pl.when(jnp.logical_and(b == 0, c == 0))
        def _():
            collect(held, parts, index_ref[0])
            keys_setup(held, here, wkv_ref, wvt_ref, maps_ref, back_ref, gw_ref, gb_ref)

    x = x_ref[...]
    kv = dot(x, wkv_ref[...])
    width = kv.shape[1] // 2
    keys = kv[:, :width]
    v_ref[...] = kv[:, width:].astype(bf16)
    vt = dot_nt(wvt_ref[...], x).astype(bf16)
    pre = dot_nt(gw_ref[...], x) + gb_ref[...]
    soft = jnp.log1p(jnp.exp(-jnp.abs(pre)))
    log_gate = -(jnp.maximum(-pre, 0.0) + soft)
    log_keep = -(jnp.maximum(pre, 0.0) + soft)
    gate = jnp.exp(log_gate)
    keep = jnp.exp(log_keep)
    cumul = dot(split3_cat(log_gate * LOG2E), tri_ref[...])
    shifted = cumul - log_keep * LOG2E
    total = cumul[:, CH - 1 : CH]
    tail = jnp.exp2(total - shifted)
    row_ref[...] = jnp.concatenate([cumul, shifted, gate, keep], 0)
    stack = jnp.concatenate(
        [cumul, shifted, tail, gate, jnp.exp2(cumul), keep, keep, keep], 0
    )
    col_ref[...] = stack.T

    @pl.when(jnp.logical_and(b == 0, c == 0))
    def _():
        gsum_ref[...] = jnp.zeros_like(gsum_ref)

    gsum_ref[...] += gate

    @pl.when(c == 0)
    def _():
        acc[...] = jnp.zeros_like(acc)
        tot_ref[0] = jnp.zeros_like(tot_ref[0])

    tot_ref[0] += jnp.broadcast_to(total, tot_ref.shape[1:])
    ones2 = ones_ref[...]
    block_ones = jnp.ones((SR - HD, CH), f32)
    for pair in range(width // 128):
        n, _ = unit(keys[:, 128 * pair : 128 * pair + 128], ones2)
        sine, cosine = sin_cos(n, maps_ref[pair])
        for i in range(2):
            h = 2 * pair + i
            phi = jnp.concatenate(
                [sine[:, NF * i : NF * i + NF], cosine[:, NF * i : NF * i + NF]], 1
            ).astype(bf16)
            phik_ref[:, FW * h : FW * h + FW] = phi
            weighted = jnp.concatenate([vt[HD * h : HD * h + HD].astype(f32), block_ones], 0)
            weighted = (weighted * tail[h : h + 1]).astype(bf16)
            update = dot(weighted, phi)
            u_ref[0, 0, h] = update
            acc[h] = jnp.exp2(total[h : h + 1]) * acc[h] + update

    @pl.when(c == pl.num_programs(1) - 1)
    def _():
        end_ref[0] = acc[...].astype(bf16)


def lower_mask(flip):
    rows = lax.broadcasted_iota(jnp.int32, (CH, CH), 0)
    columns = lax.broadcasted_iota(jnp.int32, (CH, CH), 1)
    return rows <= columns if flip else rows >= columns


def queries_setup(held, here, wq_ref, mix_ref):
    size = held.shape[0]
    width = wq_ref.shape[0]
    for d in range(size):
        at = width * here // 2
        rows = HD * here
        if here == 2:
            wq_ref[:, 128 * d : 128 * d + 128] = held[d, :width]
        elif d % 2:
            one, two = held[d - 1, :at], held[d, :at]
            lanes = slice(64 * d - 64, 64 * d + 64)
            wq_ref[:at, lanes] = jnp.concatenate([one[:, :HD], two[:, :HD]], 1)
            wq_ref[at:, lanes] = jnp.concatenate([one[:, HD:], two[:, HD:]], 1)
        for j in range(width // 128):
            mix_ref[rows * d : rows * d + rows, 128 * j : 128 * j + 128] = held[
                d, at + rows * j : at + rows * j + rows
            ]


def queries_body(*refs, size, here, skipped):
    parts, refs = refs[:size], refs[size:]
    if size:
        index_ref, refs = refs[0], refs[1:]
        held, refs = refs[-1], refs[:-1]
        wq_ref, mix_ref = refs[-2:]
        refs = refs[:-2]

        @pl.when(jnp.logical_and(pl.program_id(0) == 0, pl.program_id(1) == 0))
        def _():
            collect(held, parts, index_ref[0])
            queries_setup(held, here, wq_ref, mix_ref)

    else:
        wq_ref, refs = refs[0], refs[1:]
    x_ref, maps_ref, ones_ref, phik_ref, v_ref, row_ref, col_ref = refs[:7]
    phiq_ref, intra_ref, *ticks = refs[7 + skipped :]
    clear(ticks)
    query = dot(x_ref[...], wq_ref[...])
    width = query.shape[1]
    ones2 = ones_ref[...]
    lower = lower_mask(False)
    low = low_lanes(CH)
    for pair in range(width // 128):
        n, _ = unit(query[:, 128 * pair : 128 * pair + 128], ones2)
        sine, cosine = sin_cos(n, maps_ref[pair])
        values = v_ref[:, 128 * pair : 128 * pair + 128]
        for i in range(2):
            h = 2 * pair + i
            phi = jnp.concatenate(
                [sine[:, NF * i : NF * i + NF], cosine[:, NF * i : NF * i + NF]], 1
            ).astype(bf16)
            phiq_ref[:, FW * h : FW * h + FW] = phi
            raw = dot_nt(phi, phik_ref[:, FW * h : FW * h + FW])
            differ = col_ref[:, h : h + 1] - row_ref[GR + h : GR + h + 1, :]
            decay = jnp.exp2(jnp.where(lower, differ, -jnp.inf))
            scores = (raw * decay).astype(bf16)
            one = jnp.ones_like(values)
            augmented = jnp.where(low, one, values) if i else jnp.where(low, values, one)
            intra_ref[:, 128 * h : 128 * h + 128] = dot(scores, augmented)


def tokens_body(
    start_refs,
    x_ref,
    c_ref,
    phiq_ref,
    intra_ref,
    row_ref,
    col_ref,
    u_ref,
    mix_ref,
    up_ref,
    down_ref,
    vec_ref,
    upb_ref,
    ones_ref,
    select_ref,
    *refs,
    chunks,
    size,
):
    (
    out_ref,
    dr_ref,
    dn_ref,
    qside_ref,
    states_ref,
    vloc_ref,
    sent_ref,
    packed_ref,
    vec_acc,
    state,
    heads_low,
    numer_all,
    inner_all,
    up_acc,
    down_acc,
    mix_acc,
    ) = refs
    b = pl.program_id(0)
    heads = state.shape[0]
    pairs = heads // 2

    @pl.when(b == 0)
    def _():
        mix_acc[...] = jnp.zeros_like(mix_acc)
        vec_acc[...] = jnp.zeros_like(vec_acc)
        up_acc[...] = jnp.zeros_like(up_acc)
        down_acc[...] = jnp.zeros_like(down_acc)

    low = low_lanes(CH)
    arrived = sum(start_ref[0].astype(f32) for start_ref in start_refs[size:])
    here = heads // size
    for d in range(size):
        part = slice(here * d, here * d + here)
        state[part] = start_refs[d][0].astype(f32) + arrived[part]
    for c in range(chunks):
        rows = slice(CH * c, CH * c + CH)
        for pair in range(pairs):
            both = []
            for i in range(2):
                h = 2 * pair + i
                block = state[h].astype(bf16)
                states_ref[0, c, h] = block
                carry = dot_nt(phiq_ref[rows, FW * h : FW * h + FW], expand(block, i))
                carried = col_ref[rows, 4 * GR + h : 4 * GR + h + 1]
                both.append(intra_ref[rows, 128 * h : 128 * h + 128] + carried * carry)
                last = jnp.exp2(row_ref[c, h : h + 1, CH - 1 : CH])
                state[h] = last * state[h] + u_ref[0, c, h]
            lanes = slice(128 * pair, 128 * pair + 128)
            numer = jnp.where(low, both[0], both[1])
            inner = pltpu.roll(jnp.where(low, both[1], both[0]), HD, 1)
            numer_all[rows, lanes] = numer
            inner_all[rows, lanes] = inner
            heads_low[rows, lanes] = (numer * lax.rsqrt(inner * inner + 1.0)).astype(bf16)
    for h in range(heads):
        states_ref[0, chunks, h] = state[h].astype(bf16)

    mix = mix_ref[...]
    rest = heads_low[...]
    mixing_bias, gain, shift, down_bias = (vec_ref[i : i + 1, :] for i in range(4))
    residual = x_ref[...].astype(f32) + dot(rest, mix) + mixing_bias
    center = residual - jnp.mean(residual, -1, keepdims=True)
    scale = lax.rsqrt(jnp.mean(center * center, -1, keepdims=True) + 1e-05)
    normal = center * scale
    normal_low = (normal * gain + shift).astype(bf16)
    normal_t = normal_low.T
    upstream = c_ref[...]
    upstream_t = upstream.T
    result = residual + down_bias
    grad_normal = jnp.zeros_like(residual)
    for j in range(up_ref.shape[1] // TILE):
        part = slice(TILE * j, TILE * j + TILE)
        up = up_ref[:, part]
        down = down_ref[part, :]
        hidden = dot(normal_low, up) + upb_ref[:, part]
        square = hidden * hidden
        th = jnp.tanh(hidden * (GELU_A + (GELU_A * GELU_B) * square))
        half = 0.5 + 0.5 * th
        active = (hidden * half).astype(bf16)
        slope = half + hidden * (0.5 - 0.5 * th * th) * (
            GELU_A + (3.0 * GELU_A * GELU_B) * square
        )
        result += dot(active, down)
        grad_hidden = slope * dot_nt(upstream, down)
        grad_hidden = grad_hidden.astype(bf16)
        vec_acc[4 + j : 5 + j, :] += jnp.sum(grad_hidden.astype(f32), 0, keepdims=True)
        grad_normal += dot_nt(grad_hidden, up)
        up_acc[:, part] += dot(normal_t, grad_hidden)
        down_acc[:, part] += dot(upstream_t, active)
    out_ref[...] = result.astype(bf16)
    upstream = upstream.astype(f32)
    dn = grad_normal * gain
    grad_residual = upstream + scale * (
        dn
        - jnp.mean(dn, -1, keepdims=True)
        - normal * jnp.mean(dn * normal, -1, keepdims=True)
    )
    dr_ref[...] = grad_residual
    for i, value in enumerate((grad_residual, grad_normal * normal, grad_normal, upstream)):
        vec_acc[i : i + 1, :] += jnp.sum(value, 0, keepdims=True)
    grad_low = grad_residual.astype(bf16)
    mix_acc[...] += dot_tn(rest, grad_low)
    grad_heads = dot_nt(grad_low, mix)

    ones2 = ones_ref[...]
    following = [None] * heads
    for c in reversed(range(chunks)):
        rows = slice(CH * c, CH * c + CH)
        query_sides = []
        for pair in range(pairs):
            lanes = slice(128 * pair, 128 * pair + 128)
            numer, inner, grad = numer_all[rows, lanes], inner_all[rows, lanes], grad_heads[rows, lanes]
            square = 1.0 / (inner * inner + 1.0)
            grad_numer = grad * lax.rsqrt(inner * inner + 1.0)
            query_side = dot(split2_cat(grad_numer * numer), ones2) * square
            query_sides.append(query_side)
            grad_inner = pltpu.roll(query_side * inner * (-1.0 / HD), HD, 1)
            for i in range(2):
                h = 2 * pair + i
                if i:
                    together = jnp.where(low, grad_inner, grad_numer)
                else:
                    together = jnp.where(low, grad_numer, grad_inner)
                dn_ref[rows, 128 * h : 128 * h + 128] = together.astype(bf16)
                carried = col_ref[rows, 4 * GR + h : 4 * GR + h + 1]
                sent = (carried * together).T.astype(bf16)
                own = shrink(dot(sent, phiq_ref[rows, FW * h : FW * h + FW]), i)
                vloc_ref[0, c, h] = own
                if following[h] is not None:
                    last = jnp.exp2(row_ref[c, h : h + 1, CH - 1 : CH])
                    own = own + last * following[h]
                following[h] = own
        qside_ref[rows, :] = dot(
            split2_cat(jnp.concatenate(query_sides, 1)), select_ref[...]
        )
    for h in range(heads):
        sent_ref[0, h] = following[h].astype(bf16)

    @pl.when(b == pl.num_programs(0) - 1)
    def _():
        width, ff = up_acc.shape
        up_rows, down_rows, mix_rows = width // size, ff // size, mix_acc.shape[0] // size
        for d in range(size):
            at = d * (packed_ref.shape[0] // size)
            for j in range(ff // TILE):
                packed_ref[at : at + up_rows, :] = up_acc[
                    up_rows * d : up_rows * d + up_rows, TILE * j : TILE * j + TILE
                ].astype(bf16)
                at += up_rows
            packed_ref[at : at + down_rows, :] = (
                down_acc[:, down_rows * d : down_rows * d + down_rows].T.astype(bf16)
            )
            at += down_rows
            packed_ref[at : at + mix_rows, :] = mix_acc[
                mix_rows * d : mix_rows * d + mix_rows, :
            ].astype(bf16)


def query_back_body(
    x_ref,
    wq_ref,
    maps_back_ref,
    ones_ref,
    phiq_ref,
    phik_ref,
    v_ref,
    dn_ref,
    row_ref,
    col_ref,
    states_ref,
    *refs,
):
    dq_ref, dphik_ref, dv_ref, wqg_ref, *ticks = refs[-7:]
    clear(ticks)
    first = jnp.logical_and(pl.program_id(0) == 0, pl.program_id(1) == 0)

    @pl.when(first)
    def _():
        wqg_ref[...] = jnp.zeros_like(wqg_ref)

    x = x_ref[...]
    query = dot(x, wq_ref[...])
    width = query.shape[1]
    ones2 = ones_ref[...]
    mask = lower_mask(True)
    low = low_lanes(CH)
    for pair in range(width // 128):
        lanes = slice(128 * pair, 128 * pair + 128)
        n, inverse = unit(query[:, lanes], ones2)
        values = v_ref[:, lanes]
        angles = []
        for i in range(2):
            h = 2 * pair + i
            wide = slice(FW * h, FW * h + FW)
            phiq, phik = phiq_ref[:, wide], phik_ref[:, wide]
            grad = dn_ref[:, 128 * h : 128 * h + 128]
            differ = row_ref[h : h + 1, :] - col_ref[:, GR + h : GR + h + 1]
            decay = jnp.exp2(jnp.where(mask, differ, -jnp.inf))
            one = jnp.ones_like(values)
            augmented = jnp.where(low, one, values) if i else jnp.where(low, values, one)
            scores = (dot_nt(phik, phiq) * decay).astype(bf16)
            grad_raw = (dot_nt(augmented, grad) * decay).astype(bf16)
            dv_ref[:, 128 * h : 128 * h + 128] = dot(scores, grad).astype(bf16)
            dphik_ref[:, wide] = dot(grad_raw, phiq).astype(bf16)
            carried = col_ref[:, 4 * GR + h : 4 * GR + h + 1]
            dphi = dot_tn(grad_raw, phik) + carried * dot(grad, expand(states_ref[0, 0, h], i))
            dphi = dphi.astype(bf16).astype(f32)
            phiq = phiq.astype(f32)
            angles.append(dphi[:, :NF] * phiq[:, NF:] - dphi[:, NF:] * phiq[:, :NF])
        dq = feature_back(n, inverse, jnp.concatenate(angles, 1), maps_back_ref[pair], ones2)
        dq_ref[:, lanes] = dq.astype(bf16)
    wqg_ref[...] += dot_tn(x, dq_ref[...])


def key_back_body(
    end_refs,
    x_ref,
    wq_ref,
    wkv_ref,
    maps_back_ref,
    gw_ref,
    ones_ref,
    all_ref,
    tri_ref,
    phik_ref,
    v_ref,
    dq_ref,
    dphik_ref,
    dv_ref,
    qside_ref,
    row_ref,
    col_ref,
    states_ref,
    vloc_ref,
    dr_ref,
    factor_ref,
    *refs,
):
    dx_ref, wkvg_ref, gwg_ref, gbg_ref, *ticks, grads, state_grad, sides = refs[-10:]
    clear(ticks)
    first = jnp.logical_and(pl.program_id(0) == 0, pl.program_id(1) == 0)

    @pl.when(first)
    def _():
        wkvg_ref[...] = jnp.zeros_like(wkvg_ref)
        gwg_ref[...] = jnp.zeros_like(gwg_ref)
        gbg_ref[...] = jnp.zeros_like(gbg_ref)

    @pl.when(pl.program_id(1) == 0)
    def _():
        state_grad[...] = sum(end_ref[0].astype(f32) for end_ref in end_refs)

    x = x_ref[...]
    heads = state_grad.shape[0]
    keys = dot(x, wkv_ref[:, : wq_ref.shape[1]])
    width = wq_ref.shape[1]
    ones2 = ones_ref[...]
    low = low_lanes(CH)
    weigh = jnp.where(lax.broadcasted_iota(jnp.int32, (SR, FW), 0) < HD, 1.0, 4.0)
    bounds = []
    for pair in range(heads // 2):
        lanes = slice(128 * pair, 128 * pair + 128)
        n, inverse = unit(keys[:, lanes], ones2)
        values = v_ref[:, lanes]
        angles = []
        both = []
        for i in range(2):
            h = 2 * pair + i
            wide = slice(FW * h, FW * h + FW)
            phik = phik_ref[:, wide]
            one = jnp.ones_like(values)
            augmented = jnp.where(low, one, values) if i else jnp.where(low, values, one)
            tail = col_ref[:, 2 * GR + h : 2 * GR + h + 1]
            grad_end = state_grad[h]
            bounds.append(
                jnp.sum(grad_end * weigh * states_ref[0, 0, h].astype(f32), 0, keepdims=True)
            )
            spread = expand(grad_end.astype(bf16), i)
            dv = dv_ref[:, 128 * h : 128 * h + 128] + tail * dot_nt(phik, spread)
            sides[:, 128 * h : 128 * h + 128] = dv * augmented.astype(f32)
            both.append(dv)
            dphi = dphik_ref[:, wide].astype(f32) + tail * dot(augmented, spread)
            dphi = dphi.astype(bf16).astype(f32)
            phik = phik.astype(f32)
            angles.append(dphi[:, :NF] * phik[:, NF:] - dphi[:, NF:] * phik[:, :NF])
            last = jnp.exp2(row_ref[h : h + 1, CH - 1 : CH])
            state_grad[h] = last * grad_end + vloc_ref[0, 0, h]
        dk = feature_back(n, inverse, jnp.concatenate(angles, 1), maps_back_ref[pair], ones2)
        grads[:, lanes] = dk.astype(bf16)
        grads[:, width + 128 * pair : width + 128 * pair + 128] = jnp.where(
            low, both[0], both[1]
        ).astype(bf16)
    key_side = dot(split2_cat(sides[...]), all_ref[...])
    key_row = key_side.T[:GR]
    differ = qside_ref[...].T[:GR] - key_row
    bound = jnp.sum(jnp.concatenate(bounds, 0), 1, keepdims=True)
    bound = jnp.concatenate([bound, jnp.zeros((GR - heads, 1), f32)], 0)
    grad_log = dot(split3_cat(differ), tri_ref[...]) + bound
    gate, keep = row_ref[2 * GR : 3 * GR, :], row_ref[3 * GR : 4 * GR, :]
    grad_pre = (
        grad_log * keep - gate * key_row + factor_ref[...] * gate * keep
    ).astype(bf16)
    gbg_ref[...] += grad_pre.astype(f32)
    gwg_ref[...] += dot(grad_pre, x)
    together = grads[...]
    wkvg_ref[...] += dot_tn(x, together)
    dx_ref[...] = (
        dr_ref[...]
        + dot_nt(dq_ref[...], wq_ref[...])
        + dot_nt(together, wkv_ref[...])
        + dot_tn(grad_pre, gw_ref[...])
    )


def unpack_body(index_ref, every_ref, _, up_ref, down_ref, mix_ref, tick_ref, *, places):
    rows, ff = up_ref.shape
    width = down_ref.shape[1]
    depth = every_ref.shape[1]
    slab = depth * every_ref.shape[0] // pl.num_programs(0)
    tick_ref[...] = jnp.zeros_like(tick_ref)

    def copy(first, count, ref, lanes):
        done = 0
        while done < count:
            piece, at = divmod(first + done, depth)
            number = min(count - done, depth - at)
            ref[done : done + number, lanes] = every_ref[
                places[piece], at : at + number, :
            ].astype(f32)
            done += number

    for d in range(pl.num_programs(0)):

        @pl.when(pl.program_id(0) == d)
        def _(d=d):
            first = slab * d
            for j in range(ff // TILE):
                copy(first, rows, up_ref, slice(TILE * j, TILE * j + TILE))
                first += rows
            copy(first, down_ref.shape[0], down_ref, slice(0, width))
            first += down_ref.shape[0]

            @pl.when(index_ref[0] == d)
            def _():
                copy(first, mix_ref.shape[0], mix_ref, slice(0, width))


def pack_body(key_ref, value_ref, query_ref, mix_ref, maps_ref, tail_ref, first_ref, second_ref):
    width, own = key_ref.shape
    if own == 128:
        first_ref[:width] = key_ref[...]
        first_ref[width : 2 * width] = value_ref[...]
        second_ref[:width] = query_ref[...]
        at, then = 2 * width, width
    else:
        half = width // 2
        first_ref[:width] = jnp.concatenate([key_ref[...], value_ref[...]], 1)
        second_ref[:half] = jnp.concatenate([query_ref[:half], query_ref[half:]], 1)
        at, then = width, half
    high, rest = split2(maps_ref[...] * (0.5 / math.pi))
    first_ref[at : at + own] = high
    first_ref[at + own : at + 2 * own] = rest
    first_ref[at + 2 * own :] = tail_ref[...]
    for j in range(width // 128):
        second_ref[then + own * j : then + own * j + own] = mix_ref[:, 128 * j : 128 * j + 128]


def group_body(*refs, queries, keys, order):
    query_refs, refs = refs[:queries], refs[queries:]
    key_refs, refs = refs[:keys], refs[keys:]
    gate_refs, refs = refs[:keys], refs[keys:]
    bias_refs, (vector_ref, out_ref) = refs[:keys], refs[keys:]
    width = query_refs[0].shape[0]
    own = out_ref.shape[2]
    inner = query_refs[0].shape[1]
    here = own // HD
    cuts = width // own

    def total(parts, lanes):
        value = parts[0][:, lanes]
        for part in parts[1:]:
            value = value + part[:, lanes]
        return value

    every = slice(None)
    gates = total(gate_refs, every)
    biases = jnp.sum(total(bias_refs, every), 1, keepdims=True)
    vectors = vector_ref[...]
    vectors = jnp.concatenate(
        [vectors[r : r + 1, own * j : own * j + own] for r in range(8) for j in range(cuts)], 0
    )
    at = 3 * width + GR
    used = at + 8 * cuts
    lane = lax.broadcasted_iota(jnp.int32, (1, own), 1)
    for d, place in enumerate(order):
        lanes = slice(own * d, own * d + own)
        out_ref[place, :width] = total(query_refs, lanes).astype(bf16)
        out_ref[place, width : 2 * width] = total(key_refs, lanes).astype(bf16)
        lanes = slice(inner + own * d, inner + own * d + own)
        out_ref[place, 2 * width : 3 * width] = total(key_refs, lanes).astype(bf16)
        rows = [
            gates[h : h + 1, own * j : own * j + own]
            for h in range(here * d, here * d + here)
            for j in range(cuts)
        ]
        bias = jnp.zeros((1, own), f32)
        for i in range(here):
            bias = jnp.where(lane == i, biases[here * d + i : here * d + i + 1], bias)
        rows += [bias, jnp.zeros((GR - 1 - here * cuts, own), f32)]
        out_ref[place, 3 * width : at] = jnp.concatenate(rows, 0).astype(bf16)
        out_ref[place, at:used] = vectors.astype(bf16)
        if used < out_ref.shape[1]:
            out_ref[place, used:] = jnp.zeros((out_ref.shape[1] - used, own), bf16)


def tokens_entry(*refs, starts, **named):
    tokens_body(refs[:starts], *refs[starts:], **named)


def key_back_entry(*refs, arrivals):
    key_back_body(refs[:arrivals], *refs[arrivals:])


def whole(array):
    zeros = (0,) * len(array.shape)
    return pl.BlockSpec(array.shape, lambda *_: zeros, pipeline_mode=pl.Buffered(1))


def fixed(shape):
    zeros = (0,) * len(shape)
    return pl.BlockSpec(shape, lambda *_: zeros)


def call(body, grid, ins, outs, previous=(), after=(), scratch=(), name=None, flops=0, room=48):
    extra = list(previous) + list(after)
    specs = [spec for _, spec in ins] + [pl.BlockSpec(memory_space=pl.ANY)] * len(extra)
    return pl.pallas_call(
        body,
        grid=grid,
        in_specs=specs,
        out_specs=[spec for _, _, spec in outs],
        out_shape=[jax.ShapeDtypeStruct(shape, kind) for shape, kind, _ in outs],
        scratch_shapes=list(scratch),
        input_output_aliases={len(ins) + i: i for i in range(len(previous))},
        compiler_params=pltpu.CompilerParams(
            dimension_semantics=("arbitrary",) * len(grid), vmem_limit_bytes=room * 1024 * 1024
        ),
        cost_estimate=pl.CostEstimate(flops=flops, bytes_accessed=4 << 20, transcendentals=0),
        name=name,
    )(*[array for array, _ in ins], *extra)


def swap(x, axis, bit):
    size = lax.axis_size(axis)
    return lax.ppermute(x, axis, [(i, i ^ bit) for i in range(size)])


def spread_head(part):
    parts = [part]
    for k in range(1, lax.axis_size("head")):
        parts.append(swap(parts[k - 1], "head", 1) if k % 2 else swap(part, "head", k))
    return parts


def place_in(axis, bit, number):
    return (lax.axis_index(axis) // bit) % number


class HalvingSum:
    def __init__(self, array):
        self.terms = [(array, 0)]
        self.length = array.shape[0]

    def part(self, offset, tick=0.0):
        total = tick
        for array, start in self.terms:
            piece = lax.dynamic_slice_in_dim(array, start + offset, self.length, 0)
            total = total + piece.astype(f32)
        return total.astype(bf16)

    def step(self, axis, bit, number=2, tick=0.0):
        self.length //= number
        mine = place_in(axis, bit, number)
        sends = [self.part((mine ^ k) * self.length, tick) for k in range(1, number)]
        self.terms = [(array, start + mine * self.length) for array, start in self.terms]
        for k, send in enumerate(sends):
            self.terms.append((swap(send, axis, (k + 1) * bit), 0))
        return sends


def open_join(array, axis, bit, number):
    return [array] + [swap(array, axis, k * bit) for k in range(1, number)]


def close_join(parts, axis, bit):
    number = len(parts)
    mine = place_in(axis, bit, number).astype(jnp.int32)
    if number == 2:
        own, other = parts
        return jnp.where(
            mine == 0, jnp.concatenate([own, other], 0), jnp.concatenate([other, own], 0)
        )
    return jnp.concatenate(
        [
            lax.select_n(mine, *[parts[j ^ place] for place in range(number)])
            if number <= 4
            else jnp.take(jnp.stack(parts), mine ^ j, axis=0)
            for j in range(number)
        ],
        0,
    )


def gather_all(piece, stages):
    every = lax.all_gather(piece, ("dp", "head"), axis=0, tiled=False)
    names = [
        (axis, 1 << i)
        for axis in ("dp", "head")
        for i in reversed(range(lax.axis_size(axis).bit_length() - 1))
    ]
    places = np.arange(1 << len(names)).reshape((2,) * len(names))
    singles = []
    for axis, bit, number in stages:
        while number > 1:
            number //= 2
            singles.append((axis, bit * number))
    places = places.transpose([names.index(single) for single in singles]).reshape(-1)
    if piece.shape[0] % GR:
        every = every[places].reshape(1, -1, piece.shape[1])
        places = places[:1] * 0
    return every, tuple(int(place) for place in places)


def high_rest(x):
    high = lax.reduce_precision(x, 8, 7)
    return high, x - high


def per_device(
    tokens,
    cotangent,
    carry_state,
    carry_norm,
    random_maps,
    query_weight,
    key_weight,
    value_weight,
    gate_weight,
    gate_bias,
    mixing_weight,
    mixing_bias,
    norm_gain,
    norm_bias,
    up_weight,
    up_bias,
    down_weight,
    down_bias,
):
    seqs, length, width = tokens.shape
    here = gate_weight.shape[1]
    size = lax.axis_size("head")
    replicas = lax.axis_size("dp")
    index = lax.axis_index("head")
    heads = here * size
    chunks = length // CH
    blocks = seqs * chunks
    count = seqs * length
    inner_width = heads * HD
    own = here * HD
    ff = up_weight.shape[1]
    pairs = heads // 2
    head_bits = [1 << i for i in range(size.bit_length() - 1)]
    stages = (
        [("head", 1, 2), ("dp", 1, min(2, replicas))]
        + [("head", bit, 2) for bit in head_bits[1:]]
        + [("dp", 2, replicas // 2)]
    )
    index_array = index.astype(jnp.int32).reshape(1)
    smem = pl.BlockSpec(memory_space=pltpu.SMEM)

    bias_high, bias_rest = high_rest(gate_bias)
    bias_mid, bias_rest = high_rest(bias_rest)
    biases = jnp.pad(jnp.stack([bias_high, bias_mid, bias_rest]), ((0, 0), (0, 128 - here)))
    tail = jnp.concatenate([gate_weight.T.reshape(-1, 128).astype(f32), biases])
    tail = jnp.pad(tail, ((0, GR - tail.shape[0]), (0, 0)))
    tail = tail.astype(bf16)
    packing = (key_weight, value_weight, query_weight, mixing_weight, random_maps.reshape(own, NF), tail)
    first_rows = (width * here + 2 * own + GR, 128)
    second_rows = (width * here, 128)
    first_part, second_part = call(
        pack_body,
        (1,),
        [(array, fixed(array.shape)) for array in packing],
        [(first_rows, bf16, fixed(first_rows)), (second_rows, bf16, fixed(second_rows))],
        name="pack",
        room=62,
        flops=1_000_000,
    )
    first_parts = spread_head(first_part)

    begin = jnp.concatenate(
        [
            carry_state.transpose(0, 1, 3, 2),
            jnp.broadcast_to(carry_norm[:, :, None, :], (seqs, here, SR - HD, FW)),
        ],
        2,
    ).astype(bf16)

    half = np.arange(128) // HD
    ones2 = np.tile((half[:, None] == half[None, :]).astype(np.float32), (2, 1))
    ones2 = jnp.asarray(ones2, bf16)
    place = np.arange(CH)
    upto = jnp.asarray(np.tile((place[:, None] <= place[None, :]).astype(np.float32), (3, 1)), bf16)
    onward = jnp.asarray(np.tile((place[:, None] >= place[None, :]).astype(np.float32), (3, 1)), bf16)
    lane = np.arange(128)
    one_lane = np.zeros((inner_width, 128), np.float32)
    one_lane[np.arange(heads) * HD, np.arange(heads)] = 1.0
    select = jnp.asarray(np.tile(one_lane, (2, 1)), bf16)
    all_lanes = (np.arange(heads * 128) // 128)[:, None] == lane[None, :]
    all_lanes = jnp.asarray(np.tile(all_lanes.astype(np.float32), (2, 1)), bf16)

    x = tokens.reshape(count, width)
    c = cotangent.reshape(count, width)
    state_shape = (heads, SR, FW)
    tick_outs = [((1, lanes), f32, fixed((1, lanes))) for lanes in (128, FW, width)]

    def rows_of(columns, base=0, reverse=False):
        def at(b, t):
            return ((base + b) * chunks + (chunks - 1 - t if reverse else t), 0)

        return pl.BlockSpec((CH, columns), at)

    def row_spec(base=0, reverse=False):
        return pl.BlockSpec((4 * GR, CH), rows_of(0, base, reverse).index_map)

    def per_block(shape, base=0, offset=0, reverse=False):
        zeros = (0,) * len(shape)

        def at(b, t):
            return (base + b, offset + (chunks - 1 - t if reverse else t)) + zeros

        return pl.BlockSpec((1, 1) + shape, at)

    def per_seq(base=0):
        return pl.BlockSpec((1,) + state_shape, lambda b, t: (base + b, 0, 0, 0))

    weights = [
        ((width, 2 * inner_width), bf16),
        ((pairs, 3 * 128, FW), bf16),
        ((pairs, 3 * FW, 128), bf16),
        ((GR, width), bf16),
        ((inner_width, width), bf16),
        ((GR, CH), f32),
    ]
    weights = [(shape, kind, fixed(shape)) for shape, kind in weights]

    def keys_ins(base):
        return [(x, rows_of(width, base)), (ones2, whole(ones2)), (upto, whole(upto))]

    def keys_outs(base):
        total_spec = pl.BlockSpec((1, GR, 128), lambda b, t: (base + b, 0, 0))
        return [
            ((count, heads * FW), bf16, rows_of(heads * FW, base)),
            ((count, inner_width), bf16, rows_of(inner_width, base)),
            ((blocks * 4 * GR, CH), f32, row_spec(base)),
            ((count, 128), f32, rows_of(128, base)),
            ((seqs, chunks) + state_shape, f32, per_block(state_shape, base)),
            ((seqs,) + state_shape, bf16, per_seq(base)),
            ((seqs, GR, 128), f32, total_spec),
            ((GR, CH), f32, fixed((GR, CH))),
            ((1, FW), f32, fixed((1, FW))),
        ]

    *previous, gate_sums, tick, wkv, maps_front, maps_back, gw, wvt, gb = call(
        functools.partial(keys_body, size=size, here=here, skipped=2),
        (2, chunks),
        [(part, whole(part)) for part in first_parts] + [(index_array, smem)] + keys_ins(0),
        keys_outs(0) + weights,
        after=[second_part, begin],
        scratch=[
            pltpu.VMEM(state_shape, f32),
            pltpu.VMEM((size,) + first_part.shape, bf16),
        ],
        name="keys",
        flops=10_000_000_000,
    )
    second_parts = [second_part] + [swap(second_part, "head", k) for k in range(1, size)]
    begins = [jnp.where(index == 0, begin, jnp.zeros_like(begin))] + [
        lax.ppermute(begin, "head", [(k, 0)]) for k in range(1, size)
    ]
    phik, v, row, col, update, end, total, more_sums, tick = call(
        functools.partial(keys_body, size=0, here=here, skipped=2 * size - 2 + len(previous)),
        (seqs - 2, chunks),
        [(part, whole(part)) for part in (wkv, maps_front, gw, wvt, gb)] + keys_ins(2),
        keys_outs(2),
        previous=previous,
        after=second_parts[1:] + begins[1:],
        scratch=[pltpu.VMEM(state_shape, f32)],
        name="keys",
        flops=10_000_000_000,
    )
    gate_sums = lax.all_gather(
        jnp.concatenate([gate_sums, more_sums]), ("dp", "head"), axis=0, tiled=True
    )
    last = jnp.exp2(total[:, :heads, 0])[:, :, None, None]
    begin = jnp.concatenate(begins, 1)

    sent = (end.astype(f32) + last * begin.astype(f32)).astype(bf16)
    starts = []
    ticks = (0.0, 0.0, 0.0)
    phiq = intra = wq = mix = None
    previous = ()
    for step, (base, number) in enumerate(((0, 1), (1, 2), (3, 1))):
        arrived = None
        if step < size - 1:
            arrived = lax.ppermute(sent, "head", [(step, step + 1)])
            starts.append(arrived)
        main = [
            (x, rows_of(width, base)),
            (maps_front, whole(maps_front)),
            (ones2, whole(ones2)),
            (phik, rows_of(heads * FW, base)),
            (v, rows_of(inner_width, base)),
            (row, row_spec(base)),
            (col, rows_of(128, base)),
        ]
        outs = [
            ((count, heads * FW), bf16, rows_of(heads * FW, base)),
            ((count, heads * 128), f32, rows_of(heads * 128, base)),
        ] + tick_outs
        if step == 0:
            phiq, intra, *ticks, wq, mix = call(
                functools.partial(queries_body, size=size, here=here, skipped=1),
                (number, chunks),
                [(part, whole(part)) for part in second_parts] + [(index_array, smem)] + main,
                outs
                + [
                    ((width, inner_width), bf16, fixed((width, inner_width))),
                    ((inner_width, width), bf16, fixed((inner_width, width))),
                ],
                after=[sent],
                scratch=[pltpu.VMEM((size,) + second_part.shape, bf16)],
                name="queries",
                flops=5_000_000_000,
            )
        else:
            phiq, intra, *ticks = call(
                functools.partial(queries_body, size=0, here=here, skipped=3),
                (number, chunks),
                [(wq, whole(wq))] + main,
                outs,
                previous=[phiq, intra],
                after=[sent],
                name="queries",
                flops=5_000_000_000 * number,
            )
        if step < size - 2:
            sent = (last * arrived.astype(f32) + end.astype(f32) + ticks[1][0]).astype(bf16)
    for step in range(3, size - 1):
        arrived = lax.ppermute(sent, "head", [(step, step + 1)])
        starts.append(arrived)
        sent = (last * arrived.astype(f32) + end.astype(f32)).astype(bf16)

    vectors = jnp.stack([mixing_bias, norm_gain, norm_bias, down_bias] * 2)

    def seq_rows(columns):
        return pl.BlockSpec((length, columns), lambda b: (b, 0))

    def seq_block(*shape):
        zeros = (0,) * len(shape)
        return pl.BlockSpec((1,) + shape, lambda b: (b,) + zeros)

    up_bias2 = up_bias.reshape(1, ff)
    slab = (width // size) * (ff // TILE) + ff // size + own
    layer_out, dr, dn, qside, states, vloc, vdev, packed, vector_grads = call(
        functools.partial(
            tokens_entry, starts=len(begins) + len(starts), chunks=chunks, size=size
        ),
        (seqs,),
        [(start, seq_block(*start.shape[1:])) for start in begins + starts]
        + [
            (x, seq_rows(width)),
            (c, seq_rows(width)),
            (phiq, seq_rows(heads * FW)),
            (intra, seq_rows(heads * 128)),
            (
                row.reshape(blocks, 4 * GR, CH),
                pl.BlockSpec((chunks, 4 * GR, CH), lambda b: (b, 0, 0)),
            ),
            (col, seq_rows(128)),
            (update, seq_block(chunks, *state_shape)),
            (mix, whole(mix)),
            (up_weight, whole(up_weight)),
            (down_weight, whole(down_weight)),
            (vectors, whole(vectors)),
            (up_bias2, whole(up_bias2)),
            (ones2, whole(ones2)),
            (select, whole(select)),
        ],
        [
            ((count, width), bf16, seq_rows(width)),
            ((count, width), f32, seq_rows(width)),
            ((count, heads * 128), bf16, seq_rows(heads * 128)),
            ((count, 128), f32, seq_rows(128)),
            ((seqs, chunks + 1) + state_shape, bf16, seq_block(chunks + 1, *state_shape)),
            ((seqs, chunks) + state_shape, f32, seq_block(chunks, *state_shape)),
            ((seqs,) + state_shape, bf16, seq_block(*state_shape)),
            ((size * slab, width), bf16, fixed((size * slab, width))),
            ((8, width), f32, fixed((8, width))),
        ],
        scratch=[
            pltpu.VMEM(state_shape, f32),
            pltpu.VMEM((length, inner_width), bf16),
            pltpu.VMEM((length, inner_width), f32),
            pltpu.VMEM((length, inner_width), f32),
            pltpu.VMEM((width, ff), f32),
            pltpu.VMEM((width, ff), f32),
            pltpu.VMEM((inner_width, width), f32),
        ],
        name="tokens",
        room=62,
        flops=50_000_000_000,
    )

    sent = vdev
    waiting = list(stages)
    sums = HalvingSum(packed)
    ticks = (0.0, [0.0], 0.0)
    finishes = []
    dq = dphik = dv = None
    previous = []
    query_grads = []
    for step, (base, number) in enumerate(((0, 1), (1, 2), (3, 1))):
        after = sums.step(*waiting.pop(0), ticks[2])
        if step < size - 1:
            arrived = lax.ppermute(sent, "head", [(size - 1 - step, size - 2 - step)])
            finishes.append(arrived)
            after.append(sent)
        dq, dphik, dv, query_grad, *ticks = call(
            query_back_body,
            (number, chunks),
            [
                (x, rows_of(width, base)),
                (wq, whole(wq)),
                (maps_back, whole(maps_back)),
                (ones2, whole(ones2)),
                (phiq, rows_of(heads * FW, base)),
                (phik, rows_of(heads * FW, base)),
                (v, rows_of(inner_width, base)),
                (dn, rows_of(heads * 128, base)),
                (row, row_spec(base)),
                (col, rows_of(128, base)),
                (states, per_block(state_shape, base)),
            ],
            [
                ((count, inner_width), bf16, rows_of(inner_width, base)),
                ((count, heads * FW), bf16, rows_of(heads * FW, base)),
                ((count, heads * 128), bf16, rows_of(heads * 128, base)),
                ((width, inner_width), f32, fixed((width, inner_width))),
            ] + tick_outs,
            previous=previous,
            after=after,
            name="query_back",
            flops=8_000_000_000 * number,
        )
        previous = [dq, dphik, dv]
        query_grads.append(query_grad)
        if step < size - 2:
            sent = (last * arrived.astype(f32) + vdev.astype(f32) + ticks[1][0]).astype(bf16)
    for step in range(3, size - 1):
        arrived = lax.ppermute(sent, "head", [(size - 1 - step, size - 2 - step)])
        finishes.append(arrived)
        sent = (last * arrived.astype(f32) + vdev.astype(f32)).astype(bf16)

    gate_total = jnp.sum(gate_sums.reshape(-1, GR, CH)[:, :heads] + ticks[1][0])
    gate_count = replicas * heads * size * count
    mean_gate = gate_total / gate_count
    factor = 2.0 * penalty_weight * (mean_gate - target_gate) / heads
    factor = jnp.broadcast_to(factor, (1, CH))

    tokens_grad = None
    previous = []
    key_value_grads, gate_grads, gate_bias_grads = [], [], []
    for base, number in ((0, 2), (2, 2)):
        after = []
        if base == 0:
            while waiting:
                after = sums.step(*waiting.pop(0), ticks[2])
        else:
            piece = sums.part(0, ticks[2])
            after = [piece]
            every, places = gather_all(piece, stages)
        tokens_grad, key_value_grad, gate_grad, gate_bias_grad, *ticks = call(
            functools.partial(key_back_entry, arrivals=len(finishes)),
            (number, chunks),
            [(finish, per_seq(base)) for finish in finishes]
            + [
                (x, rows_of(width, base, True)),
                (wq, whole(wq)),
                (wkv, whole(wkv)),
                (maps_back, whole(maps_back)),
                (gw, whole(gw)),
                (ones2, whole(ones2)),
                (all_lanes, whole(all_lanes)),
                (onward, whole(onward)),
                (phik, rows_of(heads * FW, base, True)),
                (v, rows_of(inner_width, base, True)),
                (dq, rows_of(inner_width, base, True)),
                (dphik, rows_of(heads * FW, base, True)),
                (dv, rows_of(heads * 128, base, True)),
                (qside, rows_of(128, base, True)),
                (row, row_spec(base, True)),
                (col, rows_of(128, base, True)),
                (states, per_block(state_shape, base, 1, True)),
                (vloc, per_block(state_shape, base, 0, True)),
                (dr, rows_of(width, base, True)),
                (factor, whole(factor)),
            ],
            [
                ((count, width), f32, rows_of(width, base, True)),
                ((width, 2 * inner_width), f32, fixed((width, 2 * inner_width))),
                ((GR, width), f32, fixed((GR, width))),
                ((GR, CH), f32, fixed((GR, CH))),
            ] + tick_outs,
            previous=previous,
            after=after,
            scratch=[
                pltpu.VMEM((CH, 2 * inner_width), bf16),
                pltpu.VMEM(state_shape, f32),
                pltpu.VMEM((CH, heads * 128), f32),
            ],
            name="key_back",
            room=58,
            flops=8_000_000_000 * number,
        )
        previous = [tokens_grad]
        key_value_grads.append(key_value_grad)
        gate_grads.append(gate_grad)
        gate_bias_grads.append(gate_bias_grad)
    rows = 3 * width + GR + 8 * width // own
    rows += -rows % replicas
    order = [
        sum(((d >> i) & 1) << (len(head_bits) - 1 - i) for i in range(len(head_bits)))
        for d in range(size)
    ]
    parts = query_grads + key_value_grads + gate_grads + gate_bias_grads + [vector_grads]
    (group,) = call(
        functools.partial(
            group_body, queries=len(query_grads), keys=len(key_value_grads), order=order
        ),
        (1,),
        [(part, fixed(part.shape)) for part in parts],
        [((size, rows, own), bf16, fixed((size, rows, own)))],
        name="group",
        room=62,
        flops=1_000_000,
    )
    group_sums = HalvingSum(group.reshape(-1, own))
    for bit in head_bits:
        group_sums.step("head", bit)
    across = [stage for stage in stages if stage[0] == "dp"]
    for stage in across:
        group_sums.step(*stage)
    group = group_sums.part(0)
    for axis, bit, number in reversed(across[1:]):
        group = close_join(open_join(group, axis, bit, number), axis, bit)
    group, other = open_join(group, *across[0])
    up_grad, down_grad, mixing_grad, tick = call(
        functools.partial(unpack_body, places=places),
        (size,),
        [(index_array, smem), (every, whole(every))],
        [
            ((width, ff), f32, pl.BlockSpec((width // size, ff), lambda d: (d, 0))),
            ((ff, width), f32, pl.BlockSpec((ff // size, width), lambda d: (d, 0))),
            ((own, width), f32, fixed((own, width))),
            ((1, own), f32, fixed((1, own))),
        ],
        after=[group],
        name="unpack",
        flops=1_000_000_000,
    )
    group = close_join([group + tick.astype(bf16), other], *across[0][:2])
    group = group.astype(f32)
    gate_rows = here * width // own
    gate_grad = group[3 * width : 3 * width + gate_rows].reshape(here, width).T
    at = 3 * width + GR
    vector_grads = group[at : at + 8 * width // own].reshape(8, width)
    penalty = penalty_weight * (mean_gate - target_gate) * (mean_gate - target_gate)
    return (
        layer_out.reshape(seqs, length, width),
        tokens_grad.reshape(seqs, length, width),
        penalty,
        group[:width],
        group[width : 2 * width],
        group[2 * width : 3 * width],
        gate_grad,
        group[3 * width + gate_rows, :here],
        mixing_grad,
        vector_grads[0],
        vector_grads[1],
        vector_grads[2],
        up_grad,
        vector_grads[4:].reshape(ff),
        down_grad,
        vector_grads[3],
    )


def solution(mesh):
    placed = (
        P("dp", "head", None),
        P("dp", "head", None),
        P("dp", "head", None, None),
        P("dp", "head", None),
        P("head", None, None),
        P(None, "head"),
        P(None, "head"),
        P(None, "head"),
        P(None, "head"),
        P("head"),
        P("head", None),
        P(),
        P(),
        P(),
        P(),
        P(),
        P(),
        P(),
    )
    return jax.shard_map(
        per_device,
        mesh=mesh,
        in_specs=placed,
        out_specs=(
            P("dp", "head", None),
            P("dp", "head", None),
            P(),
            P(None, "head"),
            P(None, "head"),
            P(None, "head"),
            P(None, "head"),
            P("head"),
            P("head", None),
            P(),
            P(),
            P(),
            P(),
            P(),
            P(),
            P(),
        ),
        check_vma=False,
    )
```

```python
import functools
import math

import jax
import jax.numpy as jnp
import numpy as np
from jax import lax
from jax.experimental import pallas as pl
from jax.experimental.pallas import tpu as pltpu
from jax.sharding import PartitionSpec as P

CH = 256
HD = 64
NF = 128
FW = 2 * NF
SR = 80
GR = 16
TILE = 512

penalty_weight = 32.0
target_gate = 0.9
LOG2E = 1.4426950408889634
SIN_POLY = (
    3.1415925800446116,
    -5.16770687892007,
    2.5500313771889287,
    -0.5980451736320438,
    0.07722012807955428,
)
COS_POLY = (
    0.9999999534665498,
    -4.934792858660313,
    4.058411913867723,
    -1.3318801593312537,
    0.2196967947670672,
)
GELU_A = 0.7978845608028654
GELU_B = 0.044715

f32 = jnp.float32
bf16 = jnp.bfloat16


def dot(a, b):
    return lax.dot_general(a, b, (((1,), (0,)), ((), ())), preferred_element_type=f32)


def dot_nt(a, b):
    return lax.dot_general(a, b, (((1,), (1,)), ((), ())), preferred_element_type=f32)


def dot_tn(a, b):
    return lax.dot_general(a, b, (((0,), (0,)), ((), ())), preferred_element_type=f32)


def split2(x):
    high = x.astype(bf16)
    return high, (x - high.astype(f32)).astype(bf16)


def split2_cat(x):
    return jnp.concatenate(split2(x), 1)


def split3_cat(x):
    high = x.astype(bf16)
    rest = x - high.astype(f32)
    mid = rest.astype(bf16)
    return jnp.concatenate([high, mid, (rest - mid.astype(f32)).astype(bf16)], 1)


def low_lanes(rows):
    return lax.broadcasted_iota(jnp.int32, (rows, 128), 1) < HD


def unit(u, ones2):
    inverse = lax.rsqrt(dot(split2_cat(u * u), ones2) + 1e-06)
    return u * inverse, inverse


def sin_cos(n, maps):
    high, rest = split2(n)
    turns = dot(jnp.concatenate([high, rest, high], 1), maps)
    r = turns - jnp.round(turns)
    u = r * r
    scale = math.sqrt(2.0 / math.sqrt(NF))
    s = SIN_POLY[4] * scale
    c = COS_POLY[4] * scale
    for i in (3, 2, 1, 0):
        s = s * u + SIN_POLY[i] * scale
        c = c * u + COS_POLY[i] * scale
    s = s * r
    return s * c, 1.0 / math.sqrt(NF) - s * s


def pair_features(n, maps):
    sine, cosine = sin_cos(n, maps)
    return [
        jnp.concatenate(
            [sine[:, NF * i : NF * i + NF], cosine[:, NF * i : NF * i + NF]], 1
        ).astype(bf16)
        for i in range(2)
    ]


def feature_back(units, angle_grads, maps_ref, ones2):
    splits = [split2(angle_grad) for angle_grad in angle_grads]
    dns = [
        dot(jnp.concatenate([high, rest, high], 1), maps_ref[pair])
        for pair, (high, rest) in enumerate(splits)
    ]
    radials = [dot(split2_cat(n * dn), ones2) for (n, _), dn in zip(units, dns)]
    return [
        (dn - n * radial) * inverse for (n, inverse), dn, radial in zip(units, dns, radials)
    ]


def angle_gradient(dphi, phi):
    dphi = dphi.astype(bf16).astype(f32)
    phi = phi.astype(f32)
    return dphi[:, :NF] * phi[:, NF:] - dphi[:, NF:] * phi[:, :NF]


def both_augmented(values, low):
    one = jnp.ones_like(values)
    return jnp.where(low, values, one), jnp.where(low, one, values)


def expand(block, odd):
    state, norm = block[:HD], block[HD:SR]
    parts = [norm] * (HD // (SR - HD))
    return jnp.concatenate(parts + [state] if odd else [state] + parts, 0)


def shrink(block, odd):
    if odd:
        return jnp.concatenate([block[HD:], block[HD - (SR - HD) : HD]], 0)
    return block[:SR]


def clear(refs):
    for ref in refs:
        ref[...] = jnp.zeros_like(ref)


def collect(held, parts, index):
    for k, part in enumerate(parts):
        held[index ^ k] = part[...]


def block_pair(even, odd):
    none = jnp.zeros_like(even)
    return jnp.concatenate(
        [jnp.concatenate([even, none], 1), jnp.concatenate([none, odd], 1)], 0
    )


def keys_setup(held, here, wkv_ref, wvt, maps_ref, back_ref, gw_ref, gb):
    size = held.shape[0]
    width = wkv_ref.shape[0]
    inner = wvt.shape[0]
    at = width * here
    high, rest, gates, biases = [], [], [], []
    for d in range(size):
        if here == 2:
            lanes = slice(128 * d, 128 * d + 128)
            wkv_ref[:, lanes] = held[d, :width]
            wkv_ref[:, inner + 128 * d : inner + 128 * d + 128] = held[d, width : 2 * width]
            wvt[lanes, :] = held[d, width : 2 * width].T
        elif d % 2:
            lanes = slice(64 * d - 64, 64 * d + 64)
            one, two = held[d - 1, :width], held[d, :width]
            wkv_ref[:, lanes] = jnp.concatenate([one[:, :HD], two[:, :HD]], 1)
            values = jnp.concatenate([one[:, HD:], two[:, HD:]], 1)
            wkv_ref[:, inner + 64 * d - 64 : inner + 64 * d + 64] = values
            wvt[lanes, :] = values.T
        for i in range(here):
            first = at + HD * i
            high.append(held[d, first : first + HD])
            rest.append(held[d, first + HD * here : first + HD * here + HD])
        tail = held[d, at + 2 * HD * here :].astype(f32)
        for i in range(here):
            gates.append(
                jnp.concatenate([tail[4 * i + j : 4 * i + j + 1] for j in range(width // 128)], 1)
            )
            bias = sum(tail[4 * here + j : 4 * here + j + 1, i : i + 1] for j in range(3))
            biases.append(jnp.broadcast_to(bias, (1, CH)))
    for pair in range(len(high) // 2):
        top = block_pair(high[2 * pair], high[2 * pair + 1])
        low = block_pair(rest[2 * pair], rest[2 * pair + 1])
        maps_ref[pair] = jnp.concatenate([top, top, low], 0)
        back = ((top.astype(f32) + low.astype(f32)) * (2.0 * math.pi)).T
        top, low = split2(back)
        back_ref[pair] = jnp.concatenate([top, top, low], 0)
    heads = len(gates)
    gw_ref[...] = jnp.concatenate(gates + [jnp.zeros((GR - heads, width), f32)], 0).astype(bf16)
    gb[...] = jnp.concatenate(biases + [jnp.zeros((GR - heads, CH), f32)], 0)


def keys_body(*refs, size, here, skipped):
    if size:
        parts, index_ref, refs = refs[:size], refs[size], refs[size + 1 :]
        held, refs = refs[-1], refs[:-1]
        wkv_ref, maps_ref, back_ref, gw_ref, wvt_ref, gb_ref = refs[-7:-1]
        refs = refs[:-7] + refs[-1:]
    else:
        wkv_ref, maps_ref, gw_ref, wvt_ref, gb_ref = refs[:5]
        refs = refs[5:]
    refs = refs[:3] + refs[3 + skipped :]
    (
        x_ref,
        ones_ref,
        tri_ref,
        phik_ref,
        v_ref,
        row_ref,
        col_ref,
        u_ref,
        end_ref,
        tot_ref,
        gsum_ref,
        tick_ref,
        acc,
    ) = refs
    tick_ref[...] = jnp.zeros_like(tick_ref)
    b, c = pl.program_id(0), pl.program_id(1)

    if size:

        @pl.when(jnp.logical_and(b == 0, c == 0))
        def _():
            collect(held, parts, index_ref[0])
            keys_setup(held, here, wkv_ref, wvt_ref, maps_ref, back_ref, gw_ref, gb_ref)

    x = x_ref[...]
    kv = dot(x, wkv_ref[...])
    width = kv.shape[1] // 2
    keys = kv[:, :width]
    v_ref[...] = kv[:, width:].astype(bf16)
    vt = dot_nt(wvt_ref[...], x).astype(bf16)
    pre = dot_nt(gw_ref[...], x) + gb_ref[...]
    soft = jnp.log1p(jnp.exp(-jnp.abs(pre)))
    log_gate = -(jnp.maximum(-pre, 0.0) + soft)
    log_keep = -(jnp.maximum(pre, 0.0) + soft)
    gate = jnp.exp(log_gate)
    keep = jnp.exp(log_keep)
    cumul = dot(split3_cat(log_gate * LOG2E), tri_ref[...])
    shifted = cumul - log_keep * LOG2E
    total = cumul[:, CH - 1 : CH]
    tail = jnp.exp2(total - shifted)
    row_ref[...] = jnp.concatenate([cumul, shifted, gate, keep], 0)
    stack = jnp.concatenate(
        [cumul, shifted, tail, gate, jnp.exp2(cumul), keep, keep, keep], 0
    )
    col_ref[...] = stack.T

    @pl.when(jnp.logical_and(b == 0, c == 0))
    def _():
        gsum_ref[...] = jnp.zeros_like(gsum_ref)

    gsum_ref[...] += gate

    @pl.when(c == 0)
    def _():
        acc[...] = jnp.zeros_like(acc)
        tot_ref[0] = jnp.zeros_like(tot_ref[0])

    tot_ref[0] += jnp.broadcast_to(total, tot_ref.shape[1:])
    ones2 = ones_ref[...]
    block_ones = jnp.ones((SR - HD, CH), f32)
    pairs = width // 128
    units = [unit(keys[:, 128 * pair : 128 * pair + 128], ones2) for pair in range(pairs)]
    phis = []

    def update(h):
        weighted = jnp.concatenate([vt[HD * h : HD * h + HD].astype(f32), block_ones], 0)
        weighted = (weighted * tail[h : h + 1]).astype(bf16)
        own = dot(weighted, phis[h])
        u_ref[0, 0, h] = own
        acc[h] = jnp.exp2(total[h : h + 1]) * acc[h] + own

    for pair in range(pairs):
        phis += pair_features(units[pair][0], maps_ref[pair])
        for h in (2 * pair, 2 * pair + 1):
            phik_ref[:, FW * h : FW * h + FW] = phis[h]
            if pair:
                update(h - 2)
    for h in (2 * pairs - 2, 2 * pairs - 1):
        update(h)

    @pl.when(c == pl.num_programs(1) - 1)
    def _():
        end_ref[0] = acc[...].astype(bf16)


def lower_mask(flip):
    rows = lax.broadcasted_iota(jnp.int32, (CH, CH), 0)
    columns = lax.broadcasted_iota(jnp.int32, (CH, CH), 1)
    return rows <= columns if flip else rows >= columns


def queries_setup(held, here, wq_ref, mix_ref):
    size = held.shape[0]
    width = wq_ref.shape[0]
    for d in range(size):
        at = width * here // 2
        rows = HD * here
        if here == 2:
            wq_ref[:, 128 * d : 128 * d + 128] = held[d, :width]
        elif d % 2:
            one, two = held[d - 1, :at], held[d, :at]
            lanes = slice(64 * d - 64, 64 * d + 64)
            wq_ref[:at, lanes] = jnp.concatenate([one[:, :HD], two[:, :HD]], 1)
            wq_ref[at:, lanes] = jnp.concatenate([one[:, HD:], two[:, HD:]], 1)
        for j in range(width // 128):
            mix_ref[rows * d : rows * d + rows, 128 * j : 128 * j + 128] = held[
                d, at + rows * j : at + rows * j + rows
            ]


def queries_body(*refs, size, here, skipped):
    parts, refs = refs[:size], refs[size:]
    if size:
        index_ref, refs = refs[0], refs[1:]
        held, refs = refs[-1], refs[:-1]
        wq_ref, mix_ref = refs[-2:]
        refs = refs[:-2]

        @pl.when(jnp.logical_and(pl.program_id(0) == 0, pl.program_id(1) == 0))
        def _():
            collect(held, parts, index_ref[0])
            queries_setup(held, here, wq_ref, mix_ref)

    else:
        wq_ref, refs = refs[0], refs[1:]
    x_ref, maps_ref, ones_ref, phik_ref, v_ref, row_ref, col_ref = refs[:7]
    phiq_ref, intra_ref, *ticks = refs[7 + skipped :]
    clear(ticks)
    query = dot(x_ref[...], wq_ref[...])
    width = query.shape[1]
    ones2 = ones_ref[...]
    lower = lower_mask(False)
    low = low_lanes(CH)
    pairs = width // 128
    units = [unit(query[:, 128 * pair : 128 * pair + 128], ones2) for pair in range(pairs)]

    def scores_of(pair, phis):
        heads = (2 * pair, 2 * pair + 1)
        augmented = both_augmented(v_ref[:, 128 * pair : 128 * pair + 128], low)
        raws = [dot_nt(phi, phik_ref[:, FW * h : FW * h + FW]) for phi, h in zip(phis, heads)]
        decays = [
            jnp.exp2(
                jnp.where(
                    lower,
                    col_ref[:, h : h + 1] - row_ref[GR + h : GR + h + 1, :],
                    -jnp.inf,
                )
            )
            for h in heads
        ]
        scores = [(raw * decay).astype(bf16) for raw, decay in zip(raws, decays)]
        for i, h in enumerate(heads):
            intra_ref[:, 128 * h : 128 * h + 128] = dot(scores[i], augmented[i])

    before = None
    for pair in range(pairs):
        phis = pair_features(units[pair][0], maps_ref[pair])
        for i, phi in enumerate(phis):
            h = 2 * pair + i
            phiq_ref[:, FW * h : FW * h + FW] = phi
        if before is not None:
            scores_of(pair - 1, before)
        before = phis
    scores_of(pairs - 1, before)


def tokens_body(
    start_refs,
    x_ref,
    c_ref,
    phiq_ref,
    intra_ref,
    row_ref,
    col_ref,
    u_ref,
    mix_ref,
    up_ref,
    down_ref,
    vec_ref,
    upb_ref,
    ones_ref,
    select_ref,
    *refs,
    chunks,
    size,
):
    (
    out_ref,
    dr_ref,
    dn_ref,
    qside_ref,
    states_ref,
    vloc_ref,
    sent_ref,
    packed_ref,
    vec_acc,
    state,
    heads_low,
    numer_all,
    inner_all,
    up_acc,
    down_acc,
    mix_acc,
    ) = refs
    b = pl.program_id(0)
    heads = state.shape[0]
    pairs = heads // 2

    @pl.when(b == 0)
    def _():
        mix_acc[...] = jnp.zeros_like(mix_acc)
        vec_acc[...] = jnp.zeros_like(vec_acc)
        up_acc[...] = jnp.zeros_like(up_acc)
        down_acc[...] = jnp.zeros_like(down_acc)

    low = low_lanes(CH)
    arrived = sum(start_ref[0].astype(f32) for start_ref in start_refs[size:])
    here = heads // size
    for d in range(size):
        part = slice(here * d, here * d + here)
        state[part] = start_refs[d][0].astype(f32) + arrived[part]
    for c in range(chunks):
        rows = slice(CH * c, CH * c + CH)
        for pair in range(pairs):
            both = (2 * pair, 2 * pair + 1)
            held = [state[h].astype(bf16) for h in both]
            carries = [
                dot_nt(phiq_ref[rows, FW * h : FW * h + FW], expand(held[i], i))
                for i, h in enumerate(both)
            ]
            for i, h in enumerate(both):
                states_ref[0, c, h] = held[i]
                last = jnp.exp2(row_ref[c, h : h + 1, CH - 1 : CH])
                state[h] = last * state[h] + u_ref[0, c, h]
            both = [
                intra_ref[rows, 128 * h : 128 * h + 128]
                + col_ref[rows, 4 * GR + h : 4 * GR + h + 1] * carry
                for h, carry in zip(both, carries)
            ]
            lanes = slice(128 * pair, 128 * pair + 128)
            numer = jnp.where(low, both[0], both[1])
            inner = pltpu.roll(jnp.where(low, both[1], both[0]), HD, 1)
            numer_all[rows, lanes] = numer
            inner_all[rows, lanes] = inner
            heads_low[rows, lanes] = (numer * lax.rsqrt(inner * inner + 1.0)).astype(bf16)
    for h in range(heads):
        states_ref[0, chunks, h] = state[h].astype(bf16)

    mix = mix_ref[...]
    rest = heads_low[...]
    mixing_bias, gain, shift, down_bias = (vec_ref[i : i + 1, :] for i in range(4))
    residual = x_ref[...].astype(f32) + dot(rest, mix) + mixing_bias
    center = residual - jnp.mean(residual, -1, keepdims=True)
    scale = lax.rsqrt(jnp.mean(center * center, -1, keepdims=True) + 1e-05)
    normal = center * scale
    normal_low = (normal * gain + shift).astype(bf16)
    normal_t = normal_low.T
    upstream = c_ref[...]
    upstream_t = upstream.T
    result = residual + down_bias
    grad_normal = jnp.zeros_like(residual)
    for j in range(up_ref.shape[1] // TILE):
        part = slice(TILE * j, TILE * j + TILE)
        up = up_ref[:, part]
        down = down_ref[part, :]
        hidden = dot(normal_low, up) + upb_ref[:, part]
        square = hidden * hidden
        th = jnp.tanh(hidden * (GELU_A + (GELU_A * GELU_B) * square))
        half = 0.5 + 0.5 * th
        active = (hidden * half).astype(bf16)
        slope = half + hidden * (0.5 - 0.5 * th * th) * (
            GELU_A + (3.0 * GELU_A * GELU_B) * square
        )
        result += dot(active, down)
        grad_hidden = slope * dot_nt(upstream, down)
        grad_hidden = grad_hidden.astype(bf16)
        vec_acc[4 + j : 5 + j, :] += jnp.sum(grad_hidden.astype(f32), 0, keepdims=True)
        grad_normal += dot_nt(grad_hidden, up)
        up_acc[:, part] += dot(normal_t, grad_hidden)
        down_acc[:, part] += dot(upstream_t, active)
    out_ref[...] = result.astype(bf16)
    upstream = upstream.astype(f32)
    dn = grad_normal * gain
    grad_residual = upstream + scale * (
        dn
        - jnp.mean(dn, -1, keepdims=True)
        - normal * jnp.mean(dn * normal, -1, keepdims=True)
    )
    dr_ref[...] = grad_residual
    for i, value in enumerate((grad_residual, grad_normal * normal, grad_normal, upstream)):
        vec_acc[i : i + 1, :] += jnp.sum(value, 0, keepdims=True)
    grad_low = grad_residual.astype(bf16)
    mix_acc[...] += dot_tn(rest, grad_low)
    grad_heads = dot_nt(grad_low, mix)

    ones2 = ones_ref[...]
    following = [None] * heads
    for c in reversed(range(chunks)):
        rows = slice(CH * c, CH * c + CH)
        grad_numers, squares, query_sides = [], [], []
        for pair in range(pairs):
            lanes = slice(128 * pair, 128 * pair + 128)
            inner = inner_all[rows, lanes]
            squares.append(1.0 / (inner * inner + 1.0))
            grad_numers.append(grad_heads[rows, lanes] * lax.rsqrt(inner * inner + 1.0))
            query_sides.append(
                dot(split2_cat(grad_numers[pair] * numer_all[rows, lanes]), ones2)
            )
        query_sides = [side * square for side, square in zip(query_sides, squares)]
        for pair in range(pairs):
            inner = inner_all[rows, 128 * pair : 128 * pair + 128]
            grad_inner = pltpu.roll(query_sides[pair] * inner * (-1.0 / HD), HD, 1)
            low_part = jnp.where(low, grad_numers[pair], grad_inner)
            high_part = jnp.where(low, grad_inner, grad_numers[pair])
            sent = []
            for h, together in ((2 * pair, low_part), (2 * pair + 1, high_part)):
                dn_ref[rows, 128 * h : 128 * h + 128] = together.astype(bf16)
                carried = col_ref[rows, 4 * GR + h : 4 * GR + h + 1]
                sent.append((carried * together).T.astype(bf16))
            for i, h in enumerate((2 * pair, 2 * pair + 1)):
                own = shrink(dot(sent[i], phiq_ref[rows, FW * h : FW * h + FW]), i)
                vloc_ref[0, c, h] = own
                if following[h] is not None:
                    last = jnp.exp2(row_ref[c, h : h + 1, CH - 1 : CH])
                    own = own + last * following[h]
                following[h] = own
        qside_ref[rows, :] = dot(
            split2_cat(jnp.concatenate(query_sides, 1)), select_ref[...]
        )
    for h in range(heads):
        sent_ref[0, h] = following[h].astype(bf16)

    @pl.when(b == pl.num_programs(0) - 1)
    def _():
        width, ff = up_acc.shape
        up_rows, down_rows, mix_rows = width // size, ff // size, mix_acc.shape[0] // size
        for d in range(size):
            at = d * (packed_ref.shape[0] // size)
            for j in range(ff // TILE):
                packed_ref[at : at + up_rows, :] = up_acc[
                    up_rows * d : up_rows * d + up_rows, TILE * j : TILE * j + TILE
                ].astype(bf16)
                at += up_rows
            packed_ref[at : at + down_rows, :] = (
                down_acc[:, down_rows * d : down_rows * d + down_rows].T.astype(bf16)
            )
            at += down_rows
            packed_ref[at : at + mix_rows, :] = mix_acc[
                mix_rows * d : mix_rows * d + mix_rows, :
            ].astype(bf16)


def query_back_body(
    x_ref,
    wq_ref,
    maps_back_ref,
    ones_ref,
    phiq_ref,
    phik_ref,
    v_ref,
    dn_ref,
    row_ref,
    col_ref,
    states_ref,
    *refs,
):
    dq_ref, dphik_ref, dv_ref, wqg_ref, *ticks = refs[-7:]
    clear(ticks)
    first = jnp.logical_and(pl.program_id(0) == 0, pl.program_id(1) == 0)

    @pl.when(first)
    def _():
        wqg_ref[...] = jnp.zeros_like(wqg_ref)

    x = x_ref[...]
    query = dot(x, wq_ref[...])
    width = query.shape[1]
    ones2 = ones_ref[...]
    mask = lower_mask(True)
    low = low_lanes(CH)
    pairs = width // 128
    units = [unit(query[:, 128 * pair : 128 * pair + 128], ones2) for pair in range(pairs)]
    angle_grads = []
    for pair in range(pairs):
        heads = (2 * pair, 2 * pair + 1)
        augmented = both_augmented(v_ref[:, 128 * pair : 128 * pair + 128], low)
        phiqs = [phiq_ref[:, FW * h : FW * h + FW] for h in heads]
        phiks = [phik_ref[:, FW * h : FW * h + FW] for h in heads]
        grads = [dn_ref[:, 128 * h : 128 * h + 128] for h in heads]
        raws = [dot_nt(phik, phiq) for phik, phiq in zip(phiks, phiqs)]
        raw_grads = [dot_nt(values, grad) for values, grad in zip(augmented, grads)]
        decays = [
            jnp.exp2(
                jnp.where(
                    mask,
                    row_ref[h : h + 1, :] - col_ref[:, GR + h : GR + h + 1],
                    -jnp.inf,
                )
            )
            for h in heads
        ]
        scores = [(raw * decay).astype(bf16) for raw, decay in zip(raws, decays)]
        raw_grads = [(grad * decay).astype(bf16) for grad, decay in zip(raw_grads, decays)]
        for i, h in enumerate(heads):
            dv_ref[:, 128 * h : 128 * h + 128] = dot(scores[i], grads[i]).astype(bf16)
        for i, h in enumerate(heads):
            dphik_ref[:, FW * h : FW * h + FW] = dot(raw_grads[i], phiqs[i]).astype(bf16)
        dphis = [
            dot_tn(raw_grads[i], phiks[i])
            + col_ref[:, 4 * GR + h : 4 * GR + h + 1]
            * dot(grads[i], expand(states_ref[0, 0, h], i))
            for i, h in enumerate(heads)
        ]
        angle_grads.append(
            jnp.concatenate([angle_gradient(dphi, phi) for dphi, phi in zip(dphis, phiqs)], 1)
        )
    for pair, dq in enumerate(feature_back(units, angle_grads, maps_back_ref, ones2)):
        dq_ref[:, 128 * pair : 128 * pair + 128] = dq.astype(bf16)
    wqg_ref[...] += dot_tn(x, dq_ref[...])


def key_back_body(
    end_refs,
    x_ref,
    wq_ref,
    wkv_ref,
    maps_back_ref,
    gw_ref,
    ones_ref,
    all_ref,
    tri_ref,
    phik_ref,
    v_ref,
    dq_ref,
    dphik_ref,
    dv_ref,
    qside_ref,
    row_ref,
    col_ref,
    states_ref,
    vloc_ref,
    dr_ref,
    factor_ref,
    *refs,
):
    dx_ref, wkvg_ref, gwg_ref, gbg_ref, *ticks, grads, state_grad, sides = refs[-10:]
    clear(ticks)
    first = jnp.logical_and(pl.program_id(0) == 0, pl.program_id(1) == 0)

    @pl.when(first)
    def _():
        wkvg_ref[...] = jnp.zeros_like(wkvg_ref)
        gwg_ref[...] = jnp.zeros_like(gwg_ref)
        gbg_ref[...] = jnp.zeros_like(gbg_ref)

    @pl.when(pl.program_id(1) == 0)
    def _():
        state_grad[...] = sum(end_ref[0].astype(f32) for end_ref in end_refs)

    x = x_ref[...]
    heads = state_grad.shape[0]
    keys = dot(x, wkv_ref[:, : wq_ref.shape[1]])
    width = wq_ref.shape[1]
    ones2 = ones_ref[...]
    low = low_lanes(CH)
    weigh = jnp.where(lax.broadcasted_iota(jnp.int32, (SR, FW), 0) < HD, 1.0, 4.0)
    bounds = []
    units = [unit(keys[:, 128 * pair : 128 * pair + 128], ones2) for pair in range(heads // 2)]
    angle_grads = []
    for pair in range(heads // 2):
        lanes = slice(128 * pair, 128 * pair + 128)
        both = (2 * pair, 2 * pair + 1)
        augmented = both_augmented(v_ref[:, lanes], low)
        phiks = [phik_ref[:, FW * h : FW * h + FW] for h in both]
        tails = [col_ref[:, 2 * GR + h : 2 * GR + h + 1] for h in both]
        spreads = [expand(state_grad[h].astype(bf16), i) for i, h in enumerate(both)]
        dvs = [dot_nt(phik, spread) for phik, spread in zip(phiks, spreads)]
        dphis = [dot(values, spread) for values, spread in zip(augmented, spreads)]
        dvs = [
            dv_ref[:, 128 * h : 128 * h + 128] + tails[i] * dvs[i] for i, h in enumerate(both)
        ]
        for i, h in enumerate(both):
            sides[:, 128 * h : 128 * h + 128] = dvs[i] * augmented[i].astype(f32)
        angle_grads.append(
            jnp.concatenate(
                [
                    angle_gradient(
                        dphik_ref[:, FW * h : FW * h + FW].astype(f32) + tails[i] * dphis[i],
                        phiks[i],
                    )
                    for i, h in enumerate(both)
                ],
                1,
            )
        )
        grads[:, width + 128 * pair : width + 128 * pair + 128] = jnp.where(
            low, dvs[0], dvs[1]
        ).astype(bf16)
        for h in both:
            grad_end = state_grad[h]
            bounds.append(
                jnp.sum(grad_end * weigh * states_ref[0, 0, h].astype(f32), 0, keepdims=True)
            )
            last = jnp.exp2(row_ref[h : h + 1, CH - 1 : CH])
            state_grad[h] = last * grad_end + vloc_ref[0, 0, h]
    for pair, dk in enumerate(feature_back(units, angle_grads, maps_back_ref, ones2)):
        grads[:, 128 * pair : 128 * pair + 128] = dk.astype(bf16)
    key_side = dot(split2_cat(sides[...]), all_ref[...])
    key_row = key_side.T[:GR]
    differ = qside_ref[...].T[:GR] - key_row
    bound = jnp.sum(jnp.concatenate(bounds, 0), 1, keepdims=True)
    bound = jnp.concatenate([bound, jnp.zeros((GR - heads, 1), f32)], 0)
    grad_log = dot(split3_cat(differ), tri_ref[...]) + bound
    gate, keep = row_ref[2 * GR : 3 * GR, :], row_ref[3 * GR : 4 * GR, :]
    grad_pre = (
        grad_log * keep - gate * key_row + factor_ref[...] * gate * keep
    ).astype(bf16)
    gbg_ref[...] += grad_pre.astype(f32)
    gwg_ref[...] += dot(grad_pre, x)
    together = grads[...]
    wkvg_ref[...] += dot_tn(x, together)
    dx_ref[...] = (
        dr_ref[...]
        + dot_nt(dq_ref[...], wq_ref[...])
        + dot_nt(together, wkv_ref[...])
        + dot_tn(grad_pre, gw_ref[...])
    )


def unpack_body(index_ref, every_ref, _, up_ref, down_ref, mix_ref, tick_ref, *, places):
    rows, ff = up_ref.shape
    width = down_ref.shape[1]
    depth = every_ref.shape[1]
    slab = depth * every_ref.shape[0] // pl.num_programs(0)
    tick_ref[...] = jnp.zeros_like(tick_ref)

    def copy(first, count, ref, lanes):
        done = 0
        while done < count:
            piece, at = divmod(first + done, depth)
            number = min(count - done, depth - at)
            ref[done : done + number, lanes] = every_ref[
                places[piece], at : at + number, :
            ].astype(f32)
            done += number

    for d in range(pl.num_programs(0)):

        @pl.when(pl.program_id(0) == d)
        def _(d=d):
            first = slab * d
            for j in range(ff // TILE):
                copy(first, rows, up_ref, slice(TILE * j, TILE * j + TILE))
                first += rows
            copy(first, down_ref.shape[0], down_ref, slice(0, width))
            first += down_ref.shape[0]

            @pl.when(index_ref[0] == d)
            def _():
                copy(first, mix_ref.shape[0], mix_ref, slice(0, width))


def pack_body(key_ref, value_ref, query_ref, mix_ref, maps_ref, tail_ref, first_ref, second_ref):
    width, own = key_ref.shape
    if own == 128:
        first_ref[:width] = key_ref[...]
        first_ref[width : 2 * width] = value_ref[...]
        second_ref[:width] = query_ref[...]
        at, then = 2 * width, width
    else:
        half = width // 2
        first_ref[:width] = jnp.concatenate([key_ref[...], value_ref[...]], 1)
        second_ref[:half] = jnp.concatenate([query_ref[:half], query_ref[half:]], 1)
        at, then = width, half
    high, rest = split2(maps_ref[...] * (0.5 / math.pi))
    first_ref[at : at + own] = high
    first_ref[at + own : at + 2 * own] = rest
    first_ref[at + 2 * own :] = tail_ref[...]
    for j in range(width // 128):
        second_ref[then + own * j : then + own * j + own] = mix_ref[:, 128 * j : 128 * j + 128]


def group_body(*refs, queries, keys, order):
    query_refs, refs = refs[:queries], refs[queries:]
    key_refs, refs = refs[:keys], refs[keys:]
    gate_refs, refs = refs[:keys], refs[keys:]
    bias_refs, (vector_ref, out_ref) = refs[:keys], refs[keys:]
    width = query_refs[0].shape[0]
    own = out_ref.shape[2]
    inner = query_refs[0].shape[1]
    here = own // HD
    cuts = width // own

    def total(parts, lanes):
        value = parts[0][:, lanes]
        for part in parts[1:]:
            value = value + part[:, lanes]
        return value

    every = slice(None)
    gates = total(gate_refs, every)
    biases = jnp.sum(total(bias_refs, every), 1, keepdims=True)
    vectors = vector_ref[...]
    vectors = jnp.concatenate(
        [vectors[r : r + 1, own * j : own * j + own] for r in range(8) for j in range(cuts)], 0
    )
    at = 3 * width + GR
    used = at + 8 * cuts
    lane = lax.broadcasted_iota(jnp.int32, (1, own), 1)
    for d, place in enumerate(order):
        lanes = slice(own * d, own * d + own)
        out_ref[place, :width] = total(query_refs, lanes).astype(bf16)
        out_ref[place, width : 2 * width] = total(key_refs, lanes).astype(bf16)
        lanes = slice(inner + own * d, inner + own * d + own)
        out_ref[place, 2 * width : 3 * width] = total(key_refs, lanes).astype(bf16)
        rows = [
            gates[h : h + 1, own * j : own * j + own]
            for h in range(here * d, here * d + here)
            for j in range(cuts)
        ]
        bias = jnp.zeros((1, own), f32)
        for i in range(here):
            bias = jnp.where(lane == i, biases[here * d + i : here * d + i + 1], bias)
        rows += [bias, jnp.zeros((GR - 1 - here * cuts, own), f32)]
        out_ref[place, 3 * width : at] = jnp.concatenate(rows, 0).astype(bf16)
        out_ref[place, at:used] = vectors.astype(bf16)
        if used < out_ref.shape[1]:
            out_ref[place, used:] = jnp.zeros((out_ref.shape[1] - used, own), bf16)


def tokens_entry(*refs, starts, **named):
    tokens_body(refs[:starts], *refs[starts:], **named)


def key_back_entry(*refs, arrivals):
    key_back_body(refs[:arrivals], *refs[arrivals:])


def whole(array):
    zeros = (0,) * len(array.shape)
    return pl.BlockSpec(array.shape, lambda *_: zeros, pipeline_mode=pl.Buffered(1))


def fixed(shape):
    zeros = (0,) * len(shape)
    return pl.BlockSpec(shape, lambda *_: zeros)


def call(body, grid, ins, outs, previous=(), after=(), scratch=(), name=None, flops=0, room=48):
    extra = list(previous) + list(after)
    specs = [spec for _, spec in ins] + [pl.BlockSpec(memory_space=pl.ANY)] * len(extra)
    return pl.pallas_call(
        body,
        grid=grid,
        in_specs=specs,
        out_specs=[spec for _, _, spec in outs],
        out_shape=[jax.ShapeDtypeStruct(shape, kind) for shape, kind, _ in outs],
        scratch_shapes=list(scratch),
        input_output_aliases={len(ins) + i: i for i in range(len(previous))},
        compiler_params=pltpu.CompilerParams(
            dimension_semantics=("arbitrary",) * len(grid), vmem_limit_bytes=room * 1024 * 1024
        ),
        cost_estimate=pl.CostEstimate(flops=flops, bytes_accessed=4 << 20, transcendentals=0),
        name=name,
    )(*[array for array, _ in ins], *extra)


def swap(x, axis, bit):
    size = lax.axis_size(axis)
    return lax.ppermute(x, axis, [(i, i ^ bit) for i in range(size)])


def spread_head(part):
    parts = [part]
    for k in range(1, lax.axis_size("head")):
        parts.append(swap(parts[k - 1], "head", 1) if k % 2 else swap(part, "head", k))
    return parts


def place_in(axis, bit, number):
    return (lax.axis_index(axis) // bit) % number


class HalvingSum:
    def __init__(self, array):
        self.terms = [(array, 0)]
        self.length = array.shape[0]

    def part(self, offset, tick=0.0):
        total = tick
        for array, start in self.terms:
            piece = lax.dynamic_slice_in_dim(array, start + offset, self.length, 0)
            total = total + piece.astype(f32)
        return total.astype(bf16)

    def step(self, axis, bit, number=2, tick=0.0):
        self.length //= number
        mine = place_in(axis, bit, number)
        sends = [self.part((mine ^ k) * self.length, tick) for k in range(1, number)]
        self.terms = [(array, start + mine * self.length) for array, start in self.terms]
        for k, send in enumerate(sends):
            self.terms.append((swap(send, axis, (k + 1) * bit), 0))
        return sends


def open_join(array, axis, bit, number):
    return [array] + [swap(array, axis, k * bit) for k in range(1, number)]


def close_join(parts, axis, bit):
    number = len(parts)
    mine = place_in(axis, bit, number).astype(jnp.int32)
    if number == 2:
        own, other = parts
        return jnp.where(
            mine == 0, jnp.concatenate([own, other], 0), jnp.concatenate([other, own], 0)
        )
    return jnp.concatenate(
        [
            lax.select_n(mine, *[parts[j ^ place] for place in range(number)])
            if number <= 4
            else jnp.take(jnp.stack(parts), mine ^ j, axis=0)
            for j in range(number)
        ],
        0,
    )


def gather_all(piece, stages):
    every = lax.all_gather(piece, ("dp", "head"), axis=0, tiled=False)
    names = [
        (axis, 1 << i)
        for axis in ("dp", "head")
        for i in reversed(range(lax.axis_size(axis).bit_length() - 1))
    ]
    places = np.arange(1 << len(names)).reshape((2,) * len(names))
    singles = []
    for axis, bit, number in stages:
        while number > 1:
            number //= 2
            singles.append((axis, bit * number))
    places = places.transpose([names.index(single) for single in singles]).reshape(-1)
    if piece.shape[0] % GR:
        every = every[places].reshape(1, -1, piece.shape[1])
        places = places[:1] * 0
    return every, tuple(int(place) for place in places)


def high_rest(x):
    high = lax.reduce_precision(x, 8, 7)
    return high, x - high


def per_device(
    tokens,
    cotangent,
    carry_state,
    carry_norm,
    random_maps,
    query_weight,
    key_weight,
    value_weight,
    gate_weight,
    gate_bias,
    mixing_weight,
    mixing_bias,
    norm_gain,
    norm_bias,
    up_weight,
    up_bias,
    down_weight,
    down_bias,
):
    seqs, length, width = tokens.shape
    here = gate_weight.shape[1]
    size = lax.axis_size("head")
    replicas = lax.axis_size("dp")
    index = lax.axis_index("head")
    heads = here * size
    chunks = length // CH
    blocks = seqs * chunks
    count = seqs * length
    inner_width = heads * HD
    own = here * HD
    ff = up_weight.shape[1]
    pairs = heads // 2
    head_bits = [1 << i for i in range(size.bit_length() - 1)]
    stages = (
        [("head", 1, 2), ("dp", 1, min(2, replicas))]
        + [("head", bit, 2) for bit in head_bits[1:]]
        + [("dp", 2, replicas // 2)]
    )
    index_array = index.astype(jnp.int32).reshape(1)
    smem = pl.BlockSpec(memory_space=pltpu.SMEM)

    bias_high, bias_rest = high_rest(gate_bias)
    bias_mid, bias_rest = high_rest(bias_rest)
    biases = jnp.pad(jnp.stack([bias_high, bias_mid, bias_rest]), ((0, 0), (0, 128 - here)))
    tail = jnp.concatenate([gate_weight.T.reshape(-1, 128).astype(f32), biases])
    tail = jnp.pad(tail, ((0, GR - tail.shape[0]), (0, 0)))
    tail = tail.astype(bf16)
    packing = (key_weight, value_weight, query_weight, mixing_weight, random_maps.reshape(own, NF), tail)
    first_rows = (width * here + 2 * own + GR, 128)
    second_rows = (width * here, 128)
    first_part, second_part = call(
        pack_body,
        (1,),
        [(array, fixed(array.shape)) for array in packing],
        [(first_rows, bf16, fixed(first_rows)), (second_rows, bf16, fixed(second_rows))],
        name="pack",
        room=62,
        flops=1_000_000,
    )
    first_parts = spread_head(first_part)

    begin = jnp.concatenate(
        [
            carry_state.transpose(0, 1, 3, 2),
            jnp.broadcast_to(carry_norm[:, :, None, :], (seqs, here, SR - HD, FW)),
        ],
        2,
    ).astype(bf16)

    half = np.arange(128) // HD
    ones2 = np.tile((half[:, None] == half[None, :]).astype(np.float32), (2, 1))
    ones2 = jnp.asarray(ones2, bf16)
    place = np.arange(CH)
    upto = jnp.asarray(np.tile((place[:, None] <= place[None, :]).astype(np.float32), (3, 1)), bf16)
    onward = jnp.asarray(np.tile((place[:, None] >= place[None, :]).astype(np.float32), (3, 1)), bf16)
    lane = np.arange(128)
    one_lane = np.zeros((inner_width, 128), np.float32)
    one_lane[np.arange(heads) * HD, np.arange(heads)] = 1.0
    select = jnp.asarray(np.tile(one_lane, (2, 1)), bf16)
    all_lanes = (np.arange(heads * 128) // 128)[:, None] == lane[None, :]
    all_lanes = jnp.asarray(np.tile(all_lanes.astype(np.float32), (2, 1)), bf16)

    x = tokens.reshape(count, width)
    c = cotangent.reshape(count, width)
    state_shape = (heads, SR, FW)
    tick_outs = [((1, lanes), f32, fixed((1, lanes))) for lanes in (128, FW, width)]

    def rows_of(columns, base=0, reverse=False):
        def at(b, t):
            return ((base + b) * chunks + (chunks - 1 - t if reverse else t), 0)

        return pl.BlockSpec((CH, columns), at)

    def row_spec(base=0, reverse=False):
        return pl.BlockSpec((4 * GR, CH), rows_of(0, base, reverse).index_map)

    def per_block(shape, base=0, offset=0, reverse=False):
        zeros = (0,) * len(shape)

        def at(b, t):
            return (base + b, offset + (chunks - 1 - t if reverse else t)) + zeros

        return pl.BlockSpec((1, 1) + shape, at)

    def per_seq(base=0):
        return pl.BlockSpec((1,) + state_shape, lambda b, t: (base + b, 0, 0, 0))

    weights = [
        ((width, 2 * inner_width), bf16),
        ((pairs, 3 * 128, FW), bf16),
        ((pairs, 3 * FW, 128), bf16),
        ((GR, width), bf16),
        ((inner_width, width), bf16),
        ((GR, CH), f32),
    ]
    weights = [(shape, kind, fixed(shape)) for shape, kind in weights]

    def keys_ins(base):
        return [(x, rows_of(width, base)), (ones2, whole(ones2)), (upto, whole(upto))]

    def keys_outs(base):
        total_spec = pl.BlockSpec((1, GR, 128), lambda b, t: (base + b, 0, 0))
        return [
            ((count, heads * FW), bf16, rows_of(heads * FW, base)),
            ((count, inner_width), bf16, rows_of(inner_width, base)),
            ((blocks * 4 * GR, CH), f32, row_spec(base)),
            ((count, 128), f32, rows_of(128, base)),
            ((seqs, chunks) + state_shape, f32, per_block(state_shape, base)),
            ((seqs,) + state_shape, bf16, per_seq(base)),
            ((seqs, GR, 128), f32, total_spec),
            ((GR, CH), f32, fixed((GR, CH))),
            ((1, FW), f32, fixed((1, FW))),
        ]

    *previous, gate_sums, tick, wkv, maps_front, maps_back, gw, wvt, gb = call(
        functools.partial(keys_body, size=size, here=here, skipped=2),
        (2, chunks),
        [(part, whole(part)) for part in first_parts] + [(index_array, smem)] + keys_ins(0),
        keys_outs(0) + weights,
        after=[second_part, begin],
        scratch=[
            pltpu.VMEM(state_shape, f32),
            pltpu.VMEM((size,) + first_part.shape, bf16),
        ],
        name="keys",
        flops=10_000_000_000,
    )
    second_parts = [second_part] + [swap(second_part, "head", k) for k in range(1, size)]
    begins = [jnp.where(index == 0, begin, jnp.zeros_like(begin))] + [
        lax.ppermute(begin, "head", [(k, 0)]) for k in range(1, size)
    ]
    phik, v, row, col, update, end, total, more_sums, tick = call(
        functools.partial(keys_body, size=0, here=here, skipped=2 * size - 2 + len(previous)),
        (seqs - 2, chunks),
        [(part, whole(part)) for part in (wkv, maps_front, gw, wvt, gb)] + keys_ins(2),
        keys_outs(2),
        previous=previous,
        after=second_parts[1:] + begins[1:],
        scratch=[pltpu.VMEM(state_shape, f32)],
        name="keys",
        flops=10_000_000_000,
    )
    gate_sums = lax.all_gather(
        jnp.concatenate([gate_sums, more_sums]), ("dp", "head"), axis=0, tiled=True
    )
    last = jnp.exp2(total[:, :heads, 0])[:, :, None, None]
    begin = jnp.concatenate(begins, 1)

    sent = (end.astype(f32) + last * begin.astype(f32)).astype(bf16)
    starts = []
    ticks = (0.0, 0.0, 0.0)
    phiq = intra = wq = mix = None
    previous = ()
    for step, (base, number) in enumerate(((0, 1), (1, 2), (3, 1))):
        arrived = None
        if step < size - 1:
            arrived = lax.ppermute(sent, "head", [(step, step + 1)])
            starts.append(arrived)
        main = [
            (x, rows_of(width, base)),
            (maps_front, whole(maps_front)),
            (ones2, whole(ones2)),
            (phik, rows_of(heads * FW, base)),
            (v, rows_of(inner_width, base)),
            (row, row_spec(base)),
            (col, rows_of(128, base)),
        ]
        outs = [
            ((count, heads * FW), bf16, rows_of(heads * FW, base)),
            ((count, heads * 128), f32, rows_of(heads * 128, base)),
        ] + tick_outs
        if step == 0:
            phiq, intra, *ticks, wq, mix = call(
                functools.partial(queries_body, size=size, here=here, skipped=1),
                (number, chunks),
                [(part, whole(part)) for part in second_parts] + [(index_array, smem)] + main,
                outs
                + [
                    ((width, inner_width), bf16, fixed((width, inner_width))),
                    ((inner_width, width), bf16, fixed((inner_width, width))),
                ],
                after=[sent],
                scratch=[pltpu.VMEM((size,) + second_part.shape, bf16)],
                name="queries",
                flops=5_000_000_000,
            )
        else:
            phiq, intra, *ticks = call(
                functools.partial(queries_body, size=0, here=here, skipped=3),
                (number, chunks),
                [(wq, whole(wq))] + main,
                outs,
                previous=[phiq, intra],
                after=[sent],
                name="queries",
                flops=5_000_000_000 * number,
            )
        if step < size - 2:
            sent = (last * arrived.astype(f32) + end.astype(f32) + ticks[1][0]).astype(bf16)
    for step in range(3, size - 1):
        arrived = lax.ppermute(sent, "head", [(step, step + 1)])
        starts.append(arrived)
        sent = (last * arrived.astype(f32) + end.astype(f32)).astype(bf16)

    vectors = jnp.stack([mixing_bias, norm_gain, norm_bias, down_bias] * 2)

    def seq_rows(columns):
        return pl.BlockSpec((length, columns), lambda b: (b, 0))

    def seq_block(*shape):
        zeros = (0,) * len(shape)
        return pl.BlockSpec((1,) + shape, lambda b: (b,) + zeros)

    up_bias2 = up_bias.reshape(1, ff)
    slab = (width // size) * (ff // TILE) + ff // size + own
    layer_out, dr, dn, qside, states, vloc, vdev, packed, vector_grads = call(
        functools.partial(
            tokens_entry, starts=len(begins) + len(starts), chunks=chunks, size=size
        ),
        (seqs,),
        [(start, seq_block(*start.shape[1:])) for start in begins + starts]
        + [
            (x, seq_rows(width)),
            (c, seq_rows(width)),
            (phiq, seq_rows(heads * FW)),
            (intra, seq_rows(heads * 128)),
            (
                row.reshape(blocks, 4 * GR, CH),
                pl.BlockSpec((chunks, 4 * GR, CH), lambda b: (b, 0, 0)),
            ),
            (col, seq_rows(128)),
            (update, seq_block(chunks, *state_shape)),
            (mix, whole(mix)),
            (up_weight, whole(up_weight)),
            (down_weight, whole(down_weight)),
            (vectors, whole(vectors)),
            (up_bias2, whole(up_bias2)),
            (ones2, whole(ones2)),
            (select, whole(select)),
        ],
        [
            ((count, width), bf16, seq_rows(width)),
            ((count, width), f32, seq_rows(width)),
            ((count, heads * 128), bf16, seq_rows(heads * 128)),
            ((count, 128), f32, seq_rows(128)),
            ((seqs, chunks + 1) + state_shape, bf16, seq_block(chunks + 1, *state_shape)),
            ((seqs, chunks) + state_shape, f32, seq_block(chunks, *state_shape)),
            ((seqs,) + state_shape, bf16, seq_block(*state_shape)),
            ((size * slab, width), bf16, fixed((size * slab, width))),
            ((8, width), f32, fixed((8, width))),
        ],
        scratch=[
            pltpu.VMEM(state_shape, f32),
            pltpu.VMEM((length, inner_width), bf16),
            pltpu.VMEM((length, inner_width), f32),
            pltpu.VMEM((length, inner_width), f32),
            pltpu.VMEM((width, ff), f32),
            pltpu.VMEM((width, ff), f32),
            pltpu.VMEM((inner_width, width), f32),
        ],
        name="tokens",
        room=62,
        flops=50_000_000_000,
    )

    sent = vdev
    waiting = list(stages)
    sums = HalvingSum(packed)
    ticks = (0.0, [0.0], 0.0)
    finishes = []
    dq = dphik = dv = None
    previous = []
    query_grads = []
    for step, (base, number) in enumerate(((0, 1), (1, 2), (3, 1))):
        after = sums.step(*waiting.pop(0), ticks[2])
        if step < size - 1:
            arrived = lax.ppermute(sent, "head", [(size - 1 - step, size - 2 - step)])
            finishes.append(arrived)
            after.append(sent)
        dq, dphik, dv, query_grad, *ticks = call(
            query_back_body,
            (number, chunks),
            [
                (x, rows_of(width, base)),
                (wq, whole(wq)),
                (maps_back, whole(maps_back)),
                (ones2, whole(ones2)),
                (phiq, rows_of(heads * FW, base)),
                (phik, rows_of(heads * FW, base)),
                (v, rows_of(inner_width, base)),
                (dn, rows_of(heads * 128, base)),
                (row, row_spec(base)),
                (col, rows_of(128, base)),
                (states, per_block(state_shape, base)),
            ],
            [
                ((count, inner_width), bf16, rows_of(inner_width, base)),
                ((count, heads * FW), bf16, rows_of(heads * FW, base)),
                ((count, heads * 128), bf16, rows_of(heads * 128, base)),
                ((width, inner_width), f32, fixed((width, inner_width))),
            ] + tick_outs,
            previous=previous,
            after=after,
            name="query_back",
            flops=8_000_000_000 * number,
        )
        previous = [dq, dphik, dv]
        query_grads.append(query_grad)
        if step < size - 2:
            sent = (last * arrived.astype(f32) + vdev.astype(f32) + ticks[1][0]).astype(bf16)
    for step in range(3, size - 1):
        arrived = lax.ppermute(sent, "head", [(size - 1 - step, size - 2 - step)])
        finishes.append(arrived)
        sent = (last * arrived.astype(f32) + vdev.astype(f32)).astype(bf16)

    gate_total = jnp.sum(gate_sums.reshape(-1, GR, CH)[:, :heads] + ticks[1][0])
    gate_count = replicas * heads * size * count
    mean_gate = gate_total / gate_count
    factor = 2.0 * penalty_weight * (mean_gate - target_gate) / heads
    factor = jnp.broadcast_to(factor, (1, CH))

    tokens_grad = None
    previous = []
    key_value_grads, gate_grads, gate_bias_grads = [], [], []
    for base, number in ((0, 2), (2, 2)):
        after = []
        if base == 0:
            while waiting:
                after = sums.step(*waiting.pop(0), ticks[2])
        else:
            piece = sums.part(0, ticks[2])
            after = [piece]
            every, places = gather_all(piece, stages)
        tokens_grad, key_value_grad, gate_grad, gate_bias_grad, *ticks = call(
            functools.partial(key_back_entry, arrivals=len(finishes)),
            (number, chunks),
            [(finish, per_seq(base)) for finish in finishes]
            + [
                (x, rows_of(width, base, True)),
                (wq, whole(wq)),
                (wkv, whole(wkv)),
                (maps_back, whole(maps_back)),
                (gw, whole(gw)),
                (ones2, whole(ones2)),
                (all_lanes, whole(all_lanes)),
                (onward, whole(onward)),
                (phik, rows_of(heads * FW, base, True)),
                (v, rows_of(inner_width, base, True)),
                (dq, rows_of(inner_width, base, True)),
                (dphik, rows_of(heads * FW, base, True)),
                (dv, rows_of(heads * 128, base, True)),
                (qside, rows_of(128, base, True)),
                (row, row_spec(base, True)),
                (col, rows_of(128, base, True)),
                (states, per_block(state_shape, base, 1, True)),
                (vloc, per_block(state_shape, base, 0, True)),
                (dr, rows_of(width, base, True)),
                (factor, whole(factor)),
            ],
            [
                ((count, width), f32, rows_of(width, base, True)),
                ((width, 2 * inner_width), f32, fixed((width, 2 * inner_width))),
                ((GR, width), f32, fixed((GR, width))),
                ((GR, CH), f32, fixed((GR, CH))),
            ] + tick_outs,
            previous=previous,
            after=after,
            scratch=[
                pltpu.VMEM((CH, 2 * inner_width), bf16),
                pltpu.VMEM(state_shape, f32),
                pltpu.VMEM((CH, heads * 128), f32),
            ],
            name="key_back",
            room=58,
            flops=8_000_000_000 * number,
        )
        previous = [tokens_grad]
        key_value_grads.append(key_value_grad)
        gate_grads.append(gate_grad)
        gate_bias_grads.append(gate_bias_grad)
    rows = 3 * width + GR + 8 * width // own
    rows += -rows % replicas
    order = [
        sum(((d >> i) & 1) << (len(head_bits) - 1 - i) for i in range(len(head_bits)))
        for d in range(size)
    ]
    parts = query_grads + key_value_grads + gate_grads + gate_bias_grads + [vector_grads]
    (group,) = call(
        functools.partial(
            group_body, queries=len(query_grads), keys=len(key_value_grads), order=order
        ),
        (1,),
        [(part, fixed(part.shape)) for part in parts],
        [((size, rows, own), bf16, fixed((size, rows, own)))],
        name="group",
        room=62,
        flops=1_000_000,
    )
    group_sums = HalvingSum(group.reshape(-1, own))
    for bit in head_bits:
        group_sums.step("head", bit)
    across = [stage for stage in stages if stage[0] == "dp"]
    for stage in across:
        group_sums.step(*stage)
    group = group_sums.part(0)
    for axis, bit, number in reversed(across[1:]):
        group = close_join(open_join(group, axis, bit, number), axis, bit)
    group, other = open_join(group, *across[0])
    up_grad, down_grad, mixing_grad, tick = call(
        functools.partial(unpack_body, places=places),
        (size,),
        [(index_array, smem), (every, whole(every))],
        [
            ((width, ff), f32, pl.BlockSpec((width // size, ff), lambda d: (d, 0))),
            ((ff, width), f32, pl.BlockSpec((ff // size, width), lambda d: (d, 0))),
            ((own, width), f32, fixed((own, width))),
            ((1, own), f32, fixed((1, own))),
        ],
        after=[group],
        name="unpack",
        flops=1_000_000_000,
    )
    group = close_join([group + tick.astype(bf16), other], *across[0][:2])
    group = group.astype(f32)
    gate_rows = here * width // own
    gate_grad = group[3 * width : 3 * width + gate_rows].reshape(here, width).T
    at = 3 * width + GR
    vector_grads = group[at : at + 8 * width // own].reshape(8, width)
    penalty = penalty_weight * (mean_gate - target_gate) * (mean_gate - target_gate)
    return (
        layer_out.reshape(seqs, length, width),
        tokens_grad.reshape(seqs, length, width),
        penalty,
        group[:width],
        group[width : 2 * width],
        group[2 * width : 3 * width],
        gate_grad,
        group[3 * width + gate_rows, :here],
        mixing_grad,
        vector_grads[0],
        vector_grads[1],
        vector_grads[2],
        up_grad,
        vector_grads[4:].reshape(ff),
        down_grad,
        vector_grads[3],
    )


def solution(mesh):
    placed = (
        P("dp", "head", None),
        P("dp", "head", None),
        P("dp", "head", None, None),
        P("dp", "head", None),
        P("head", None, None),
        P(None, "head"),
        P(None, "head"),
        P(None, "head"),
        P(None, "head"),
        P("head"),
        P("head", None),
        P(),
        P(),
        P(),
        P(),
        P(),
        P(),
        P(),
    )
    return jax.shard_map(
        per_device,
        mesh=mesh,
        in_specs=placed,
        out_specs=(
            P("dp", "head", None),
            P("dp", "head", None),
            P(),
            P(None, "head"),
            P(None, "head"),
            P(None, "head"),
            P(None, "head"),
            P("head"),
            P("head", None),
            P(),
            P(),
            P(),
            P(),
            P(),
            P(),
            P(),
        ),
        check_vma=False,
    )
```

```python
import functools
import math

import jax
import jax.numpy as jnp
import numpy as np
from jax import lax
from jax.experimental import pallas as pl
from jax.experimental.pallas import tpu as pltpu
from jax.sharding import PartitionSpec as P

CH = 256
HD = 64
NF = 128
FW = 2 * NF
SR = 80
GR = 16
TILE = 512

penalty_weight = 32.0
target_gate = 0.9
LOG2E = 1.4426950408889634
SIN_POLY = (
    3.1415925800446116,
    -5.16770687892007,
    2.5500313771889287,
    -0.5980451736320438,
    0.07722012807955428,
)
COS_POLY = (
    0.9999999534665498,
    -4.934792858660313,
    4.058411913867723,
    -1.3318801593312537,
    0.2196967947670672,
)
GELU_A = 0.7978845608028654
GELU_B = 0.044715

f32 = jnp.float32
bf16 = jnp.bfloat16


def dot(a, b):
    return lax.dot_general(a, b, (((1,), (0,)), ((), ())), preferred_element_type=f32)


def dot_nt(a, b):
    return lax.dot_general(a, b, (((1,), (1,)), ((), ())), preferred_element_type=f32)


def dot_tn(a, b):
    return lax.dot_general(a, b, (((0,), (0,)), ((), ())), preferred_element_type=f32)


def split2(x):
    high = x.astype(bf16)
    return high, (x - high.astype(f32)).astype(bf16)


def split2_cat(x):
    return jnp.concatenate(split2(x), 1)


def split3_cat(x):
    high = x.astype(bf16)
    rest = x - high.astype(f32)
    mid = rest.astype(bf16)
    return jnp.concatenate([high, mid, (rest - mid.astype(f32)).astype(bf16)], 1)


def low_lanes(rows):
    return lax.broadcasted_iota(jnp.int32, (rows, 128), 1) < HD


def unit(u, ones2):
    inverse = lax.rsqrt(dot(split2_cat(u * u), ones2) + 1e-06)
    return u * inverse, inverse


def sin_cos(n, maps):
    high, rest = split2(n)
    turns = dot(jnp.concatenate([high, rest, high], 1), maps)
    r = turns - jnp.round(turns)
    u = r * r
    scale = math.sqrt(2.0 / math.sqrt(NF))
    s = SIN_POLY[4] * scale
    c = COS_POLY[4] * scale
    for i in (3, 2, 1, 0):
        s = s * u + SIN_POLY[i] * scale
        c = c * u + COS_POLY[i] * scale
    s = s * r
    return s * c, 1.0 / math.sqrt(NF) - s * s


def pair_features(n, maps):
    sine, cosine = sin_cos(n, maps)
    return [
        jnp.concatenate(
            [sine[:, NF * i : NF * i + NF], cosine[:, NF * i : NF * i + NF]], 1
        ).astype(bf16)
        for i in range(2)
    ]


def feature_back(units, angle_grads, maps_ref, ones2):
    splits = [split2(angle_grad) for angle_grad in angle_grads]
    dns = [
        dot(jnp.concatenate([high, rest, high], 1), maps_ref[pair])
        for pair, (high, rest) in enumerate(splits)
    ]
    radials = [dot(split2_cat(n * dn), ones2) for (n, _), dn in zip(units, dns)]
    return [
        (dn - n * radial) * inverse for (n, inverse), dn, radial in zip(units, dns, radials)
    ]


def angle_gradient(dphi, phi):
    dphi = dphi.astype(bf16).astype(f32)
    phi = phi.astype(f32)
    return dphi[:, :NF] * phi[:, NF:] - dphi[:, NF:] * phi[:, :NF]


def both_augmented(values, low):
    one = jnp.ones_like(values)
    return jnp.where(low, values, one), jnp.where(low, one, values)


def expand(block, odd):
    state, norm = block[:HD], block[HD:SR]
    parts = [norm] * (HD // (SR - HD))
    return jnp.concatenate(parts + [state] if odd else [state] + parts, 0)


def shrink(block, odd):
    if odd:
        return jnp.concatenate([block[HD:], block[HD - (SR - HD) : HD]], 0)
    return block[:SR]


def clear(refs):
    for ref in refs:
        ref[...] = jnp.zeros_like(ref)


def collect(held, parts, index):
    for k, part in enumerate(parts):
        held[index ^ k] = part[...]


def block_pair(even, odd):
    none = jnp.zeros_like(even)
    return jnp.concatenate(
        [jnp.concatenate([even, none], 1), jnp.concatenate([none, odd], 1)], 0
    )


def keys_setup(held, here, wkv_ref, wvt, maps_ref, back_ref, gw_ref, gb):
    size = held.shape[0]
    width = wkv_ref.shape[0]
    inner = wvt.shape[0]
    at = width * here
    high, rest, gates, biases = [], [], [], []
    for d in range(size):
        if here == 2:
            lanes = slice(128 * d, 128 * d + 128)
            wkv_ref[:, lanes] = held[d, :width]
            wkv_ref[:, inner + 128 * d : inner + 128 * d + 128] = held[d, width : 2 * width]
            wvt[lanes, :] = held[d, width : 2 * width].T
        elif d % 2:
            lanes = slice(64 * d - 64, 64 * d + 64)
            one, two = held[d - 1, :width], held[d, :width]
            wkv_ref[:, lanes] = jnp.concatenate([one[:, :HD], two[:, :HD]], 1)
            values = jnp.concatenate([one[:, HD:], two[:, HD:]], 1)
            wkv_ref[:, inner + 64 * d - 64 : inner + 64 * d + 64] = values
            wvt[lanes, :] = values.T
        for i in range(here):
            first = at + HD * i
            high.append(held[d, first : first + HD])
            rest.append(held[d, first + HD * here : first + HD * here + HD])
        tail = held[d, at + 2 * HD * here :].astype(f32)
        for i in range(here):
            gates.append(
                jnp.concatenate([tail[4 * i + j : 4 * i + j + 1] for j in range(width // 128)], 1)
            )
            bias = sum(tail[4 * here + j : 4 * here + j + 1, i : i + 1] for j in range(3))
            biases.append(jnp.broadcast_to(bias, (1, CH)))
    for pair in range(len(high) // 2):
        top = block_pair(high[2 * pair], high[2 * pair + 1])
        low = block_pair(rest[2 * pair], rest[2 * pair + 1])
        maps_ref[pair] = jnp.concatenate([top, top, low], 0)
        back = ((top.astype(f32) + low.astype(f32)) * (2.0 * math.pi)).T
        top, low = split2(back)
        back_ref[pair] = jnp.concatenate([top, top, low], 0)
    heads = len(gates)
    gw_ref[...] = jnp.concatenate(gates + [jnp.zeros((GR - heads, width), f32)], 0).astype(bf16)
    gb[...] = jnp.concatenate(biases + [jnp.zeros((GR - heads, CH), f32)], 0)


def keys_body(*refs, size, here, skipped):
    if size:
        parts, index_ref, refs = refs[:size], refs[size], refs[size + 1 :]
        held, refs = refs[-1], refs[:-1]
        wkv_ref, maps_ref, back_ref, gw_ref, wvt_ref, gb_ref = refs[-7:-1]
        refs = refs[:-7] + refs[-1:]
    else:
        wkv_ref, maps_ref, gw_ref, wvt_ref, gb_ref = refs[:5]
        refs = refs[5:]
    refs = refs[:3] + refs[3 + skipped :]
    (
        x_ref,
        ones_ref,
        tri_ref,
        phik_ref,
        v_ref,
        row_ref,
        col_ref,
        u_ref,
        end_ref,
        tot_ref,
        gsum_ref,
        tick_ref,
        acc,
    ) = refs
    tick_ref[...] = jnp.zeros_like(tick_ref)
    b, c = pl.program_id(0), pl.program_id(1)

    if size:

        @pl.when(jnp.logical_and(b == 0, c == 0))
        def _():
            collect(held, parts, index_ref[0])
            keys_setup(held, here, wkv_ref, wvt_ref, maps_ref, back_ref, gw_ref, gb_ref)

    x = x_ref[...]
    kv = dot(x, wkv_ref[...])
    width = kv.shape[1] // 2
    keys = kv[:, :width]
    v_ref[...] = kv[:, width:].astype(bf16)
    vt = dot_nt(wvt_ref[...], x).astype(bf16)
    pre = dot_nt(gw_ref[...], x) + gb_ref[...]
    soft = jnp.log1p(jnp.exp(-jnp.abs(pre)))
    log_gate = -(jnp.maximum(-pre, 0.0) + soft)
    log_keep = -(jnp.maximum(pre, 0.0) + soft)
    gate = jnp.exp(log_gate)
    keep = jnp.exp(log_keep)
    cumul = dot(split3_cat(log_gate * LOG2E), tri_ref[...])
    shifted = cumul - log_keep * LOG2E
    total = cumul[:, CH - 1 : CH]
    tail = jnp.exp2(total - shifted)
    row_ref[...] = jnp.concatenate([cumul, shifted, gate, keep], 0)
    stack = jnp.concatenate(
        [cumul, shifted, tail, gate, jnp.exp2(cumul), keep, keep, keep], 0
    )
    col_ref[...] = stack.T

    @pl.when(jnp.logical_and(b == 0, c == 0))
    def _():
        gsum_ref[...] = jnp.zeros_like(gsum_ref)

    gsum_ref[...] += gate

    @pl.when(c == 0)
    def _():
        acc[...] = jnp.zeros_like(acc)
        tot_ref[0] = jnp.zeros_like(tot_ref[0])

    tot_ref[0] += jnp.broadcast_to(total, tot_ref.shape[1:])
    ones2 = ones_ref[...]
    block_ones = jnp.ones((SR - HD, CH), f32)
    pairs = width // 128
    units = [unit(keys[:, 128 * pair : 128 * pair + 128], ones2) for pair in range(pairs)]
    phis = []

    def update(h):
        weighted = jnp.concatenate([vt[HD * h : HD * h + HD].astype(f32), block_ones], 0)
        weighted = (weighted * tail[h : h + 1]).astype(bf16)
        own = dot(weighted, phis[h])
        u_ref[0, 0, h] = own
        acc[h] = jnp.exp2(total[h : h + 1]) * acc[h] + own

    for pair in range(pairs):
        phis += pair_features(units[pair][0], maps_ref[pair])
        for h in (2 * pair, 2 * pair + 1):
            phik_ref[:, FW * h : FW * h + FW] = phis[h]
            if pair:
                update(h - 2)
    for h in (2 * pairs - 2, 2 * pairs - 1):
        update(h)

    @pl.when(c == pl.num_programs(1) - 1)
    def _():
        end_ref[0] = acc[...].astype(bf16)


def lower_mask(flip):
    rows = lax.broadcasted_iota(jnp.int32, (CH, CH), 0)
    columns = lax.broadcasted_iota(jnp.int32, (CH, CH), 1)
    return rows <= columns if flip else rows >= columns


def queries_setup(held, here, wq_ref, mix_ref):
    size = held.shape[0]
    width = wq_ref.shape[0]
    for d in range(size):
        at = width * here // 2
        rows = HD * here
        if here == 2:
            wq_ref[:, 128 * d : 128 * d + 128] = held[d, :width]
        elif d % 2:
            one, two = held[d - 1, :at], held[d, :at]
            lanes = slice(64 * d - 64, 64 * d + 64)
            wq_ref[:at, lanes] = jnp.concatenate([one[:, :HD], two[:, :HD]], 1)
            wq_ref[at:, lanes] = jnp.concatenate([one[:, HD:], two[:, HD:]], 1)
        for j in range(width // 128):
            mix_ref[rows * d : rows * d + rows, 128 * j : 128 * j + 128] = held[
                d, at + rows * j : at + rows * j + rows
            ]


def queries_body(*refs, size, here, skipped):
    parts, refs = refs[:size], refs[size:]
    if size:
        index_ref, refs = refs[0], refs[1:]
        held, refs = refs[-1], refs[:-1]
        wq_ref, mix_ref = refs[-2:]
        refs = refs[:-2]

        @pl.when(jnp.logical_and(pl.program_id(0) == 0, pl.program_id(1) == 0))
        def _():
            collect(held, parts, index_ref[0])
            queries_setup(held, here, wq_ref, mix_ref)

    else:
        wq_ref, refs = refs[0], refs[1:]
    x_ref, maps_ref, ones_ref, phik_ref, v_ref, row_ref, col_ref = refs[:7]
    phiq_ref, intra_ref, *ticks = refs[7 + skipped :]
    clear(ticks)
    query = dot(x_ref[...], wq_ref[...])
    width = query.shape[1]
    ones2 = ones_ref[...]
    lower = lower_mask(False)
    low = low_lanes(CH)
    pairs = width // 128
    units = [unit(query[:, 128 * pair : 128 * pair + 128], ones2) for pair in range(pairs)]

    def scores_of(pair, phis):
        heads = (2 * pair, 2 * pair + 1)
        augmented = both_augmented(v_ref[:, 128 * pair : 128 * pair + 128], low)
        raws = [dot_nt(phi, phik_ref[:, FW * h : FW * h + FW]) for phi, h in zip(phis, heads)]
        decays = [
            jnp.exp2(
                jnp.where(
                    lower,
                    col_ref[:, h : h + 1] - row_ref[GR + h : GR + h + 1, :],
                    -jnp.inf,
                )
            )
            for h in heads
        ]
        scores = [(raw * decay).astype(bf16) for raw, decay in zip(raws, decays)]
        for i, h in enumerate(heads):
            intra_ref[:, 128 * h : 128 * h + 128] = dot(scores[i], augmented[i]).astype(bf16)

    before = None
    for pair in range(pairs):
        phis = pair_features(units[pair][0], maps_ref[pair])
        for i, phi in enumerate(phis):
            h = 2 * pair + i
            phiq_ref[:, FW * h : FW * h + FW] = phi
        if before is not None:
            scores_of(pair - 1, before)
        before = phis
    scores_of(pairs - 1, before)


def tokens_body(
    start_refs,
    index_ref,
    x_ref,
    c_ref,
    phiq_ref,
    intra_ref,
    row_ref,
    col_ref,
    u_ref,
    mix_ref,
    up_ref,
    down_ref,
    vec_ref,
    upb_ref,
    ones_ref,
    select_ref,
    *refs,
    chunks,
    size,
):
    (
    out_ref,
    dr_ref,
    dn_ref,
    qside_ref,
    states_ref,
    vloc_ref,
    sent_ref,
    keep_ref,
    send_ref,
    vec_acc,
    state,
    heads_low,
    numer_all,
    inner_all,
    up_acc,
    down_acc,
    mix_acc,
    ) = refs
    b = pl.program_id(0)
    heads = state.shape[0]
    pairs = heads // 2

    @pl.when(b == 0)
    def _():
        mix_acc[...] = jnp.zeros_like(mix_acc)
        vec_acc[...] = jnp.zeros_like(vec_acc)
        up_acc[...] = jnp.zeros_like(up_acc)
        down_acc[...] = jnp.zeros_like(down_acc)

    low = low_lanes(CH)
    arrived = sum(start_ref[0].astype(f32) for start_ref in start_refs[size:])
    here = heads // size
    for d in range(size):
        part = slice(here * d, here * d + here)
        state[part] = start_refs[d][0].astype(f32) + arrived[part]
    for c in range(chunks):
        rows = slice(CH * c, CH * c + CH)
        for pair in range(pairs):
            both = (2 * pair, 2 * pair + 1)
            held = [state[h].astype(bf16) for h in both]
            carries = [
                dot_nt(phiq_ref[rows, FW * h : FW * h + FW], expand(held[i], i))
                for i, h in enumerate(both)
            ]
            for i, h in enumerate(both):
                states_ref[0, c, h] = held[i]
                last = jnp.exp2(row_ref[c, h : h + 1, CH - 1 : CH])
                state[h] = last * state[h] + u_ref[0, c, h]
            both = [
                intra_ref[rows, 128 * h : 128 * h + 128]
                + col_ref[rows, 4 * GR + h : 4 * GR + h + 1] * carry
                for h, carry in zip(both, carries)
            ]
            lanes = slice(128 * pair, 128 * pair + 128)
            numer = jnp.where(low, both[0], both[1])
            inner = pltpu.roll(jnp.where(low, both[1], both[0]), HD, 1)
            numer_all[rows, lanes] = numer
            inner_all[rows, lanes] = inner
            heads_low[rows, lanes] = (numer * lax.rsqrt(inner * inner + 1.0)).astype(bf16)
    for h in range(heads):
        states_ref[0, chunks, h] = state[h].astype(bf16)

    mix = mix_ref[...]
    rest = heads_low[...]
    mixing_bias, gain, shift, down_bias = (vec_ref[i : i + 1, :] for i in range(4))
    residual = x_ref[...].astype(f32) + dot(rest, mix) + mixing_bias
    center = residual - jnp.mean(residual, -1, keepdims=True)
    scale = lax.rsqrt(jnp.mean(center * center, -1, keepdims=True) + 1e-05)
    normal = center * scale
    normal_low = (normal * gain + shift).astype(bf16)
    normal_t = normal_low.T
    upstream = c_ref[...]
    upstream_t = upstream.T
    result = residual + down_bias
    grad_normal = jnp.zeros_like(residual)
    for j in range(up_ref.shape[1] // TILE):
        part = slice(TILE * j, TILE * j + TILE)
        up = up_ref[:, part]
        down = down_ref[part, :]
        hidden = dot(normal_low, up) + upb_ref[:, part]
        square = hidden * hidden
        th = jnp.tanh(hidden * (GELU_A + (GELU_A * GELU_B) * square))
        half = 0.5 + 0.5 * th
        active = (hidden * half).astype(bf16)
        slope = half + hidden * (0.5 - 0.5 * th * th) * (
            GELU_A + (3.0 * GELU_A * GELU_B) * square
        )
        result += dot(active, down)
        grad_hidden = slope * dot_nt(upstream, down)
        grad_hidden = grad_hidden.astype(bf16)
        vec_acc[4 + j : 5 + j, :] += jnp.sum(grad_hidden.astype(f32), 0, keepdims=True)
        grad_normal += dot_nt(grad_hidden, up)
        up_acc[:, part] += dot(normal_t, grad_hidden)
        down_acc[:, part] += dot(upstream_t, active)
    out_ref[...] = result.astype(bf16)
    upstream = upstream.astype(f32)
    dn = grad_normal * gain
    grad_residual = upstream + scale * (
        dn
        - jnp.mean(dn, -1, keepdims=True)
        - normal * jnp.mean(dn * normal, -1, keepdims=True)
    )
    dr_ref[...] = grad_residual
    for i, value in enumerate((grad_residual, grad_normal * normal, grad_normal, upstream)):
        vec_acc[i : i + 1, :] += jnp.sum(value, 0, keepdims=True)
    grad_low = grad_residual.astype(bf16)
    mix_acc[...] += dot_tn(rest, grad_low)
    grad_heads = dot_nt(grad_low, mix)

    ones2 = ones_ref[...]
    following = [None] * heads
    for c in reversed(range(chunks)):
        rows = slice(CH * c, CH * c + CH)
        grad_numers, squares, query_sides = [], [], []
        for pair in range(pairs):
            lanes = slice(128 * pair, 128 * pair + 128)
            inner = inner_all[rows, lanes]
            squares.append(1.0 / (inner * inner + 1.0))
            grad_numers.append(grad_heads[rows, lanes] * lax.rsqrt(inner * inner + 1.0))
            query_sides.append(
                dot(split2_cat(grad_numers[pair] * numer_all[rows, lanes]), ones2)
            )
        query_sides = [side * square for side, square in zip(query_sides, squares)]
        for pair in range(pairs):
            inner = inner_all[rows, 128 * pair : 128 * pair + 128]
            grad_inner = pltpu.roll(query_sides[pair] * inner * (-1.0 / HD), HD, 1)
            low_part = jnp.where(low, grad_numers[pair], grad_inner)
            high_part = jnp.where(low, grad_inner, grad_numers[pair])
            sent = []
            for h, together in ((2 * pair, low_part), (2 * pair + 1, high_part)):
                dn_ref[rows, 128 * h : 128 * h + 128] = together.astype(bf16)
                carried = col_ref[rows, 4 * GR + h : 4 * GR + h + 1]
                sent.append((carried * together).T.astype(bf16))
            for i, h in enumerate((2 * pair, 2 * pair + 1)):
                own = shrink(dot(sent[i], phiq_ref[rows, FW * h : FW * h + FW]), i)
                vloc_ref[0, c, h] = own
                if following[h] is not None:
                    last = jnp.exp2(row_ref[c, h : h + 1, CH - 1 : CH])
                    own = own + last * following[h]
                following[h] = own
        qside_ref[rows, :] = dot(
            split2_cat(jnp.concatenate(query_sides, 1)), select_ref[...]
        )
    for h in range(heads):
        sent_ref[0, h] = following[h].astype(bf16)

    @pl.when(b == pl.num_programs(0) - 1)
    def _():
        width, ff = up_acc.shape
        up_rows, down_rows, mix_rows = width // size, ff // size, mix_acc.shape[0] // size
        group = size // 2
        slab = keep_ref.shape[0] // group

        def write(ref, d):
            at = d % group * slab
            for j in range(ff // TILE):
                ref[at : at + up_rows, :] = up_acc[
                    up_rows * d : up_rows * d + up_rows, TILE * j : TILE * j + TILE
                ].astype(bf16)
                at += up_rows
            ref[at : at + down_rows, :] = (
                down_acc[:, down_rows * d : down_rows * d + down_rows].T.astype(bf16)
            )
            at += down_rows
            ref[at : at + mix_rows, :] = mix_acc[
                mix_rows * d : mix_rows * d + mix_rows, :
            ].astype(bf16)

        for d in range(size):
            kept = index_ref[0] % 2 == d // group

            @pl.when(kept)
            def _(d=d):
                write(keep_ref, d)

            @pl.when(jnp.logical_not(kept))
            def _(d=d):
                write(send_ref, d)


def query_back_body(
    x_ref,
    wq_ref,
    maps_back_ref,
    ones_ref,
    phiq_ref,
    phik_ref,
    v_ref,
    dn_ref,
    row_ref,
    col_ref,
    states_ref,
    *refs,
):
    dq_ref, dphik_ref, dv_ref, wqg_ref, *ticks = refs[-7:]
    clear(ticks)
    first = jnp.logical_and(pl.program_id(0) == 0, pl.program_id(1) == 0)

    @pl.when(first)
    def _():
        wqg_ref[...] = jnp.zeros_like(wqg_ref)

    x = x_ref[...]
    query = dot(x, wq_ref[...])
    width = query.shape[1]
    ones2 = ones_ref[...]
    mask = lower_mask(True)
    low = low_lanes(CH)
    pairs = width // 128
    units = [unit(query[:, 128 * pair : 128 * pair + 128], ones2) for pair in range(pairs)]
    angle_grads = []
    for pair in range(pairs):
        heads = (2 * pair, 2 * pair + 1)
        augmented = both_augmented(v_ref[:, 128 * pair : 128 * pair + 128], low)
        phiqs = [phiq_ref[:, FW * h : FW * h + FW] for h in heads]
        phiks = [phik_ref[:, FW * h : FW * h + FW] for h in heads]
        grads = [dn_ref[:, 128 * h : 128 * h + 128] for h in heads]
        raws = [dot_nt(phik, phiq) for phik, phiq in zip(phiks, phiqs)]
        raw_grads = [dot_nt(values, grad) for values, grad in zip(augmented, grads)]
        decays = [
            jnp.exp2(
                jnp.where(
                    mask,
                    row_ref[h : h + 1, :] - col_ref[:, GR + h : GR + h + 1],
                    -jnp.inf,
                )
            )
            for h in heads
        ]
        scores = [(raw * decay).astype(bf16) for raw, decay in zip(raws, decays)]
        raw_grads = [(grad * decay).astype(bf16) for grad, decay in zip(raw_grads, decays)]
        for i, h in enumerate(heads):
            dv_ref[:, 128 * h : 128 * h + 128] = dot(scores[i], grads[i]).astype(bf16)
        for i, h in enumerate(heads):
            dphik_ref[:, FW * h : FW * h + FW] = dot(raw_grads[i], phiqs[i]).astype(bf16)
        dphis = [
            dot_tn(raw_grads[i], phiks[i])
            + col_ref[:, 4 * GR + h : 4 * GR + h + 1]
            * dot(grads[i], expand(states_ref[0, 0, h], i))
            for i, h in enumerate(heads)
        ]
        angle_grads.append(
            jnp.concatenate([angle_gradient(dphi, phi) for dphi, phi in zip(dphis, phiqs)], 1)
        )
    for pair, dq in enumerate(feature_back(units, angle_grads, maps_back_ref, ones2)):
        dq_ref[:, 128 * pair : 128 * pair + 128] = dq.astype(bf16)
    wqg_ref[...] += dot_tn(x, dq_ref[...])


def key_back_body(
    end_refs,
    x_ref,
    wq_ref,
    wkv_ref,
    maps_back_ref,
    gw_ref,
    ones_ref,
    all_ref,
    tri_ref,
    phik_ref,
    v_ref,
    dq_ref,
    dphik_ref,
    dv_ref,
    qside_ref,
    row_ref,
    col_ref,
    states_ref,
    vloc_ref,
    dr_ref,
    factor_ref,
    *refs,
):
    dx_ref, wkvg_ref, gwg_ref, gbg_ref, *ticks, grads, state_grad, sides = refs[-10:]
    clear(ticks)
    first = jnp.logical_and(pl.program_id(0) == 0, pl.program_id(1) == 0)

    @pl.when(first)
    def _():
        wkvg_ref[...] = jnp.zeros_like(wkvg_ref)
        gwg_ref[...] = jnp.zeros_like(gwg_ref)
        gbg_ref[...] = jnp.zeros_like(gbg_ref)

    @pl.when(pl.program_id(1) == 0)
    def _():
        state_grad[...] = sum(end_ref[0].astype(f32) for end_ref in end_refs)

    x = x_ref[...]
    heads = state_grad.shape[0]
    keys = dot(x, wkv_ref[:, : wq_ref.shape[1]])
    width = wq_ref.shape[1]
    ones2 = ones_ref[...]
    low = low_lanes(CH)
    weigh = jnp.where(lax.broadcasted_iota(jnp.int32, (SR, FW), 0) < HD, 1.0, 4.0)
    bounds = []
    units = [unit(keys[:, 128 * pair : 128 * pair + 128], ones2) for pair in range(heads // 2)]
    angle_grads = []
    for pair in range(heads // 2):
        lanes = slice(128 * pair, 128 * pair + 128)
        both = (2 * pair, 2 * pair + 1)
        augmented = both_augmented(v_ref[:, lanes], low)
        phiks = [phik_ref[:, FW * h : FW * h + FW] for h in both]
        tails = [col_ref[:, 2 * GR + h : 2 * GR + h + 1] for h in both]
        spreads = [expand(state_grad[h].astype(bf16), i) for i, h in enumerate(both)]
        dvs = [dot_nt(phik, spread) for phik, spread in zip(phiks, spreads)]
        dphis = [dot(values, spread) for values, spread in zip(augmented, spreads)]
        dvs = [
            dv_ref[:, 128 * h : 128 * h + 128] + tails[i] * dvs[i] for i, h in enumerate(both)
        ]
        for i, h in enumerate(both):
            sides[:, 128 * h : 128 * h + 128] = dvs[i] * augmented[i].astype(f32)
        angle_grads.append(
            jnp.concatenate(
                [
                    angle_gradient(
                        dphik_ref[:, FW * h : FW * h + FW].astype(f32) + tails[i] * dphis[i],
                        phiks[i],
                    )
                    for i, h in enumerate(both)
                ],
                1,
            )
        )
        grads[:, width + 128 * pair : width + 128 * pair + 128] = jnp.where(
            low, dvs[0], dvs[1]
        ).astype(bf16)
        for h in both:
            grad_end = state_grad[h]
            bounds.append(
                jnp.sum(grad_end * weigh * states_ref[0, 0, h].astype(f32), 0, keepdims=True)
            )
            last = jnp.exp2(row_ref[h : h + 1, CH - 1 : CH])
            state_grad[h] = last * grad_end + vloc_ref[0, 0, h]
    for pair, dk in enumerate(feature_back(units, angle_grads, maps_back_ref, ones2)):
        grads[:, 128 * pair : 128 * pair + 128] = dk.astype(bf16)
    key_side = dot(split2_cat(sides[...]), all_ref[...])
    key_row = key_side.T[:GR]
    differ = qside_ref[...].T[:GR] - key_row
    bound = jnp.sum(jnp.concatenate(bounds, 0), 1, keepdims=True)
    bound = jnp.concatenate([bound, jnp.zeros((GR - heads, 1), f32)], 0)
    grad_log = dot(split3_cat(differ), tri_ref[...]) + bound
    gate, keep = row_ref[2 * GR : 3 * GR, :], row_ref[3 * GR : 4 * GR, :]
    grad_pre = (
        grad_log * keep - gate * key_row + factor_ref[...] * gate * keep
    ).astype(bf16)
    gbg_ref[...] += grad_pre.astype(f32)
    gwg_ref[...] += dot(grad_pre, x)
    together = grads[...]
    wkvg_ref[...] += dot_tn(x, together)
    dx_ref[...] = (
        dr_ref[...]
        + dot_nt(dq_ref[...], wq_ref[...])
        + dot_nt(together, wkv_ref[...])
        + dot_tn(grad_pre, gw_ref[...])
    )


def unpack_body(index_ref, every_ref, _, up_ref, down_ref, mix_ref, tick_ref, *, places):
    rows, ff = up_ref.shape
    width = down_ref.shape[1]
    depth = every_ref.shape[1]
    slab = depth * every_ref.shape[0] // pl.num_programs(0)
    tick_ref[...] = jnp.zeros_like(tick_ref)

    def copy(first, count, ref, lanes):
        done = 0
        while done < count:
            piece, at = divmod(first + done, depth)
            number = min(count - done, depth - at)
            ref[done : done + number, lanes] = every_ref[
                places[piece], at : at + number, :
            ].astype(f32)
            done += number

    for d in range(pl.num_programs(0)):

        @pl.when(pl.program_id(0) == d)
        def _(d=d):
            first = slab * d
            for j in range(ff // TILE):
                copy(first, rows, up_ref, slice(TILE * j, TILE * j + TILE))
                first += rows
            copy(first, down_ref.shape[0], down_ref, slice(0, width))
            first += down_ref.shape[0]

            @pl.when(index_ref[0] == d)
            def _():
                copy(first, mix_ref.shape[0], mix_ref, slice(0, width))


def pack_body(key_ref, value_ref, query_ref, mix_ref, maps_ref, tail_ref, first_ref, second_ref):
    width, own = key_ref.shape
    if own == 128:
        first_ref[:width] = key_ref[...]
        first_ref[width : 2 * width] = value_ref[...]
        second_ref[:width] = query_ref[...]
        at, then = 2 * width, width
    else:
        half = width // 2
        first_ref[:width] = jnp.concatenate([key_ref[...], value_ref[...]], 1)
        second_ref[:half] = jnp.concatenate([query_ref[:half], query_ref[half:]], 1)
        at, then = width, half
    high, rest = split2(maps_ref[...] * (0.5 / math.pi))
    first_ref[at : at + own] = high
    first_ref[at + own : at + 2 * own] = rest
    first_ref[at + 2 * own :] = tail_ref[...]
    for j in range(width // 128):
        second_ref[then + own * j : then + own * j + own] = mix_ref[:, 128 * j : 128 * j + 128]


def group_body(*refs, queries, keys, order):
    query_refs, refs = refs[:queries], refs[queries:]
    key_refs, refs = refs[:keys], refs[keys:]
    gate_refs, refs = refs[:keys], refs[keys:]
    bias_refs, (vector_ref, index_ref, keep_ref, send_ref) = refs[:keys], refs[keys:]
    width = query_refs[0].shape[0]
    half, rows_all, own = keep_ref.shape
    inner = query_refs[0].shape[1]
    here = own // HD
    cuts = width // own

    def total(parts, lanes):
        value = parts[0][:, lanes]
        for part in parts[1:]:
            value = value + part[:, lanes]
        return value

    every = slice(None)
    gates = total(gate_refs, every)
    biases = jnp.sum(total(bias_refs, every), 1, keepdims=True)
    vectors = vector_ref[...]
    vectors = jnp.concatenate(
        [vectors[r : r + 1, own * j : own * j + own] for r in range(8) for j in range(cuts)], 0
    )
    at = 3 * width + GR
    used = at + 8 * cuts
    lane = lax.broadcasted_iota(jnp.int32, (1, own), 1)

    def write(out_ref, d, place):
        lanes = slice(own * d, own * d + own)
        out_ref[place, :width] = total(query_refs, lanes).astype(bf16)
        out_ref[place, width : 2 * width] = total(key_refs, lanes).astype(bf16)
        lanes = slice(inner + own * d, inner + own * d + own)
        out_ref[place, 2 * width : 3 * width] = total(key_refs, lanes).astype(bf16)
        rows = [
            gates[h : h + 1, own * j : own * j + own]
            for h in range(here * d, here * d + here)
            for j in range(cuts)
        ]
        bias = jnp.zeros((1, own), f32)
        for i in range(here):
            bias = jnp.where(lane == i, biases[here * d + i : here * d + i + 1], bias)
        rows += [bias, jnp.zeros((GR - 1 - here * cuts, own), f32)]
        out_ref[place, 3 * width : at] = jnp.concatenate(rows, 0).astype(bf16)
        out_ref[place, at:used] = vectors.astype(bf16)
        if used < rows_all:
            out_ref[place, used:] = jnp.zeros((rows_all - used, own), bf16)

    for d, place in enumerate(order):
        kept = index_ref[0] % 2 == place // half

        @pl.when(kept)
        def _(d=d, place=place):
            write(keep_ref, d, place % half)

        @pl.when(jnp.logical_not(kept))
        def _(d=d, place=place):
            write(send_ref, d, place % half)


def tokens_entry(*refs, starts, **named):
    tokens_body(refs[:starts], *refs[starts:], **named)


def key_back_entry(*refs, arrivals):
    key_back_body(refs[:arrivals], *refs[arrivals:])


def whole(array):
    zeros = (0,) * len(array.shape)
    return pl.BlockSpec(array.shape, lambda *_: zeros, pipeline_mode=pl.Buffered(1))


def fixed(shape):
    zeros = (0,) * len(shape)
    return pl.BlockSpec(shape, lambda *_: zeros)


def call(body, grid, ins, outs, previous=(), after=(), scratch=(), name=None, flops=0, room=48):
    extra = list(previous) + list(after)
    specs = [spec for _, spec in ins] + [pl.BlockSpec(memory_space=pl.ANY)] * len(extra)
    return pl.pallas_call(
        body,
        grid=grid,
        in_specs=specs,
        out_specs=[spec for _, _, spec in outs],
        out_shape=[jax.ShapeDtypeStruct(shape, kind) for shape, kind, _ in outs],
        scratch_shapes=list(scratch),
        input_output_aliases={len(ins) + i: i for i in range(len(previous))},
        compiler_params=pltpu.CompilerParams(
            dimension_semantics=("arbitrary",) * len(grid), vmem_limit_bytes=room * 1024 * 1024
        ),
        cost_estimate=pl.CostEstimate(flops=flops, bytes_accessed=4 << 20, transcendentals=0),
        name=name,
    )(*[array for array, _ in ins], *extra)


def swap(x, axis, bit):
    size = lax.axis_size(axis)
    return lax.ppermute(x, axis, [(i, i ^ bit) for i in range(size)])


def spread_head(part):
    parts = [part]
    for k in range(1, lax.axis_size("head")):
        parts.append(swap(parts[k - 1], "head", 1) if k % 2 else swap(part, "head", k))
    return parts


def place_in(axis, bit, number):
    return (lax.axis_index(axis) // bit) % number


class HalvingSum:
    def __init__(self, array):
        self.terms = [(array, 0)]
        self.length = array.shape[0]

    @classmethod
    def begun(cls, keep, send):
        sums = cls(keep)
        sums.terms.append((swap(send, "head", 1), 0))
        return sums

    def part(self, offset, tick=0.0):
        total = tick
        for array, start in self.terms:
            piece = lax.dynamic_slice_in_dim(array, start + offset, self.length, 0)
            total = total + piece.astype(f32)
        return total.astype(bf16)

    def step(self, axis, bit, number=2, tick=0.0):
        self.length //= number
        mine = place_in(axis, bit, number)
        sends = [self.part((mine ^ k) * self.length, tick) for k in range(1, number)]
        self.terms = [(array, start + mine * self.length) for array, start in self.terms]
        for k, send in enumerate(sends):
            self.terms.append((swap(send, axis, (k + 1) * bit), 0))
        return sends


def open_join(array, axis, bit, number):
    return [array] + [swap(array, axis, k * bit) for k in range(1, number)]


def close_join(parts, axis, bit):
    number = len(parts)
    mine = place_in(axis, bit, number).astype(jnp.int32)
    if number == 2:
        own, other = parts
        return jnp.where(
            mine == 0, jnp.concatenate([own, other], 0), jnp.concatenate([other, own], 0)
        )
    return jnp.concatenate(
        [
            lax.select_n(mine, *[parts[j ^ place] for place in range(number)])
            if number <= 4
            else jnp.take(jnp.stack(parts), mine ^ j, axis=0)
            for j in range(number)
        ],
        0,
    )


def gather_all(piece, stages):
    every = lax.all_gather(piece, ("dp", "head"), axis=0, tiled=False)
    names = [
        (axis, 1 << i)
        for axis in ("dp", "head")
        for i in reversed(range(lax.axis_size(axis).bit_length() - 1))
    ]
    places = np.arange(1 << len(names)).reshape((2,) * len(names))
    singles = []
    for axis, bit, number in stages:
        while number > 1:
            number //= 2
            singles.append((axis, bit * number))
    places = places.transpose([names.index(single) for single in singles]).reshape(-1)
    if piece.shape[0] % GR:
        every = every[places].reshape(1, -1, piece.shape[1])
        places = places[:1] * 0
    return every, tuple(int(place) for place in places)


def high_rest(x):
    high = lax.reduce_precision(x, 8, 7)
    return high, x - high


def per_device(
    tokens,
    cotangent,
    carry_state,
    carry_norm,
    random_maps,
    query_weight,
    key_weight,
    value_weight,
    gate_weight,
    gate_bias,
    mixing_weight,
    mixing_bias,
    norm_gain,
    norm_bias,
    up_weight,
    up_bias,
    down_weight,
    down_bias,
):
    seqs, length, width = tokens.shape
    here = gate_weight.shape[1]
    size = lax.axis_size("head")
    replicas = lax.axis_size("dp")
    index = lax.axis_index("head")
    heads = here * size
    chunks = length // CH
    blocks = seqs * chunks
    count = seqs * length
    inner_width = heads * HD
    own = here * HD
    ff = up_weight.shape[1]
    pairs = heads // 2
    head_bits = [1 << i for i in range(size.bit_length() - 1)]
    stages = (
        [("head", 1, 2), ("dp", 1, min(2, replicas))]
        + [("head", bit, 2) for bit in head_bits[1:]]
        + [("dp", 2, replicas // 2)]
    )
    index_array = index.astype(jnp.int32).reshape(1)
    smem = pl.BlockSpec(memory_space=pltpu.SMEM)

    bias_high, bias_rest = high_rest(gate_bias)
    bias_mid, bias_rest = high_rest(bias_rest)
    biases = jnp.pad(jnp.stack([bias_high, bias_mid, bias_rest]), ((0, 0), (0, 128 - here)))
    tail = jnp.concatenate([gate_weight.T.reshape(-1, 128).astype(f32), biases])
    tail = jnp.pad(tail, ((0, GR - tail.shape[0]), (0, 0)))
    tail = tail.astype(bf16)
    packing = (key_weight, value_weight, query_weight, mixing_weight, random_maps.reshape(own, NF), tail)
    first_rows = (width * here + 2 * own + GR, 128)
    second_rows = (width * here, 128)
    first_part, second_part = call(
        pack_body,
        (1,),
        [(array, fixed(array.shape)) for array in packing],
        [(first_rows, bf16, fixed(first_rows)), (second_rows, bf16, fixed(second_rows))],
        name="pack",
        room=62,
        flops=1_000_000,
    )
    first_parts = spread_head(first_part)

    begin = jnp.concatenate(
        [
            carry_state.transpose(0, 1, 3, 2),
            jnp.broadcast_to(carry_norm[:, :, None, :], (seqs, here, SR - HD, FW)),
        ],
        2,
    ).astype(bf16)

    half = np.arange(128) // HD
    ones2 = np.tile((half[:, None] == half[None, :]).astype(np.float32), (2, 1))
    ones2 = jnp.asarray(ones2, bf16)
    place = np.arange(CH)
    upto = jnp.asarray(np.tile((place[:, None] <= place[None, :]).astype(np.float32), (3, 1)), bf16)
    onward = jnp.asarray(np.tile((place[:, None] >= place[None, :]).astype(np.float32), (3, 1)), bf16)
    lane = np.arange(128)
    one_lane = np.zeros((inner_width, 128), np.float32)
    one_lane[np.arange(heads) * HD, np.arange(heads)] = 1.0
    select = jnp.asarray(np.tile(one_lane, (2, 1)), bf16)
    all_lanes = (np.arange(heads * 128) // 128)[:, None] == lane[None, :]
    all_lanes = jnp.asarray(np.tile(all_lanes.astype(np.float32), (2, 1)), bf16)

    x = tokens.reshape(count, width)
    c = cotangent.reshape(count, width)
    state_shape = (heads, SR, FW)
    tick_outs = [((1, lanes), f32, fixed((1, lanes))) for lanes in (128, FW, width)]

    def rows_of(columns, base=0, reverse=False):
        def at(b, t):
            return ((base + b) * chunks + (chunks - 1 - t if reverse else t), 0)

        return pl.BlockSpec((CH, columns), at)

    def row_spec(base=0, reverse=False):
        return pl.BlockSpec((4 * GR, CH), rows_of(0, base, reverse).index_map)

    def per_block(shape, base=0, offset=0, reverse=False):
        zeros = (0,) * len(shape)

        def at(b, t):
            return (base + b, offset + (chunks - 1 - t if reverse else t)) + zeros

        return pl.BlockSpec((1, 1) + shape, at)

    def per_seq(base=0):
        return pl.BlockSpec((1,) + state_shape, lambda b, t: (base + b, 0, 0, 0))

    weights = [
        ((width, 2 * inner_width), bf16),
        ((pairs, 3 * 128, FW), bf16),
        ((pairs, 3 * FW, 128), bf16),
        ((GR, width), bf16),
        ((inner_width, width), bf16),
        ((GR, CH), f32),
    ]
    weights = [(shape, kind, fixed(shape)) for shape, kind in weights]

    def keys_ins(base):
        return [(x, rows_of(width, base)), (ones2, whole(ones2)), (upto, whole(upto))]

    def keys_outs(base):
        total_spec = pl.BlockSpec((1, GR, 128), lambda b, t: (base + b, 0, 0))
        return [
            ((count, heads * FW), bf16, rows_of(heads * FW, base)),
            ((count, inner_width), bf16, rows_of(inner_width, base)),
            ((blocks * 4 * GR, CH), f32, row_spec(base)),
            ((count, 128), f32, rows_of(128, base)),
            ((seqs, chunks) + state_shape, f32, per_block(state_shape, base)),
            ((seqs,) + state_shape, bf16, per_seq(base)),
            ((seqs, GR, 128), f32, total_spec),
            ((GR, CH), f32, fixed((GR, CH))),
            ((1, FW), f32, fixed((1, FW))),
        ]

    *previous, gate_sums, tick, wkv, maps_front, maps_back, gw, wvt, gb = call(
        functools.partial(keys_body, size=size, here=here, skipped=2),
        (2, chunks),
        [(part, whole(part)) for part in first_parts] + [(index_array, smem)] + keys_ins(0),
        keys_outs(0) + weights,
        after=[second_part, begin],
        scratch=[
            pltpu.VMEM(state_shape, f32),
            pltpu.VMEM((size,) + first_part.shape, bf16),
        ],
        name="keys",
        flops=10_000_000_000,
    )
    second_parts = [second_part] + [swap(second_part, "head", k) for k in range(1, size)]
    begins = [jnp.where(index == 0, begin, jnp.zeros_like(begin))] + [
        lax.ppermute(begin, "head", [(k, 0)]) for k in range(1, size)
    ]
    phik, v, row, col, update, end, total, more_sums, tick = call(
        functools.partial(keys_body, size=0, here=here, skipped=2 * size - 2 + len(previous)),
        (seqs - 2, chunks),
        [(part, whole(part)) for part in (wkv, maps_front, gw, wvt, gb)] + keys_ins(2),
        keys_outs(2),
        previous=previous,
        after=second_parts[1:] + begins[1:],
        scratch=[pltpu.VMEM(state_shape, f32)],
        name="keys",
        flops=10_000_000_000,
    )
    gate_sums = lax.all_gather(
        jnp.concatenate([gate_sums, more_sums]), ("dp", "head"), axis=0, tiled=True
    )
    last = jnp.exp2(total[:, :heads, 0])[:, :, None, None]
    begin = jnp.concatenate(begins, 1)

    sent = (end.astype(f32) + last * begin.astype(f32)).astype(bf16)
    starts = []
    ticks = (0.0, 0.0, 0.0)
    phiq = intra = wq = mix = None
    previous = ()
    for step, (base, number) in enumerate(((0, 1), (1, 2), (3, 1))):
        arrived = None
        if step < size - 1:
            arrived = lax.ppermute(sent, "head", [(step, step + 1)])
            starts.append(arrived)
        main = [
            (x, rows_of(width, base)),
            (maps_front, whole(maps_front)),
            (ones2, whole(ones2)),
            (phik, rows_of(heads * FW, base)),
            (v, rows_of(inner_width, base)),
            (row, row_spec(base)),
            (col, rows_of(128, base)),
        ]
        outs = [
            ((count, heads * FW), bf16, rows_of(heads * FW, base)),
            ((count, heads * 128), bf16, rows_of(heads * 128, base)),
        ] + tick_outs
        if step == 0:
            phiq, intra, *ticks, wq, mix = call(
                functools.partial(queries_body, size=size, here=here, skipped=1),
                (number, chunks),
                [(part, whole(part)) for part in second_parts] + [(index_array, smem)] + main,
                outs
                + [
                    ((width, inner_width), bf16, fixed((width, inner_width))),
                    ((inner_width, width), bf16, fixed((inner_width, width))),
                ],
                after=[sent],
                scratch=[pltpu.VMEM((size,) + second_part.shape, bf16)],
                name="queries",
                flops=5_000_000_000,
            )
        else:
            phiq, intra, *ticks = call(
                functools.partial(queries_body, size=0, here=here, skipped=3),
                (number, chunks),
                [(wq, whole(wq))] + main,
                outs,
                previous=[phiq, intra],
                after=[sent],
                name="queries",
                flops=5_000_000_000 * number,
            )
        if step < size - 2:
            sent = (last * arrived.astype(f32) + end.astype(f32) + ticks[1][0]).astype(bf16)
    for step in range(3, size - 1):
        arrived = lax.ppermute(sent, "head", [(step, step + 1)])
        starts.append(arrived)
        sent = (last * arrived.astype(f32) + end.astype(f32)).astype(bf16)

    vectors = jnp.stack([mixing_bias, norm_gain, norm_bias, down_bias] * 2)

    def seq_rows(columns):
        return pl.BlockSpec((length, columns), lambda b: (b, 0))

    def seq_block(*shape):
        zeros = (0,) * len(shape)
        return pl.BlockSpec((1,) + shape, lambda b: (b,) + zeros)

    up_bias2 = up_bias.reshape(1, ff)
    slab = (width // size) * (ff // TILE) + ff // size + own
    layer_out, dr, dn, qside, states, vloc, vdev, keep, send, vector_grads = call(
        functools.partial(
            tokens_entry, starts=len(begins) + len(starts), chunks=chunks, size=size
        ),
        (seqs,),
        [(start, seq_block(*start.shape[1:])) for start in begins + starts]
        + [
            (index_array, smem),
            (x, seq_rows(width)),
            (c, seq_rows(width)),
            (phiq, seq_rows(heads * FW)),
            (intra, seq_rows(heads * 128)),
            (
                row.reshape(blocks, 4 * GR, CH),
                pl.BlockSpec((chunks, 4 * GR, CH), lambda b: (b, 0, 0)),
            ),
            (col, seq_rows(128)),
            (update, seq_block(chunks, *state_shape)),
            (mix, whole(mix)),
            (up_weight, whole(up_weight)),
            (down_weight, whole(down_weight)),
            (vectors, whole(vectors)),
            (up_bias2, whole(up_bias2)),
            (ones2, whole(ones2)),
            (select, whole(select)),
        ],
        [
            ((count, width), bf16, seq_rows(width)),
            ((count, width), f32, seq_rows(width)),
            ((count, heads * 128), bf16, seq_rows(heads * 128)),
            ((count, 128), f32, seq_rows(128)),
            ((seqs, chunks + 1) + state_shape, bf16, seq_block(chunks + 1, *state_shape)),
            ((seqs, chunks) + state_shape, f32, seq_block(chunks, *state_shape)),
            ((seqs,) + state_shape, bf16, seq_block(*state_shape)),
            ((size // 2 * slab, width), bf16, fixed((size // 2 * slab, width))),
            ((size // 2 * slab, width), bf16, fixed((size // 2 * slab, width))),
            ((8, width), f32, fixed((8, width))),
        ],
        scratch=[
            pltpu.VMEM(state_shape, f32),
            pltpu.VMEM((length, inner_width), bf16),
            pltpu.VMEM((length, inner_width), f32),
            pltpu.VMEM((length, inner_width), f32),
            pltpu.VMEM((width, ff), f32),
            pltpu.VMEM((width, ff), f32),
            pltpu.VMEM((inner_width, width), f32),
        ],
        name="tokens",
        room=62,
        flops=50_000_000_000,
    )

    sent = vdev
    waiting = list(stages)
    sums = HalvingSum.begun(keep, send)
    ticks = (0.0, [0.0], 0.0)
    finishes = []
    dq = dphik = dv = None
    previous = []
    query_grads = []
    for step, (base, number) in enumerate(((0, 1), (1, 2), (3, 1))):
        stage = waiting.pop(0)
        after = sums.step(*stage, ticks[2]) if step else [send]
        if step < size - 1:
            arrived = lax.ppermute(sent, "head", [(size - 1 - step, size - 2 - step)])
            finishes.append(arrived)
            after.append(sent)
        dq, dphik, dv, query_grad, *ticks = call(
            query_back_body,
            (number, chunks),
            [
                (x, rows_of(width, base)),
                (wq, whole(wq)),
                (maps_back, whole(maps_back)),
                (ones2, whole(ones2)),
                (phiq, rows_of(heads * FW, base)),
                (phik, rows_of(heads * FW, base)),
                (v, rows_of(inner_width, base)),
                (dn, rows_of(heads * 128, base)),
                (row, row_spec(base)),
                (col, rows_of(128, base)),
                (states, per_block(state_shape, base)),
            ],
            [
                ((count, inner_width), bf16, rows_of(inner_width, base)),
                ((count, heads * FW), bf16, rows_of(heads * FW, base)),
                ((count, heads * 128), bf16, rows_of(heads * 128, base)),
                ((width, inner_width), f32, fixed((width, inner_width))),
            ] + tick_outs,
            previous=previous,
            after=after,
            name="query_back",
            room=48 if step else 60,
            flops=8_000_000_000 * number,
        )
        previous = [dq, dphik, dv]
        query_grads.append(query_grad)
        if step < size - 2:
            sent = (last * arrived.astype(f32) + vdev.astype(f32) + ticks[1][0]).astype(bf16)
    for step in range(3, size - 1):
        arrived = lax.ppermute(sent, "head", [(size - 1 - step, size - 2 - step)])
        finishes.append(arrived)
        sent = (last * arrived.astype(f32) + vdev.astype(f32)).astype(bf16)

    gate_total = jnp.sum(gate_sums.reshape(-1, GR, CH)[:, :heads] + ticks[1][0])
    gate_count = replicas * heads * size * count
    mean_gate = gate_total / gate_count
    factor = 2.0 * penalty_weight * (mean_gate - target_gate) / heads
    factor = jnp.broadcast_to(factor, (1, CH))

    tokens_grad = None
    previous = []
    key_value_grads, gate_grads, gate_bias_grads = [], [], []
    for base, number in ((0, 2), (2, 2)):
        after = []
        if base == 0:
            while waiting:
                after = sums.step(*waiting.pop(0), ticks[2])
        else:
            piece = sums.part(0, ticks[2])
            after = [piece]
            every, places = gather_all(piece, stages)
        tokens_grad, key_value_grad, gate_grad, gate_bias_grad, *ticks = call(
            functools.partial(key_back_entry, arrivals=len(finishes)),
            (number, chunks),
            [(finish, per_seq(base)) for finish in finishes]
            + [
                (x, rows_of(width, base, True)),
                (wq, whole(wq)),
                (wkv, whole(wkv)),
                (maps_back, whole(maps_back)),
                (gw, whole(gw)),
                (ones2, whole(ones2)),
                (all_lanes, whole(all_lanes)),
                (onward, whole(onward)),
                (phik, rows_of(heads * FW, base, True)),
                (v, rows_of(inner_width, base, True)),
                (dq, rows_of(inner_width, base, True)),
                (dphik, rows_of(heads * FW, base, True)),
                (dv, rows_of(heads * 128, base, True)),
                (qside, rows_of(128, base, True)),
                (row, row_spec(base, True)),
                (col, rows_of(128, base, True)),
                (states, per_block(state_shape, base, 1, True)),
                (vloc, per_block(state_shape, base, 0, True)),
                (dr, rows_of(width, base, True)),
                (factor, whole(factor)),
            ],
            [
                ((count, width), f32, rows_of(width, base, True)),
                ((width, 2 * inner_width), f32, fixed((width, 2 * inner_width))),
                ((GR, width), f32, fixed((GR, width))),
                ((GR, CH), f32, fixed((GR, CH))),
            ] + tick_outs,
            previous=previous,
            after=after,
            scratch=[
                pltpu.VMEM((CH, 2 * inner_width), bf16),
                pltpu.VMEM(state_shape, f32),
                pltpu.VMEM((CH, heads * 128), f32),
            ],
            name="key_back",
            room=58,
            flops=8_000_000_000 * number,
        )
        previous = [tokens_grad]
        key_value_grads.append(key_value_grad)
        gate_grads.append(gate_grad)
        gate_bias_grads.append(gate_bias_grad)
    rows = 3 * width + GR + 8 * width // own
    rows += -rows % replicas
    order = [
        sum(((d >> i) & 1) << (len(head_bits) - 1 - i) for i in range(len(head_bits)))
        for d in range(size)
    ]
    parts = query_grads + key_value_grads + gate_grads + gate_bias_grads + [vector_grads]
    group = call(
        functools.partial(
            group_body, queries=len(query_grads), keys=len(key_value_grads), order=order
        ),
        (1,),
        [(part, fixed(part.shape)) for part in parts] + [(index_array, smem)],
        [((size // 2, rows, own), bf16, fixed((size // 2, rows, own)))] * 2,
        name="group",
        room=62,
        flops=1_000_000,
    )
    group_sums = HalvingSum.begun(*[half.reshape(-1, own) for half in group])
    for bit in head_bits[1:]:
        group_sums.step("head", bit)
    across = [stage for stage in stages if stage[0] == "dp"]
    for stage in across:
        group_sums.step(*stage)
    group = group_sums.part(0)
    for axis, bit, number in reversed(across[1:]):
        group = close_join(open_join(group, axis, bit, number), axis, bit)
    group, other = open_join(group, *across[0])
    up_grad, down_grad, mixing_grad, tick = call(
        functools.partial(unpack_body, places=places),
        (size,),
        [(index_array, smem), (every, whole(every))],
        [
            ((width, ff), f32, pl.BlockSpec((width // size, ff), lambda d: (d, 0))),
            ((ff, width), f32, pl.BlockSpec((ff // size, width), lambda d: (d, 0))),
            ((own, width), f32, fixed((own, width))),
            ((1, own), f32, fixed((1, own))),
        ],
        after=[group],
        name="unpack",
        flops=1_000_000_000,
    )
    group = close_join([group + tick.astype(bf16), other], *across[0][:2])
    group = group.astype(f32)
    gate_rows = here * width // own
    gate_grad = group[3 * width : 3 * width + gate_rows].reshape(here, width).T
    at = 3 * width + GR
    vector_grads = group[at : at + 8 * width // own].reshape(8, width)
    penalty = penalty_weight * (mean_gate - target_gate) * (mean_gate - target_gate)
    return (
        layer_out.reshape(seqs, length, width),
        tokens_grad.reshape(seqs, length, width),
        penalty,
        group[:width],
        group[width : 2 * width],
        group[2 * width : 3 * width],
        gate_grad,
        group[3 * width + gate_rows, :here],
        mixing_grad,
        vector_grads[0],
        vector_grads[1],
        vector_grads[2],
        up_grad,
        vector_grads[4:].reshape(ff),
        down_grad,
        vector_grads[3],
    )


def solution(mesh):
    placed = (
        P("dp", "head", None),
        P("dp", "head", None),
        P("dp", "head", None, None),
        P("dp", "head", None),
        P("head", None, None),
        P(None, "head"),
        P(None, "head"),
        P(None, "head"),
        P(None, "head"),
        P("head"),
        P("head", None),
        P(),
        P(),
        P(),
        P(),
        P(),
        P(),
        P(),
    )
    return jax.shard_map(
        per_device,
        mesh=mesh,
        in_specs=placed,
        out_specs=(
            P("dp", "head", None),
            P("dp", "head", None),
            P(),
            P(None, "head"),
            P(None, "head"),
            P(None, "head"),
            P(None, "head"),
            P("head"),
            P("head", None),
            P(),
            P(),
            P(),
            P(),
            P(),
            P(),
            P(),
        ),
        check_vma=False,
    )
```

```python
import functools
import math

import jax
import jax.numpy as jnp
import numpy as np
from jax import lax
from jax.experimental import pallas as pl
from jax.experimental.pallas import tpu as pltpu
from jax.sharding import PartitionSpec as P

CH = 256
HD = 64
NF = 128
FW = 2 * NF
SR = 80
GR = 16
TILE = 512

penalty_weight = 32.0
target_gate = 0.9
LOG2E = 1.4426950408889634
SIN_POLY = (
    3.1415925800446116,
    -5.16770687892007,
    2.5500313771889287,
    -0.5980451736320438,
    0.07722012807955428,
)
COS_POLY = (
    0.9999999534665498,
    -4.934792858660313,
    4.058411913867723,
    -1.3318801593312537,
    0.2196967947670672,
)
GELU_A = 0.7978845608028654
GELU_B = 0.044715

f32 = jnp.float32
bf16 = jnp.bfloat16


def dot(a, b):
    return lax.dot_general(a, b, (((1,), (0,)), ((), ())), preferred_element_type=f32)


def dot_nt(a, b):
    return lax.dot_general(a, b, (((1,), (1,)), ((), ())), preferred_element_type=f32)


def dot_tn(a, b):
    return lax.dot_general(a, b, (((0,), (0,)), ((), ())), preferred_element_type=f32)


def split2(x):
    high = x.astype(bf16)
    return high, (x - high.astype(f32)).astype(bf16)


def split2_cat(x):
    return jnp.concatenate(split2(x), 1)


def split3_cat(x):
    high = x.astype(bf16)
    rest = x - high.astype(f32)
    mid = rest.astype(bf16)
    return jnp.concatenate([high, mid, (rest - mid.astype(f32)).astype(bf16)], 1)


def low_lanes(rows):
    return lax.broadcasted_iota(jnp.int32, (rows, 128), 1) < HD


def unit(u, ones2):
    inverse = lax.rsqrt(dot(split2_cat(u * u), ones2) + 1e-06)
    return u * inverse, inverse


def sin_cos(n, maps):
    high, rest = split2(n)
    turns = dot(jnp.concatenate([high, rest, high], 1), maps)
    r = turns - jnp.round(turns)
    u = r * r
    scale = math.sqrt(2.0 / math.sqrt(NF))
    s = SIN_POLY[4] * scale
    c = COS_POLY[4] * scale
    for i in (3, 2, 1, 0):
        s = s * u + SIN_POLY[i] * scale
        c = c * u + COS_POLY[i] * scale
    s = s * r
    return s * c, 1.0 / math.sqrt(NF) - s * s


def pair_features(n, maps):
    sine, cosine = sin_cos(n, maps)
    return [
        jnp.concatenate(
            [sine[:, NF * i : NF * i + NF], cosine[:, NF * i : NF * i + NF]], 1
        ).astype(bf16)
        for i in range(2)
    ]


def feature_back(units, angle_grads, maps_ref, ones2):
    splits = [split2(angle_grad) for angle_grad in angle_grads]
    dns = [
        dot(jnp.concatenate([high, rest, high], 1), maps_ref[pair])
        for pair, (high, rest) in enumerate(splits)
    ]
    radials = [dot(split2_cat(n * dn), ones2) for (n, _), dn in zip(units, dns)]
    return [
        (dn - n * radial) * inverse for (n, inverse), dn, radial in zip(units, dns, radials)
    ]


def angle_gradient(dphi, phi):
    dphi = dphi.astype(bf16).astype(f32)
    phi = phi.astype(f32)
    return dphi[:, :NF] * phi[:, NF:] - dphi[:, NF:] * phi[:, :NF]


def both_augmented(values, low):
    one = jnp.ones_like(values)
    return jnp.where(low, values, one), jnp.where(low, one, values)


def expand(block, odd):
    state, norm = block[:HD], block[HD:SR]
    parts = [norm] * (HD // (SR - HD))
    return jnp.concatenate(parts + [state] if odd else [state] + parts, 0)


def shrink(block, odd):
    if odd:
        return jnp.concatenate([block[HD:], block[HD - (SR - HD) : HD]], 0)
    return block[:SR]


def clear(refs):
    for ref in refs:
        ref[...] = jnp.zeros_like(ref)


def collect(held, parts, index):
    for k, part in enumerate(parts):
        held[index ^ k] = part[...]


def block_pair(even, odd):
    none = jnp.zeros_like(even)
    return jnp.concatenate(
        [jnp.concatenate([even, none], 1), jnp.concatenate([none, odd], 1)], 0
    )


def keys_setup(held, here, wkv_ref, wvt, maps_ref, back_ref, gw_ref, gb):
    size = held.shape[0]
    width = wkv_ref.shape[0]
    inner = wvt.shape[0]
    at = width * here
    high, rest, gates, biases = [], [], [], []
    for d in range(size):
        if here == 2:
            lanes = slice(128 * d, 128 * d + 128)
            wkv_ref[:, lanes] = held[d, :width]
            wkv_ref[:, inner + 128 * d : inner + 128 * d + 128] = held[d, width : 2 * width]
            wvt[lanes, :] = held[d, width : 2 * width].T
        elif d % 2:
            lanes = slice(64 * d - 64, 64 * d + 64)
            one, two = held[d - 1, :width], held[d, :width]
            wkv_ref[:, lanes] = jnp.concatenate([one[:, :HD], two[:, :HD]], 1)
            values = jnp.concatenate([one[:, HD:], two[:, HD:]], 1)
            wkv_ref[:, inner + 64 * d - 64 : inner + 64 * d + 64] = values
            wvt[lanes, :] = values.T
        for i in range(here):
            first = at + HD * i
            high.append(held[d, first : first + HD])
            rest.append(held[d, first + HD * here : first + HD * here + HD])
        tail = held[d, at + 2 * HD * here :].astype(f32)
        for i in range(here):
            gates.append(
                jnp.concatenate([tail[4 * i + j : 4 * i + j + 1] for j in range(width // 128)], 1)
            )
            bias = sum(tail[4 * here + j : 4 * here + j + 1, i : i + 1] for j in range(3))
            biases.append(jnp.broadcast_to(bias, (1, CH)))
    for pair in range(len(high) // 2):
        top = block_pair(high[2 * pair], high[2 * pair + 1])
        low = block_pair(rest[2 * pair], rest[2 * pair + 1])
        maps_ref[pair] = jnp.concatenate([top, top, low], 0)
        back = ((top.astype(f32) + low.astype(f32)) * (2.0 * math.pi)).T
        top, low = split2(back)
        back_ref[pair] = jnp.concatenate([top, top, low], 0)
    heads = len(gates)
    gw_ref[...] = jnp.concatenate(gates + [jnp.zeros((GR - heads, width), f32)], 0).astype(bf16)
    gb[...] = jnp.concatenate(biases + [jnp.zeros((GR - heads, CH), f32)], 0)


def keys_body(*refs, size, here, skipped):
    if size:
        parts, index_ref, refs = refs[:size], refs[size], refs[size + 1 :]
        held, refs = refs[-1], refs[:-1]
        wkv_ref, maps_ref, back_ref, gw_ref, wvt_ref, gb_ref = refs[-7:-1]
        refs = refs[:-7] + refs[-1:]
    else:
        wkv_ref, maps_ref, gw_ref, wvt_ref, gb_ref = refs[:5]
        refs = refs[5:]
    refs = refs[:3] + refs[3 + skipped :]
    (
        x_ref,
        ones_ref,
        tri_ref,
        phik_ref,
        v_ref,
        row_ref,
        col_ref,
        u_ref,
        end_ref,
        tot_ref,
        gsum_ref,
        tick_ref,
        acc,
    ) = refs
    tick_ref[...] = jnp.zeros_like(tick_ref)
    b, c = pl.program_id(0), pl.program_id(1)

    if size:

        @pl.when(jnp.logical_and(b == 0, c == 0))
        def _():
            collect(held, parts, index_ref[0])
            keys_setup(held, here, wkv_ref, wvt_ref, maps_ref, back_ref, gw_ref, gb_ref)

    x = x_ref[...]
    kv = dot(x, wkv_ref[...])
    width = kv.shape[1] // 2
    keys = kv[:, :width]
    v_ref[...] = kv[:, width:].astype(bf16)
    vt = dot_nt(wvt_ref[...], x).astype(bf16)
    pre = dot_nt(gw_ref[...], x) + gb_ref[...]
    soft = jnp.log1p(jnp.exp(-jnp.abs(pre)))
    log_gate = -(jnp.maximum(-pre, 0.0) + soft)
    log_keep = -(jnp.maximum(pre, 0.0) + soft)
    gate = jnp.exp(log_gate)
    keep = jnp.exp(log_keep)
    cumul = dot(split3_cat(log_gate * LOG2E), tri_ref[...])
    shifted = cumul - log_keep * LOG2E
    total = cumul[:, CH - 1 : CH]
    tail = jnp.exp2(total - shifted)
    row_ref[...] = jnp.concatenate([cumul, shifted, gate, keep], 0)
    stack = jnp.concatenate(
        [cumul, shifted, tail, gate, jnp.exp2(cumul), keep, keep, keep], 0
    )
    col_ref[...] = stack.T

    @pl.when(jnp.logical_and(b == 0, c == 0))
    def _():
        gsum_ref[...] = jnp.zeros_like(gsum_ref)

    gsum_ref[...] += gate

    @pl.when(c == 0)
    def _():
        acc[...] = jnp.zeros_like(acc)
        tot_ref[0] = jnp.zeros_like(tot_ref[0])

    tot_ref[0] += jnp.broadcast_to(total, tot_ref.shape[1:])
    ones2 = ones_ref[...]
    block_ones = jnp.ones((SR - HD, CH), f32)
    pairs = width // 128
    units = [unit(keys[:, 128 * pair : 128 * pair + 128], ones2) for pair in range(pairs)]
    phis = []

    def update(h):
        weighted = jnp.concatenate([vt[HD * h : HD * h + HD].astype(f32), block_ones], 0)
        weighted = (weighted * tail[h : h + 1]).astype(bf16)
        own = dot(weighted, phis[h])
        u_ref[0, 0, h] = own
        acc[h] = jnp.exp2(total[h : h + 1]) * acc[h] + own

    for pair in range(pairs):
        phis += pair_features(units[pair][0], maps_ref[pair])
        for h in (2 * pair, 2 * pair + 1):
            phik_ref[:, FW * h : FW * h + FW] = phis[h]
            if pair:
                update(h - 2)
    for h in (2 * pairs - 2, 2 * pairs - 1):
        update(h)

    @pl.when(c == pl.num_programs(1) - 1)
    def _():
        end_ref[0] = acc[...].astype(bf16)


def lower_mask(flip):
    rows = lax.broadcasted_iota(jnp.int32, (CH, CH), 0)
    columns = lax.broadcasted_iota(jnp.int32, (CH, CH), 1)
    return rows <= columns if flip else rows >= columns


def queries_setup(held, here, wq_ref, mix_ref):
    size = held.shape[0]
    width = wq_ref.shape[0]
    for d in range(size):
        at = width * here // 2
        rows = HD * here
        if here == 2:
            wq_ref[:, 128 * d : 128 * d + 128] = held[d, :width]
        elif d % 2:
            one, two = held[d - 1, :at], held[d, :at]
            lanes = slice(64 * d - 64, 64 * d + 64)
            wq_ref[:at, lanes] = jnp.concatenate([one[:, :HD], two[:, :HD]], 1)
            wq_ref[at:, lanes] = jnp.concatenate([one[:, HD:], two[:, HD:]], 1)
        for j in range(width // 128):
            mix_ref[rows * d : rows * d + rows, 128 * j : 128 * j + 128] = held[
                d, at + rows * j : at + rows * j + rows
            ]


def queries_body(*refs, size, here, skipped):
    parts, refs = refs[:size], refs[size:]
    if size:
        index_ref, refs = refs[0], refs[1:]
        held, refs = refs[-1], refs[:-1]
        wq_ref, mix_ref = refs[-2:]
        refs = refs[:-2]

        @pl.when(jnp.logical_and(pl.program_id(0) == 0, pl.program_id(1) == 0))
        def _():
            collect(held, parts, index_ref[0])
            queries_setup(held, here, wq_ref, mix_ref)

    else:
        wq_ref, refs = refs[0], refs[1:]
    x_ref, maps_ref, ones_ref, phik_ref, v_ref, row_ref, col_ref = refs[:7]
    phiq_ref, intra_ref, *ticks = refs[7 + skipped :]
    clear(ticks)
    query = dot(x_ref[...], wq_ref[...])
    width = query.shape[1]
    ones2 = ones_ref[...]
    lower = lower_mask(False)
    low = low_lanes(CH)
    pairs = width // 128
    units = [unit(query[:, 128 * pair : 128 * pair + 128], ones2) for pair in range(pairs)]

    def scores_of(pair, phis):
        heads = (2 * pair, 2 * pair + 1)
        augmented = both_augmented(v_ref[:, 128 * pair : 128 * pair + 128], low)
        raws = [dot_nt(phi, phik_ref[:, FW * h : FW * h + FW]) for phi, h in zip(phis, heads)]
        decays = [
            jnp.exp2(
                jnp.where(
                    lower,
                    col_ref[:, h : h + 1] - row_ref[GR + h : GR + h + 1, :],
                    -jnp.inf,
                )
            )
            for h in heads
        ]
        scores = [(raw * decay).astype(bf16) for raw, decay in zip(raws, decays)]
        for i, h in enumerate(heads):
            intra_ref[:, 128 * h : 128 * h + 128] = dot(scores[i], augmented[i])

    before = None
    for pair in range(pairs):
        phis = pair_features(units[pair][0], maps_ref[pair])
        for i, phi in enumerate(phis):
            h = 2 * pair + i
            phiq_ref[:, FW * h : FW * h + FW] = phi
        if before is not None:
            scores_of(pair - 1, before)
        before = phis
    scores_of(pairs - 1, before)


def tokens_body(
    start_refs,
    index_ref,
    x_ref,
    c_ref,
    phiq_ref,
    intra_ref,
    row_ref,
    col_ref,
    u_ref,
    mix_ref,
    up_ref,
    down_ref,
    vec_ref,
    upb_ref,
    ones_ref,
    select_ref,
    *refs,
    chunks,
    size,
):
    (
    out_ref,
    dr_ref,
    dn_ref,
    qside_ref,
    states_ref,
    vloc_ref,
    sent_ref,
    keep_ref,
    send_ref,
    vec_acc,
    state,
    heads_low,
    numer_all,
    inner_all,
    up_acc,
    down_acc,
    mix_acc,
    ) = refs
    b = pl.program_id(0)
    heads = state.shape[0]
    pairs = heads // 2

    @pl.when(b == 0)
    def _():
        mix_acc[...] = jnp.zeros_like(mix_acc)
        vec_acc[...] = jnp.zeros_like(vec_acc)
        up_acc[...] = jnp.zeros_like(up_acc)
        down_acc[...] = jnp.zeros_like(down_acc)

    low = low_lanes(CH)
    arrived = sum(start_ref[0].astype(f32) for start_ref in start_refs[size:])
    here = heads // size
    for d in range(size):
        part = slice(here * d, here * d + here)
        state[part] = start_refs[d][0].astype(f32) + arrived[part]
    for c in range(chunks):
        rows = slice(CH * c, CH * c + CH)
        for pair in range(pairs):
            both = (2 * pair, 2 * pair + 1)
            held = [state[h].astype(bf16) for h in both]
            carries = [
                dot_nt(phiq_ref[rows, FW * h : FW * h + FW], expand(held[i], i))
                for i, h in enumerate(both)
            ]
            for i, h in enumerate(both):
                states_ref[0, c, h] = held[i]
                last = jnp.exp2(row_ref[c, h : h + 1, CH - 1 : CH])
                state[h] = last * state[h] + u_ref[0, c, h]
            both = [
                intra_ref[rows, 128 * h : 128 * h + 128]
                + col_ref[rows, 4 * GR + h : 4 * GR + h + 1] * carry
                for h, carry in zip(both, carries)
            ]
            lanes = slice(128 * pair, 128 * pair + 128)
            numer = jnp.where(low, both[0], both[1])
            inner = pltpu.roll(jnp.where(low, both[1], both[0]), HD, 1)
            numer_all[rows, lanes] = numer
            inner_all[rows, lanes] = inner
            heads_low[rows, lanes] = (numer * lax.rsqrt(inner * inner + 1.0)).astype(bf16)
    for h in range(heads):
        states_ref[0, chunks, h] = state[h].astype(bf16)

    mix = mix_ref[...]
    rest = heads_low[...]
    mixing_bias, gain, shift, down_bias = (vec_ref[i : i + 1, :] for i in range(4))
    residual = x_ref[...].astype(f32) + dot(rest, mix) + mixing_bias
    center = residual - jnp.mean(residual, -1, keepdims=True)
    scale = lax.rsqrt(jnp.mean(center * center, -1, keepdims=True) + 1e-05)
    normal = center * scale
    normal_low = (normal * gain + shift).astype(bf16)
    normal_t = normal_low.T
    upstream = c_ref[...]
    upstream_t = upstream.T
    result = residual + down_bias
    grad_normal = jnp.zeros_like(residual)
    for j in range(up_ref.shape[1] // TILE):
        part = slice(TILE * j, TILE * j + TILE)
        up = up_ref[:, part]
        down = down_ref[part, :]
        hidden = dot(normal_low, up) + upb_ref[:, part]
        square = hidden * hidden
        th = jnp.tanh(hidden * (GELU_A + (GELU_A * GELU_B) * square))
        half = 0.5 + 0.5 * th
        active = (hidden * half).astype(bf16)
        slope = half + hidden * (0.5 - 0.5 * th * th) * (
            GELU_A + (3.0 * GELU_A * GELU_B) * square
        )
        result += dot(active, down)
        grad_hidden = slope * dot_nt(upstream, down)
        grad_hidden = grad_hidden.astype(bf16)
        vec_acc[4 + j : 5 + j, :] += jnp.sum(grad_hidden.astype(f32), 0, keepdims=True)
        grad_normal += dot_nt(grad_hidden, up)
        up_acc[:, part] += dot(normal_t, grad_hidden)
        down_acc[:, part] += dot(upstream_t, active)
    out_ref[...] = result.astype(bf16)
    upstream = upstream.astype(f32)
    dn = grad_normal * gain
    grad_residual = upstream + scale * (
        dn
        - jnp.mean(dn, -1, keepdims=True)
        - normal * jnp.mean(dn * normal, -1, keepdims=True)
    )
    dr_ref[...] = grad_residual
    for i, value in enumerate((grad_residual, grad_normal * normal, grad_normal, upstream)):
        vec_acc[i : i + 1, :] += jnp.sum(value, 0, keepdims=True)
    grad_low = grad_residual.astype(bf16)
    mix_acc[...] += dot_tn(rest, grad_low)
    grad_heads = dot_nt(grad_low, mix)

    ones2 = ones_ref[...]
    following = [None] * heads
    for c in reversed(range(chunks)):
        rows = slice(CH * c, CH * c + CH)
        grad_numers, squares, query_sides = [], [], []
        for pair in range(pairs):
            lanes = slice(128 * pair, 128 * pair + 128)
            inner = inner_all[rows, lanes]
            squares.append(1.0 / (inner * inner + 1.0))
            grad_numers.append(grad_heads[rows, lanes] * lax.rsqrt(inner * inner + 1.0))
            query_sides.append(
                dot(split2_cat(grad_numers[pair] * numer_all[rows, lanes]), ones2)
            )
        query_sides = [side * square for side, square in zip(query_sides, squares)]
        for pair in range(pairs):
            inner = inner_all[rows, 128 * pair : 128 * pair + 128]
            grad_inner = pltpu.roll(query_sides[pair] * inner * (-1.0 / HD), HD, 1)
            low_part = jnp.where(low, grad_numers[pair], grad_inner)
            high_part = jnp.where(low, grad_inner, grad_numers[pair])
            sent = []
            for h, together in ((2 * pair, low_part), (2 * pair + 1, high_part)):
                dn_ref[rows, 128 * h : 128 * h + 128] = together.astype(bf16)
                carried = col_ref[rows, 4 * GR + h : 4 * GR + h + 1]
                sent.append((carried * together).T.astype(bf16))
            for i, h in enumerate((2 * pair, 2 * pair + 1)):
                own = shrink(dot(sent[i], phiq_ref[rows, FW * h : FW * h + FW]), i)
                vloc_ref[0, c, h] = own
                if following[h] is not None:
                    last = jnp.exp2(row_ref[c, h : h + 1, CH - 1 : CH])
                    own = own + last * following[h]
                following[h] = own
        qside_ref[rows, :] = dot(
            split2_cat(jnp.concatenate(query_sides, 1)), select_ref[...]
        )
    for h in range(heads):
        sent_ref[0, h] = following[h].astype(bf16)

    @pl.when(b == pl.num_programs(0) - 1)
    def _():
        width, ff = up_acc.shape
        up_rows, down_rows, mix_rows = width // size, ff // size, mix_acc.shape[0] // size
        group = size // 2
        slab = keep_ref.shape[0] // group

        def write(ref, d):
            at = d % group * slab
            for j in range(ff // TILE):
                ref[at : at + up_rows, :] = up_acc[
                    up_rows * d : up_rows * d + up_rows, TILE * j : TILE * j + TILE
                ].astype(bf16)
                at += up_rows
            ref[at : at + down_rows, :] = (
                down_acc[:, down_rows * d : down_rows * d + down_rows].T.astype(bf16)
            )
            at += down_rows
            ref[at : at + mix_rows, :] = mix_acc[
                mix_rows * d : mix_rows * d + mix_rows, :
            ].astype(bf16)

        for d in range(size):
            kept = index_ref[0] % 2 == d // group

            @pl.when(kept)
            def _(d=d):
                write(keep_ref, d)

            @pl.when(jnp.logical_not(kept))
            def _(d=d):
                write(send_ref, d)


def query_back_body(
    x_ref,
    wq_ref,
    maps_back_ref,
    ones_ref,
    phiq_ref,
    phik_ref,
    v_ref,
    dn_ref,
    row_ref,
    col_ref,
    states_ref,
    *refs,
):
    dq_ref, dphik_ref, dv_ref, wqg_ref, *ticks = refs[-7:]
    clear(ticks)
    first = jnp.logical_and(pl.program_id(0) == 0, pl.program_id(1) == 0)

    @pl.when(first)
    def _():
        wqg_ref[...] = jnp.zeros_like(wqg_ref)

    x = x_ref[...]
    query = dot(x, wq_ref[...])
    width = query.shape[1]
    ones2 = ones_ref[...]
    mask = lower_mask(True)
    low = low_lanes(CH)
    pairs = width // 128
    units = [unit(query[:, 128 * pair : 128 * pair + 128], ones2) for pair in range(pairs)]
    angle_grads = []
    for pair in range(pairs):
        heads = (2 * pair, 2 * pair + 1)
        augmented = both_augmented(v_ref[:, 128 * pair : 128 * pair + 128], low)
        phiqs = [phiq_ref[:, FW * h : FW * h + FW] for h in heads]
        phiks = [phik_ref[:, FW * h : FW * h + FW] for h in heads]
        grads = [dn_ref[:, 128 * h : 128 * h + 128] for h in heads]
        raws = [dot_nt(phik, phiq) for phik, phiq in zip(phiks, phiqs)]
        raw_grads = [dot_nt(values, grad) for values, grad in zip(augmented, grads)]
        decays = [
            jnp.exp2(
                jnp.where(
                    mask,
                    row_ref[h : h + 1, :] - col_ref[:, GR + h : GR + h + 1],
                    -jnp.inf,
                )
            )
            for h in heads
        ]
        scores = [(raw * decay).astype(bf16) for raw, decay in zip(raws, decays)]
        raw_grads = [(grad * decay).astype(bf16) for grad, decay in zip(raw_grads, decays)]
        for i, h in enumerate(heads):
            dv_ref[:, 128 * h : 128 * h + 128] = dot(scores[i], grads[i]).astype(bf16)
        for i, h in enumerate(heads):
            dphik_ref[:, FW * h : FW * h + FW] = dot(raw_grads[i], phiqs[i]).astype(bf16)
        dphis = [
            dot_tn(raw_grads[i], phiks[i])
            + col_ref[:, 4 * GR + h : 4 * GR + h + 1]
            * dot(grads[i], expand(states_ref[0, 0, h], i))
            for i, h in enumerate(heads)
        ]
        angle_grads.append(
            jnp.concatenate([angle_gradient(dphi, phi) for dphi, phi in zip(dphis, phiqs)], 1)
        )
    for pair, dq in enumerate(feature_back(units, angle_grads, maps_back_ref, ones2)):
        dq_ref[:, 128 * pair : 128 * pair + 128] = dq.astype(bf16)
    wqg_ref[...] += dot_tn(x, dq_ref[...])


def key_back_body(
    end_refs,
    x_ref,
    wq_ref,
    wkv_ref,
    maps_back_ref,
    gw_ref,
    ones_ref,
    all_ref,
    tri_ref,
    phik_ref,
    v_ref,
    dq_ref,
    dphik_ref,
    dv_ref,
    qside_ref,
    row_ref,
    col_ref,
    states_ref,
    vloc_ref,
    dr_ref,
    factor_ref,
    *refs,
):
    dx_ref, wkvg_ref, gwg_ref, gbg_ref, *ticks, grads, state_grad, sides = refs[-10:]
    clear(ticks)
    first = jnp.logical_and(pl.program_id(0) == 0, pl.program_id(1) == 0)

    @pl.when(first)
    def _():
        wkvg_ref[...] = jnp.zeros_like(wkvg_ref)
        gwg_ref[...] = jnp.zeros_like(gwg_ref)
        gbg_ref[...] = jnp.zeros_like(gbg_ref)

    @pl.when(pl.program_id(1) == 0)
    def _():
        state_grad[...] = sum(end_ref[0].astype(f32) for end_ref in end_refs)

    x = x_ref[...]
    heads = state_grad.shape[0]
    keys = dot(x, wkv_ref[:, : wq_ref.shape[1]])
    width = wq_ref.shape[1]
    ones2 = ones_ref[...]
    low = low_lanes(CH)
    weigh = jnp.where(lax.broadcasted_iota(jnp.int32, (SR, FW), 0) < HD, 1.0, 4.0)
    bounds = []
    units = [unit(keys[:, 128 * pair : 128 * pair + 128], ones2) for pair in range(heads // 2)]
    angle_grads = []
    for pair in range(heads // 2):
        lanes = slice(128 * pair, 128 * pair + 128)
        both = (2 * pair, 2 * pair + 1)
        augmented = both_augmented(v_ref[:, lanes], low)
        phiks = [phik_ref[:, FW * h : FW * h + FW] for h in both]
        tails = [col_ref[:, 2 * GR + h : 2 * GR + h + 1] for h in both]
        spreads = [expand(state_grad[h].astype(bf16), i) for i, h in enumerate(both)]
        dvs = [dot_nt(phik, spread) for phik, spread in zip(phiks, spreads)]
        dphis = [dot(values, spread) for values, spread in zip(augmented, spreads)]
        dvs = [
            dv_ref[:, 128 * h : 128 * h + 128] + tails[i] * dvs[i] for i, h in enumerate(both)
        ]
        for i, h in enumerate(both):
            sides[:, 128 * h : 128 * h + 128] = dvs[i] * augmented[i].astype(f32)
        angle_grads.append(
            jnp.concatenate(
                [
                    angle_gradient(
                        dphik_ref[:, FW * h : FW * h + FW].astype(f32) + tails[i] * dphis[i],
                        phiks[i],
                    )
                    for i, h in enumerate(both)
                ],
                1,
            )
        )
        grads[:, width + 128 * pair : width + 128 * pair + 128] = jnp.where(
            low, dvs[0], dvs[1]
        ).astype(bf16)
        for h in both:
            grad_end = state_grad[h]
            bounds.append(
                jnp.sum(grad_end * weigh * states_ref[0, 0, h].astype(f32), 0, keepdims=True)
            )
            last = jnp.exp2(row_ref[h : h + 1, CH - 1 : CH])
            state_grad[h] = last * grad_end + vloc_ref[0, 0, h]
    for pair, dk in enumerate(feature_back(units, angle_grads, maps_back_ref, ones2)):
        grads[:, 128 * pair : 128 * pair + 128] = dk.astype(bf16)
    key_side = dot(split2_cat(sides[...]), all_ref[...])
    key_row = key_side.T[:GR]
    differ = qside_ref[...].T[:GR] - key_row
    bound = jnp.sum(jnp.concatenate(bounds, 0), 1, keepdims=True)
    bound = jnp.concatenate([bound, jnp.zeros((GR - heads, 1), f32)], 0)
    grad_log = dot(split3_cat(differ), tri_ref[...]) + bound
    gate, keep = row_ref[2 * GR : 3 * GR, :], row_ref[3 * GR : 4 * GR, :]
    grad_pre = (
        grad_log * keep - gate * key_row + factor_ref[...] * gate * keep
    ).astype(bf16)
    gbg_ref[...] += grad_pre.astype(f32)
    gwg_ref[...] += dot(grad_pre, x)
    together = grads[...]
    wkvg_ref[...] += dot_tn(x, together)
    dx_ref[...] = (
        dr_ref[...]
        + dot_nt(dq_ref[...], wq_ref[...])
        + dot_nt(together, wkv_ref[...])
        + dot_tn(grad_pre, gw_ref[...])
    )


def unpack_body(index_ref, every_ref, _, up_ref, down_ref, mix_ref, tick_ref, *, places):
    rows, ff = up_ref.shape
    width = down_ref.shape[1]
    depth = every_ref.shape[1]
    slab = depth * every_ref.shape[0] // pl.num_programs(0)
    tick_ref[...] = jnp.zeros_like(tick_ref)

    def copy(first, count, ref, lanes):
        done = 0
        while done < count:
            piece, at = divmod(first + done, depth)
            number = min(count - done, depth - at)
            ref[done : done + number, lanes] = every_ref[
                places[piece], at : at + number, :
            ].astype(f32)
            done += number

    for d in range(pl.num_programs(0)):

        @pl.when(pl.program_id(0) == d)
        def _(d=d):
            first = slab * d
            for j in range(ff // TILE):
                copy(first, rows, up_ref, slice(TILE * j, TILE * j + TILE))
                first += rows
            copy(first, down_ref.shape[0], down_ref, slice(0, width))
            first += down_ref.shape[0]

            @pl.when(index_ref[0] == d)
            def _():
                copy(first, mix_ref.shape[0], mix_ref, slice(0, width))


def pack_body(key_ref, value_ref, query_ref, mix_ref, maps_ref, tail_ref, first_ref, second_ref):
    width, own = key_ref.shape
    if own == 128:
        first_ref[:width] = key_ref[...]
        first_ref[width : 2 * width] = value_ref[...]
        second_ref[:width] = query_ref[...]
        at, then = 2 * width, width
    else:
        half = width // 2
        first_ref[:width] = jnp.concatenate([key_ref[...], value_ref[...]], 1)
        second_ref[:half] = jnp.concatenate([query_ref[:half], query_ref[half:]], 1)
        at, then = width, half
    high, rest = split2(maps_ref[...] * (0.5 / math.pi))
    first_ref[at : at + own] = high
    first_ref[at + own : at + 2 * own] = rest
    first_ref[at + 2 * own :] = tail_ref[...]
    for j in range(width // 128):
        second_ref[then + own * j : then + own * j + own] = mix_ref[:, 128 * j : 128 * j + 128]


def group_body(*refs, queries, keys, order):
    query_refs, refs = refs[:queries], refs[queries:]
    key_refs, refs = refs[:keys], refs[keys:]
    gate_refs, refs = refs[:keys], refs[keys:]
    bias_refs, (vector_ref, index_ref, keep_ref, send_ref) = refs[:keys], refs[keys:]
    width = query_refs[0].shape[0]
    half, rows_all, own = keep_ref.shape
    inner = query_refs[0].shape[1]
    here = own // HD
    cuts = width // own

    def total(parts, lanes):
        value = parts[0][:, lanes]
        for part in parts[1:]:
            value = value + part[:, lanes]
        return value

    every = slice(None)
    gates = total(gate_refs, every)
    biases = jnp.sum(total(bias_refs, every), 1, keepdims=True)
    vectors = vector_ref[...]
    vectors = jnp.concatenate(
        [vectors[r : r + 1, own * j : own * j + own] for r in range(8) for j in range(cuts)], 0
    )
    at = 3 * width + GR
    used = at + 8 * cuts
    lane = lax.broadcasted_iota(jnp.int32, (1, own), 1)

    def write(out_ref, d, place):
        lanes = slice(own * d, own * d + own)
        out_ref[place, :width] = total(query_refs, lanes).astype(bf16)
        out_ref[place, width : 2 * width] = total(key_refs, lanes).astype(bf16)
        lanes = slice(inner + own * d, inner + own * d + own)
        out_ref[place, 2 * width : 3 * width] = total(key_refs, lanes).astype(bf16)
        rows = [
            gates[h : h + 1, own * j : own * j + own]
            for h in range(here * d, here * d + here)
            for j in range(cuts)
        ]
        bias = jnp.zeros((1, own), f32)
        for i in range(here):
            bias = jnp.where(lane == i, biases[here * d + i : here * d + i + 1], bias)
        rows += [bias, jnp.zeros((GR - 1 - here * cuts, own), f32)]
        out_ref[place, 3 * width : at] = jnp.concatenate(rows, 0).astype(bf16)
        out_ref[place, at:used] = vectors.astype(bf16)
        if used < rows_all:
            out_ref[place, used:] = jnp.zeros((rows_all - used, own), bf16)

    for d, place in enumerate(order):
        kept = index_ref[0] % 2 == place // half

        @pl.when(kept)
        def _(d=d, place=place):
            write(keep_ref, d, place % half)

        @pl.when(jnp.logical_not(kept))
        def _(d=d, place=place):
            write(send_ref, d, place % half)


def tokens_entry(*refs, starts, **named):
    tokens_body(refs[:starts], *refs[starts:], **named)


def key_back_entry(*refs, arrivals):
    key_back_body(refs[:arrivals], *refs[arrivals:])


def whole(array):
    zeros = (0,) * len(array.shape)
    return pl.BlockSpec(array.shape, lambda *_: zeros, pipeline_mode=pl.Buffered(1))


def fixed(shape):
    zeros = (0,) * len(shape)
    return pl.BlockSpec(shape, lambda *_: zeros)


def call(body, grid, ins, outs, previous=(), after=(), scratch=(), name=None, flops=0, room=48):
    extra = list(previous) + list(after)
    specs = [spec for _, spec in ins] + [pl.BlockSpec(memory_space=pl.ANY)] * len(extra)
    return pl.pallas_call(
        body,
        grid=grid,
        in_specs=specs,
        out_specs=[spec for _, _, spec in outs],
        out_shape=[jax.ShapeDtypeStruct(shape, kind) for shape, kind, _ in outs],
        scratch_shapes=list(scratch),
        input_output_aliases={len(ins) + i: i for i in range(len(previous))},
        compiler_params=pltpu.CompilerParams(
            dimension_semantics=("arbitrary",) * len(grid), vmem_limit_bytes=room * 1024 * 1024
        ),
        cost_estimate=pl.CostEstimate(flops=flops, bytes_accessed=4 << 20, transcendentals=0),
        name=name,
    )(*[array for array, _ in ins], *extra)


def swap(x, axis, bit):
    size = lax.axis_size(axis)
    return lax.ppermute(x, axis, [(i, i ^ bit) for i in range(size)])


def spread_head(part):
    parts = [part]
    for k in range(1, lax.axis_size("head")):
        parts.append(swap(parts[k - 1], "head", 1) if k % 2 else swap(part, "head", k))
    return parts


def place_in(axis, bit, number):
    return (lax.axis_index(axis) // bit) % number


class HalvingSum:
    def __init__(self, array):
        self.terms = [(array, 0)]
        self.length = array.shape[0]

    @classmethod
    def begun(cls, keep, send):
        sums = cls(keep)
        sums.terms.append((swap(send, "head", 1), 0))
        return sums

    def part(self, offset, tick=0.0):
        total = tick
        for array, start in self.terms:
            piece = lax.dynamic_slice_in_dim(array, start + offset, self.length, 0)
            total = total + piece.astype(f32)
        return total.astype(bf16)

    def step(self, axis, bit, number=2, tick=0.0):
        self.length //= number
        mine = place_in(axis, bit, number)
        sends = [self.part((mine ^ k) * self.length, tick) for k in range(1, number)]
        self.terms = [(array, start + mine * self.length) for array, start in self.terms]
        for k, send in enumerate(sends):
            self.terms.append((swap(send, axis, (k + 1) * bit), 0))
        return sends


def open_join(array, axis, bit, number):
    return [array] + [swap(array, axis, k * bit) for k in range(1, number)]


def close_join(parts, axis, bit):
    number = len(parts)
    mine = place_in(axis, bit, number).astype(jnp.int32)
    if number == 2:
        own, other = parts
        return jnp.where(
            mine == 0, jnp.concatenate([own, other], 0), jnp.concatenate([other, own], 0)
        )
    return jnp.concatenate(
        [
            lax.select_n(mine, *[parts[j ^ place] for place in range(number)])
            if number <= 4
            else jnp.take(jnp.stack(parts), mine ^ j, axis=0)
            for j in range(number)
        ],
        0,
    )


def gather_all(piece, stages):
    every = lax.all_gather(piece, ("dp", "head"), axis=0, tiled=False)
    names = [
        (axis, 1 << i)
        for axis in ("dp", "head")
        for i in reversed(range(lax.axis_size(axis).bit_length() - 1))
    ]
    places = np.arange(1 << len(names)).reshape((2,) * len(names))
    singles = []
    for axis, bit, number in stages:
        while number > 1:
            number //= 2
            singles.append((axis, bit * number))
    places = places.transpose([names.index(single) for single in singles]).reshape(-1)
    if piece.shape[0] % GR:
        every = every[places].reshape(1, -1, piece.shape[1])
        places = places[:1] * 0
    return every, tuple(int(place) for place in places)


def high_rest(x):
    high = lax.reduce_precision(x, 8, 7)
    return high, x - high


def per_device(
    tokens,
    cotangent,
    carry_state,
    carry_norm,
    random_maps,
    query_weight,
    key_weight,
    value_weight,
    gate_weight,
    gate_bias,
    mixing_weight,
    mixing_bias,
    norm_gain,
    norm_bias,
    up_weight,
    up_bias,
    down_weight,
    down_bias,
):
    seqs, length, width = tokens.shape
    here = gate_weight.shape[1]
    size = lax.axis_size("head")
    replicas = lax.axis_size("dp")
    index = lax.axis_index("head")
    heads = here * size
    chunks = length // CH
    blocks = seqs * chunks
    count = seqs * length
    inner_width = heads * HD
    own = here * HD
    ff = up_weight.shape[1]
    pairs = heads // 2
    head_bits = [1 << i for i in range(size.bit_length() - 1)]
    stages = (
        [("head", 1, 2), ("dp", 1, min(2, replicas))]
        + [("head", bit, 2) for bit in head_bits[1:]]
        + [("dp", 2, replicas // 2)]
    )
    index_array = index.astype(jnp.int32).reshape(1)
    smem = pl.BlockSpec(memory_space=pltpu.SMEM)

    bias_high, bias_rest = high_rest(gate_bias)
    bias_mid, bias_rest = high_rest(bias_rest)
    biases = jnp.pad(jnp.stack([bias_high, bias_mid, bias_rest]), ((0, 0), (0, 128 - here)))
    tail = jnp.concatenate([gate_weight.T.reshape(-1, 128).astype(f32), biases])
    tail = jnp.pad(tail, ((0, GR - tail.shape[0]), (0, 0)))
    tail = tail.astype(bf16)
    packing = (key_weight, value_weight, query_weight, mixing_weight, random_maps.reshape(own, NF), tail)
    first_rows = (width * here + 2 * own + GR, 128)
    second_rows = (width * here, 128)
    first_part, second_part = call(
        pack_body,
        (1,),
        [(array, fixed(array.shape)) for array in packing],
        [(first_rows, bf16, fixed(first_rows)), (second_rows, bf16, fixed(second_rows))],
        name="pack",
        room=62,
        flops=1_000_000,
    )
    first_parts = spread_head(first_part)

    begin = jnp.concatenate(
        [
            carry_state.transpose(0, 1, 3, 2),
            jnp.broadcast_to(carry_norm[:, :, None, :], (seqs, here, SR - HD, FW)),
        ],
        2,
    ).astype(bf16)

    half = np.arange(128) // HD
    ones2 = np.tile((half[:, None] == half[None, :]).astype(np.float32), (2, 1))
    ones2 = jnp.asarray(ones2, bf16)
    place = np.arange(CH)
    upto = jnp.asarray(np.tile((place[:, None] <= place[None, :]).astype(np.float32), (3, 1)), bf16)
    onward = jnp.asarray(np.tile((place[:, None] >= place[None, :]).astype(np.float32), (3, 1)), bf16)
    lane = np.arange(128)
    one_lane = np.zeros((inner_width, 128), np.float32)
    one_lane[np.arange(heads) * HD, np.arange(heads)] = 1.0
    select = jnp.asarray(np.tile(one_lane, (2, 1)), bf16)
    all_lanes = (np.arange(heads * 128) // 128)[:, None] == lane[None, :]
    all_lanes = jnp.asarray(np.tile(all_lanes.astype(np.float32), (2, 1)), bf16)

    x = tokens.reshape(count, width)
    c = cotangent.reshape(count, width)
    state_shape = (heads, SR, FW)
    tick_outs = [((1, lanes), f32, fixed((1, lanes))) for lanes in (128, FW, width)]

    def rows_of(columns, base=0, reverse=False):
        def at(b, t):
            return ((base + b) * chunks + (chunks - 1 - t if reverse else t), 0)

        return pl.BlockSpec((CH, columns), at)

    def row_spec(base=0, reverse=False):
        return pl.BlockSpec((4 * GR, CH), rows_of(0, base, reverse).index_map)

    def per_block(shape, base=0, offset=0, reverse=False):
        zeros = (0,) * len(shape)

        def at(b, t):
            return (base + b, offset + (chunks - 1 - t if reverse else t)) + zeros

        return pl.BlockSpec((1, 1) + shape, at)

    def per_seq(base=0):
        return pl.BlockSpec((1,) + state_shape, lambda b, t: (base + b, 0, 0, 0))

    weights = [
        ((width, 2 * inner_width), bf16),
        ((pairs, 3 * 128, FW), bf16),
        ((pairs, 3 * FW, 128), bf16),
        ((GR, width), bf16),
        ((inner_width, width), bf16),
        ((GR, CH), f32),
    ]
    weights = [(shape, kind, fixed(shape)) for shape, kind in weights]

    def keys_ins(base):
        return [(x, rows_of(width, base)), (ones2, whole(ones2)), (upto, whole(upto))]

    def keys_outs(base):
        total_spec = pl.BlockSpec((1, GR, 128), lambda b, t: (base + b, 0, 0))
        return [
            ((count, heads * FW), bf16, rows_of(heads * FW, base)),
            ((count, inner_width), bf16, rows_of(inner_width, base)),
            ((blocks * 4 * GR, CH), f32, row_spec(base)),
            ((count, 128), f32, rows_of(128, base)),
            ((seqs, chunks) + state_shape, f32, per_block(state_shape, base)),
            ((seqs,) + state_shape, bf16, per_seq(base)),
            ((seqs, GR, 128), f32, total_spec),
            ((GR, CH), f32, fixed((GR, CH))),
            ((1, FW), f32, fixed((1, FW))),
        ]

    *previous, gate_sums, tick, wkv, maps_front, maps_back, gw, wvt, gb = call(
        functools.partial(keys_body, size=size, here=here, skipped=2),
        (2, chunks),
        [(part, whole(part)) for part in first_parts] + [(index_array, smem)] + keys_ins(0),
        keys_outs(0) + weights,
        after=[second_part, begin],
        scratch=[
            pltpu.VMEM(state_shape, f32),
            pltpu.VMEM((size,) + first_part.shape, bf16),
        ],
        name="keys",
        flops=10_000_000_000,
    )
    second_parts = [second_part] + [swap(second_part, "head", k) for k in range(1, size)]
    begins = [jnp.where(index == 0, begin, jnp.zeros_like(begin))] + [
        lax.ppermute(begin, "head", [(k, 0)]) for k in range(1, size)
    ]
    phik, v, row, col, update, end, total, more_sums, tick = call(
        functools.partial(keys_body, size=0, here=here, skipped=2 * size - 2 + len(previous)),
        (seqs - 2, chunks),
        [(part, whole(part)) for part in (wkv, maps_front, gw, wvt, gb)] + keys_ins(2),
        keys_outs(2),
        previous=previous,
        after=second_parts[1:] + begins[1:],
        scratch=[pltpu.VMEM(state_shape, f32)],
        name="keys",
        flops=10_000_000_000,
    )
    gate_sums = lax.all_gather(
        jnp.concatenate([gate_sums, more_sums]), ("dp", "head"), axis=0, tiled=True
    )
    last = jnp.exp2(total[:, :heads, 0])[:, :, None, None]
    begin = jnp.concatenate(begins, 1)

    sent = (end.astype(f32) + last * begin.astype(f32)).astype(bf16)
    starts = []
    ticks = (0.0, 0.0, 0.0)
    phiq = intra = wq = mix = None
    previous = ()
    for step, (base, number) in enumerate(((0, 1), (1, 2), (3, 1))):
        arrived = None
        if step < size - 1:
            arrived = lax.ppermute(sent, "head", [(step, step + 1)])
            starts.append(arrived)
        main = [
            (x, rows_of(width, base)),
            (maps_front, whole(maps_front)),
            (ones2, whole(ones2)),
            (phik, rows_of(heads * FW, base)),
            (v, rows_of(inner_width, base)),
            (row, row_spec(base)),
            (col, rows_of(128, base)),
        ]
        outs = [
            ((count, heads * FW), bf16, rows_of(heads * FW, base)),
            ((count, heads * 128), f32, rows_of(heads * 128, base)),
        ] + tick_outs
        if step == 0:
            phiq, intra, *ticks, wq, mix = call(
                functools.partial(queries_body, size=size, here=here, skipped=1),
                (number, chunks),
                [(part, whole(part)) for part in second_parts] + [(index_array, smem)] + main,
                outs
                + [
                    ((width, inner_width), bf16, fixed((width, inner_width))),
                    ((inner_width, width), bf16, fixed((inner_width, width))),
                ],
                after=[sent],
                scratch=[pltpu.VMEM((size,) + second_part.shape, bf16)],
                name="queries",
                flops=5_000_000_000,
            )
        else:
            phiq, intra, *ticks = call(
                functools.partial(queries_body, size=0, here=here, skipped=3),
                (number, chunks),
                [(wq, whole(wq))] + main,
                outs,
                previous=[phiq, intra],
                after=[sent],
                name="queries",
                flops=5_000_000_000 * number,
            )
        if step < size - 2:
            sent = (last * arrived.astype(f32) + end.astype(f32) + ticks[1][0]).astype(bf16)
    for step in range(3, size - 1):
        arrived = lax.ppermute(sent, "head", [(step, step + 1)])
        starts.append(arrived)
        sent = (last * arrived.astype(f32) + end.astype(f32)).astype(bf16)

    vectors = jnp.stack([mixing_bias, norm_gain, norm_bias, down_bias] * 2)

    def seq_rows(columns):
        return pl.BlockSpec((length, columns), lambda b: (b, 0))

    def seq_block(*shape):
        zeros = (0,) * len(shape)
        return pl.BlockSpec((1,) + shape, lambda b: (b,) + zeros)

    up_bias2 = up_bias.reshape(1, ff)
    slab = (width // size) * (ff // TILE) + ff // size + own
    layer_out, dr, dn, qside, states, vloc, vdev, keep, send, vector_grads = call(
        functools.partial(
            tokens_entry, starts=len(begins) + len(starts), chunks=chunks, size=size
        ),
        (seqs,),
        [(start, seq_block(*start.shape[1:])) for start in begins + starts]
        + [
            (index_array, smem),
            (x, seq_rows(width)),
            (c, seq_rows(width)),
            (phiq, seq_rows(heads * FW)),
            (intra, seq_rows(heads * 128)),
            (
                row.reshape(blocks, 4 * GR, CH),
                pl.BlockSpec((chunks, 4 * GR, CH), lambda b: (b, 0, 0)),
            ),
            (col, seq_rows(128)),
            (update, seq_block(chunks, *state_shape)),
            (mix, whole(mix)),
            (up_weight, whole(up_weight)),
            (down_weight, whole(down_weight)),
            (vectors, whole(vectors)),
            (up_bias2, whole(up_bias2)),
            (ones2, whole(ones2)),
            (select, whole(select)),
        ],
        [
            ((count, width), bf16, seq_rows(width)),
            ((count, width), f32, seq_rows(width)),
            ((count, heads * 128), bf16, seq_rows(heads * 128)),
            ((count, 128), f32, seq_rows(128)),
            ((seqs, chunks + 1) + state_shape, bf16, seq_block(chunks + 1, *state_shape)),
            ((seqs, chunks) + state_shape, f32, seq_block(chunks, *state_shape)),
            ((seqs,) + state_shape, bf16, seq_block(*state_shape)),
            ((size // 2 * slab, width), bf16, fixed((size // 2 * slab, width))),
            ((size // 2 * slab, width), bf16, fixed((size // 2 * slab, width))),
            ((8, width), f32, fixed((8, width))),
        ],
        scratch=[
            pltpu.VMEM(state_shape, f32),
            pltpu.VMEM((length, inner_width), bf16),
            pltpu.VMEM((length, inner_width), f32),
            pltpu.VMEM((length, inner_width), f32),
            pltpu.VMEM((width, ff), f32),
            pltpu.VMEM((width, ff), f32),
            pltpu.VMEM((inner_width, width), f32),
        ],
        name="tokens",
        room=62,
        flops=50_000_000_000,
    )

    sent = vdev
    waiting = list(stages)
    sums = HalvingSum.begun(keep, send)
    ticks = (0.0, [0.0], 0.0)
    finishes = []
    dq = dphik = dv = None
    previous = []
    query_grads = []
    for step, (base, number) in enumerate(((0, 1), (1, 2), (3, 1))):
        stage = waiting.pop(0)
        after = sums.step(*stage, ticks[2]) if step else [send]
        if step < size - 1:
            arrived = lax.ppermute(sent, "head", [(size - 1 - step, size - 2 - step)])
            finishes.append(arrived)
            after.append(sent)
        dq, dphik, dv, query_grad, *ticks = call(
            query_back_body,
            (number, chunks),
            [
                (x, rows_of(width, base)),
                (wq, whole(wq)),
                (maps_back, whole(maps_back)),
                (ones2, whole(ones2)),
                (phiq, rows_of(heads * FW, base)),
                (phik, rows_of(heads * FW, base)),
                (v, rows_of(inner_width, base)),
                (dn, rows_of(heads * 128, base)),
                (row, row_spec(base)),
                (col, rows_of(128, base)),
                (states, per_block(state_shape, base)),
            ],
            [
                ((count, inner_width), bf16, rows_of(inner_width, base)),
                ((count, heads * FW), bf16, rows_of(heads * FW, base)),
                ((count, heads * 128), bf16, rows_of(heads * 128, base)),
                ((width, inner_width), f32, fixed((width, inner_width))),
            ] + tick_outs,
            previous=previous,
            after=after,
            name="query_back",
            room=48 if step else 60,
            flops=8_000_000_000 * number,
        )
        previous = [dq, dphik, dv]
        query_grads.append(query_grad)
        if step < size - 2:
            sent = (last * arrived.astype(f32) + vdev.astype(f32) + ticks[1][0]).astype(bf16)
    for step in range(3, size - 1):
        arrived = lax.ppermute(sent, "head", [(size - 1 - step, size - 2 - step)])
        finishes.append(arrived)
        sent = (last * arrived.astype(f32) + vdev.astype(f32)).astype(bf16)

    gate_total = jnp.sum(gate_sums.reshape(-1, GR, CH)[:, :heads] + ticks[1][0])
    gate_count = replicas * heads * size * count
    mean_gate = gate_total / gate_count
    factor = 2.0 * penalty_weight * (mean_gate - target_gate) / heads
    factor = jnp.broadcast_to(factor, (1, CH))

    tokens_grad = None
    previous = []
    key_value_grads, gate_grads, gate_bias_grads = [], [], []
    for base, number in ((0, 2), (2, 2)):
        after = []
        if base == 0:
            while waiting:
                after = sums.step(*waiting.pop(0), ticks[2])
        else:
            piece = sums.part(0, ticks[2])
            after = [piece]
            every, places = gather_all(piece, stages)
        tokens_grad, key_value_grad, gate_grad, gate_bias_grad, *ticks = call(
            functools.partial(key_back_entry, arrivals=len(finishes)),
            (number, chunks),
            [(finish, per_seq(base)) for finish in finishes]
            + [
                (x, rows_of(width, base, True)),
                (wq, whole(wq)),
                (wkv, whole(wkv)),
                (maps_back, whole(maps_back)),
                (gw, whole(gw)),
                (ones2, whole(ones2)),
                (all_lanes, whole(all_lanes)),
                (onward, whole(onward)),
                (phik, rows_of(heads * FW, base, True)),
                (v, rows_of(inner_width, base, True)),
                (dq, rows_of(inner_width, base, True)),
                (dphik, rows_of(heads * FW, base, True)),
                (dv, rows_of(heads * 128, base, True)),
                (qside, rows_of(128, base, True)),
                (row, row_spec(base, True)),
                (col, rows_of(128, base, True)),
                (states, per_block(state_shape, base, 1, True)),
                (vloc, per_block(state_shape, base, 0, True)),
                (dr, rows_of(width, base, True)),
                (factor, whole(factor)),
            ],
            [
                ((count, width), f32, rows_of(width, base, True)),
                ((width, 2 * inner_width), f32, fixed((width, 2 * inner_width))),
                ((GR, width), f32, fixed((GR, width))),
                ((GR, CH), f32, fixed((GR, CH))),
            ] + tick_outs,
            previous=previous,
            after=after,
            scratch=[
                pltpu.VMEM((CH, 2 * inner_width), bf16),
                pltpu.VMEM(state_shape, f32),
                pltpu.VMEM((CH, heads * 128), f32),
            ],
            name="key_back",
            room=58,
            flops=8_000_000_000 * number,
        )
        previous = [tokens_grad]
        key_value_grads.append(key_value_grad)
        gate_grads.append(gate_grad)
        gate_bias_grads.append(gate_bias_grad)
    rows = 3 * width + GR + 8 * width // own
    rows += -rows % replicas
    order = [
        sum(((d >> i) & 1) << (len(head_bits) - 1 - i) for i in range(len(head_bits)))
        for d in range(size)
    ]
    parts = query_grads + key_value_grads + gate_grads + gate_bias_grads + [vector_grads]
    group = call(
        functools.partial(
            group_body, queries=len(query_grads), keys=len(key_value_grads), order=order
        ),
        (1,),
        [(part, fixed(part.shape)) for part in parts] + [(index_array, smem)],
        [((size // 2, rows, own), bf16, fixed((size // 2, rows, own)))] * 2,
        name="group",
        room=62,
        flops=1_000_000,
    )
    group_sums = HalvingSum.begun(*[half.reshape(-1, own) for half in group])
    for bit in head_bits[1:]:
        group_sums.step("head", bit)
    across = [stage for stage in stages if stage[0] == "dp"]
    for stage in across:
        group_sums.step(*stage)
    group = group_sums.part(0)
    for axis, bit, number in reversed(across[1:]):
        group = close_join(open_join(group, axis, bit, number), axis, bit)
    group, other = open_join(group, *across[0])
    up_grad, down_grad, mixing_grad, tick = call(
        functools.partial(unpack_body, places=places),
        (size,),
        [(index_array, smem), (every, whole(every))],
        [
            ((width, ff), f32, pl.BlockSpec((width // size, ff), lambda d: (d, 0))),
            ((ff, width), f32, pl.BlockSpec((ff // size, width), lambda d: (d, 0))),
            ((own, width), f32, fixed((own, width))),
            ((1, own), f32, fixed((1, own))),
        ],
        after=[group],
        name="unpack",
        flops=1_000_000_000,
    )
    group = close_join([group + tick.astype(bf16), other], *across[0][:2])
    group = group.astype(f32)
    gate_rows = here * width // own
    gate_grad = group[3 * width : 3 * width + gate_rows].reshape(here, width).T
    at = 3 * width + GR
    vector_grads = group[at : at + 8 * width // own].reshape(8, width)
    penalty = penalty_weight * (mean_gate - target_gate) * (mean_gate - target_gate)
    return (
        layer_out.reshape(seqs, length, width),
        tokens_grad.reshape(seqs, length, width),
        penalty,
        group[:width],
        group[width : 2 * width],
        group[2 * width : 3 * width],
        gate_grad,
        group[3 * width + gate_rows, :here],
        mixing_grad,
        vector_grads[0],
        vector_grads[1],
        vector_grads[2],
        up_grad,
        vector_grads[4:].reshape(ff),
        down_grad,
        vector_grads[3],
    )


def solution(mesh):
    placed = (
        P("dp", "head", None),
        P("dp", "head", None),
        P("dp", "head", None, None),
        P("dp", "head", None),
        P("head", None, None),
        P(None, "head"),
        P(None, "head"),
        P(None, "head"),
        P(None, "head"),
        P("head"),
        P("head", None),
        P(),
        P(),
        P(),
        P(),
        P(),
        P(),
        P(),
    )
    return jax.shard_map(
        per_device,
        mesh=mesh,
        in_specs=placed,
        out_specs=(
            P("dp", "head", None),
            P("dp", "head", None),
            P(),
            P(None, "head"),
            P(None, "head"),
            P(None, "head"),
            P(None, "head"),
            P("head"),
            P("head", None),
            P(),
            P(),
            P(),
            P(),
            P(),
            P(),
            P(),
        ),
        check_vma=False,
    )
```

```python
import functools
import math

import jax
import jax.numpy as jnp
import numpy as np
from jax import lax
from jax.experimental import pallas as pl
from jax.experimental.pallas import tpu as pltpu
from jax.sharding import PartitionSpec as P

CH = 256
HD = 64
NF = 128
FW = 2 * NF
SR = 80
GR = 16
TILE = 512

penalty_weight = 32.0
target_gate = 0.9
LOG2E = 1.4426950408889634
SIN_POLY = (
    3.1415925800446116,
    -5.16770687892007,
    2.5500313771889287,
    -0.5980451736320438,
    0.07722012807955428,
)
COS_POLY = (
    0.9999999534665498,
    -4.934792858660313,
    4.058411913867723,
    -1.3318801593312537,
    0.2196967947670672,
)
GELU_A = 0.7978845608028654
GELU_B = 0.044715

f32 = jnp.float32
bf16 = jnp.bfloat16


def dot(a, b):
    return lax.dot_general(a, b, (((1,), (0,)), ((), ())), preferred_element_type=f32)


def dot_nt(a, b):
    return lax.dot_general(a, b, (((1,), (1,)), ((), ())), preferred_element_type=f32)


def dot_tn(a, b):
    return lax.dot_general(a, b, (((0,), (0,)), ((), ())), preferred_element_type=f32)


def split2(x):
    high = x.astype(bf16)
    return high, (x - high.astype(f32)).astype(bf16)


def split2_cat(x):
    return jnp.concatenate(split2(x), 1)


def split3_cat(x):
    high = x.astype(bf16)
    rest = x - high.astype(f32)
    mid = rest.astype(bf16)
    return jnp.concatenate([high, mid, (rest - mid.astype(f32)).astype(bf16)], 1)


def low_lanes(rows):
    return lax.broadcasted_iota(jnp.int32, (rows, 128), 1) < HD


def unit(u, ones2):
    inverse = lax.rsqrt(dot(split2_cat(u * u), ones2) + 1e-06)
    return u * inverse, inverse


def sin_cos(n, maps):
    high, rest = split2(n)
    turns = dot(jnp.concatenate([high, rest, high], 1), maps)
    r = turns - jnp.round(turns)
    u = r * r
    scale = math.sqrt(2.0 / math.sqrt(NF))
    s = SIN_POLY[4] * scale
    c = COS_POLY[4] * scale
    for i in (3, 2, 1, 0):
        s = s * u + SIN_POLY[i] * scale
        c = c * u + COS_POLY[i] * scale
    s = s * r
    return s * c, 1.0 / math.sqrt(NF) - s * s


def pair_features(n, maps):
    sine, cosine = sin_cos(n, maps)
    return [
        jnp.concatenate(
            [sine[:, NF * i : NF * i + NF], cosine[:, NF * i : NF * i + NF]], 1
        ).astype(bf16)
        for i in range(2)
    ]


def feature_back(units, angle_grads, maps_ref, ones2):
    splits = [split2(angle_grad) for angle_grad in angle_grads]
    dns = [
        dot(jnp.concatenate([high, rest, high], 1), maps_ref[pair])
        for pair, (high, rest) in enumerate(splits)
    ]
    radials = [dot(split2_cat(n * dn), ones2) for (n, _), dn in zip(units, dns)]
    return [
        (dn - n * radial) * inverse for (n, inverse), dn, radial in zip(units, dns, radials)
    ]


def angle_gradient(dphi, phi):
    dphi = dphi.astype(bf16).astype(f32)
    phi = phi.astype(f32)
    return dphi[:, :NF] * phi[:, NF:] - dphi[:, NF:] * phi[:, :NF]


def both_augmented(values, low):
    one = jnp.ones_like(values)
    return jnp.where(low, values, one), jnp.where(low, one, values)


def expand(block, odd):
    state, norm = block[:HD], block[HD:SR]
    parts = [norm] * (HD // (SR - HD))
    return jnp.concatenate(parts + [state] if odd else [state] + parts, 0)


def shrink(block, odd):
    if odd:
        return jnp.concatenate([block[HD:], block[HD - (SR - HD) : HD]], 0)
    return block[:SR]


def clear(refs):
    for ref in refs:
        ref[...] = jnp.zeros_like(ref)


def collect(held, parts, index):
    for k, part in enumerate(parts):
        held[index ^ k] = part[...]


def block_pair(even, odd):
    none = jnp.zeros_like(even)
    return jnp.concatenate(
        [jnp.concatenate([even, none], 1), jnp.concatenate([none, odd], 1)], 0
    )


def keys_setup(held, here, wkv_ref, wvt, maps_ref, back_ref, gw_ref, gb):
    size = held.shape[0]
    width = wkv_ref.shape[0]
    inner = wvt.shape[0]
    at = width * here
    high, rest, gates, biases = [], [], [], []
    for d in range(size):
        if here == 2:
            lanes = slice(128 * d, 128 * d + 128)
            wkv_ref[:, lanes] = held[d, :width]
            wkv_ref[:, inner + 128 * d : inner + 128 * d + 128] = held[d, width : 2 * width]
            wvt[lanes, :] = held[d, width : 2 * width].T
        elif d % 2:
            lanes = slice(64 * d - 64, 64 * d + 64)
            one, two = held[d - 1, :width], held[d, :width]
            wkv_ref[:, lanes] = jnp.concatenate([one[:, :HD], two[:, :HD]], 1)
            values = jnp.concatenate([one[:, HD:], two[:, HD:]], 1)
            wkv_ref[:, inner + 64 * d - 64 : inner + 64 * d + 64] = values
            wvt[lanes, :] = values.T
        for i in range(here):
            first = at + HD * i
            high.append(held[d, first : first + HD])
            rest.append(held[d, first + HD * here : first + HD * here + HD])
        tail = held[d, at + 2 * HD * here :].astype(f32)
        for i in range(here):
            gates.append(
                jnp.concatenate([tail[4 * i + j : 4 * i + j + 1] for j in range(width // 128)], 1)
            )
            bias = sum(tail[4 * here + j : 4 * here + j + 1, i : i + 1] for j in range(3))
            biases.append(jnp.broadcast_to(bias, (1, CH)))
    for pair in range(len(high) // 2):
        top = block_pair(high[2 * pair], high[2 * pair + 1])
        low = block_pair(rest[2 * pair], rest[2 * pair + 1])
        maps_ref[pair] = jnp.concatenate([top, top, low], 0)
        back = ((top.astype(f32) + low.astype(f32)) * (2.0 * math.pi)).T
        top, low = split2(back)
        back_ref[pair] = jnp.concatenate([top, top, low], 0)
    heads = len(gates)
    gw_ref[...] = jnp.concatenate(gates + [jnp.zeros((GR - heads, width), f32)], 0).astype(bf16)
    gb[...] = jnp.concatenate(biases + [jnp.zeros((GR - heads, CH), f32)], 0)


def keys_body(*refs, size, here, skipped):
    if size:
        parts, index_ref, refs = refs[:size], refs[size], refs[size + 1 :]
        held, refs = refs[-1], refs[:-1]
        wkv_ref, maps_ref, back_ref, gw_ref, wvt_ref, gb_ref = refs[-7:-1]
        refs = refs[:-7] + refs[-1:]
    else:
        wkv_ref, maps_ref, gw_ref, wvt_ref, gb_ref = refs[:5]
        refs = refs[5:]
    refs = refs[:3] + refs[3 + skipped :]
    (
        x_ref,
        ones_ref,
        tri_ref,
        phik_ref,
        v_ref,
        row_ref,
        col_ref,
        u_ref,
        end_ref,
        tot_ref,
        gsum_ref,
        tick_ref,
        acc,
    ) = refs
    tick_ref[...] = jnp.zeros_like(tick_ref)
    b, c = pl.program_id(0), pl.program_id(1)

    if size:

        @pl.when(jnp.logical_and(b == 0, c == 0))
        def _():
            collect(held, parts, index_ref[0])
            keys_setup(held, here, wkv_ref, wvt_ref, maps_ref, back_ref, gw_ref, gb_ref)

    x = x_ref[...]
    kv = dot(x, wkv_ref[...])
    width = kv.shape[1] // 2
    keys = kv[:, :width]
    v_ref[...] = kv[:, width:].astype(bf16)
    vt = dot_nt(wvt_ref[...], x).astype(bf16)
    pre = dot_nt(gw_ref[...], x) + gb_ref[...]
    soft = jnp.log1p(jnp.exp(-jnp.abs(pre)))
    log_gate = -(jnp.maximum(-pre, 0.0) + soft)
    log_keep = -(jnp.maximum(pre, 0.0) + soft)
    gate = jnp.exp(log_gate)
    keep = jnp.exp(log_keep)
    cumul = dot(split3_cat(log_gate * LOG2E), tri_ref[...])
    shifted = cumul - log_keep * LOG2E
    total = cumul[:, CH - 1 : CH]
    tail = jnp.exp2(total - shifted)
    row_ref[...] = jnp.concatenate([cumul, shifted, gate, keep], 0)
    stack = jnp.concatenate(
        [cumul, shifted, tail, gate, jnp.exp2(cumul), keep, keep, keep], 0
    )
    col_ref[...] = stack.T

    @pl.when(jnp.logical_and(b == 0, c == 0))
    def _():
        gsum_ref[...] = jnp.zeros_like(gsum_ref)

    gsum_ref[...] += gate

    @pl.when(c == 0)
    def _():
        acc[...] = jnp.zeros_like(acc)
        tot_ref[0] = jnp.zeros_like(tot_ref[0])

    tot_ref[0] += jnp.broadcast_to(total, tot_ref.shape[1:])
    ones2 = ones_ref[...]
    block_ones = jnp.ones((SR - HD, CH), f32)
    pairs = width // 128
    units = [unit(keys[:, 128 * pair : 128 * pair + 128], ones2) for pair in range(pairs)]
    phis = []

    def update(h):
        weighted = jnp.concatenate([vt[HD * h : HD * h + HD].astype(f32), block_ones], 0)
        weighted = (weighted * tail[h : h + 1]).astype(bf16)
        own = dot(weighted, phis[h])
        u_ref[0, 0, h] = own
        acc[h] = jnp.exp2(total[h : h + 1]) * acc[h] + own

    for pair in range(pairs):
        phis += pair_features(units[pair][0], maps_ref[pair])
        for h in (2 * pair, 2 * pair + 1):
            phik_ref[:, FW * h : FW * h + FW] = phis[h]
            if pair:
                update(h - 2)
    for h in (2 * pairs - 2, 2 * pairs - 1):
        update(h)

    @pl.when(c == pl.num_programs(1) - 1)
    def _():
        end_ref[0] = acc[...].astype(bf16)


def lower_mask(flip):
    rows = lax.broadcasted_iota(jnp.int32, (CH, CH), 0)
    columns = lax.broadcasted_iota(jnp.int32, (CH, CH), 1)
    return rows <= columns if flip else rows >= columns


def queries_setup(held, here, wq_ref, mix_ref):
    size = held.shape[0]
    width = wq_ref.shape[0]
    for d in range(size):
        at = width * here // 2
        rows = HD * here
        if here == 2:
            wq_ref[:, 128 * d : 128 * d + 128] = held[d, :width]
        elif d % 2:
            one, two = held[d - 1, :at], held[d, :at]
            lanes = slice(64 * d - 64, 64 * d + 64)
            wq_ref[:at, lanes] = jnp.concatenate([one[:, :HD], two[:, :HD]], 1)
            wq_ref[at:, lanes] = jnp.concatenate([one[:, HD:], two[:, HD:]], 1)
        for j in range(width // 128):
            mix_ref[rows * d : rows * d + rows, 128 * j : 128 * j + 128] = held[
                d, at + rows * j : at + rows * j + rows
            ]


def queries_body(*refs, size, here, skipped):
    parts, refs = refs[:size], refs[size:]
    if size:
        index_ref, refs = refs[0], refs[1:]
        held, refs = refs[-1], refs[:-1]
        wq_ref, mix_ref = refs[-2:]
        refs = refs[:-2]

        @pl.when(jnp.logical_and(pl.program_id(0) == 0, pl.program_id(1) == 0))
        def _():
            collect(held, parts, index_ref[0])
            queries_setup(held, here, wq_ref, mix_ref)

    else:
        wq_ref, refs = refs[0], refs[1:]
    x_ref, maps_ref, ones_ref, phik_ref, v_ref, row_ref, col_ref = refs[:7]
    phiq_ref, intra_ref, *ticks = refs[7 + skipped :]
    clear(ticks)
    query = dot(x_ref[...], wq_ref[...])
    width = query.shape[1]
    ones2 = ones_ref[...]
    lower = lower_mask(False)
    low = low_lanes(CH)
    pairs = width // 128
    units = [unit(query[:, 128 * pair : 128 * pair + 128], ones2) for pair in range(pairs)]

    def scores_of(pair, phis):
        heads = (2 * pair, 2 * pair + 1)
        augmented = both_augmented(v_ref[:, 128 * pair : 128 * pair + 128], low)
        raws = [dot_nt(phi, phik_ref[:, FW * h : FW * h + FW]) for phi, h in zip(phis, heads)]
        decays = [
            jnp.exp2(
                jnp.where(
                    lower,
                    col_ref[:, h : h + 1] - row_ref[GR + h : GR + h + 1, :],
                    -jnp.inf,
                )
            )
            for h in heads
        ]
        scores = [(raw * decay).astype(bf16) for raw, decay in zip(raws, decays)]
        for i, h in enumerate(heads):
            intra_ref[:, 128 * h : 128 * h + 128] = dot(scores[i], augmented[i])

    before = None
    for pair in range(pairs):
        phis = pair_features(units[pair][0], maps_ref[pair])
        for i, phi in enumerate(phis):
            h = 2 * pair + i
            phiq_ref[:, FW * h : FW * h + FW] = phi
        if before is not None:
            scores_of(pair - 1, before)
        before = phis
    scores_of(pairs - 1, before)


def tokens_body(
    start_refs,
    index_ref,
    x_ref,
    c_ref,
    phiq_ref,
    intra_ref,
    row_ref,
    col_ref,
    u_ref,
    mix_ref,
    up_ref,
    down_ref,
    vec_ref,
    upb_ref,
    ones_ref,
    select_ref,
    *refs,
    chunks,
    size,
):
    (
    out_ref,
    dr_ref,
    dn_ref,
    qside_ref,
    states_ref,
    vloc_ref,
    sent_ref,
    keep_ref,
    send_ref,
    vec_acc,
    state,
    heads_low,
    numer_all,
    inner_all,
    up_acc,
    down_acc,
    mix_acc,
    ) = refs
    b = pl.program_id(0)
    heads = state.shape[0]
    pairs = heads // 2

    @pl.when(b == 0)
    def _():
        mix_acc[...] = jnp.zeros_like(mix_acc)
        vec_acc[...] = jnp.zeros_like(vec_acc)
        up_acc[...] = jnp.zeros_like(up_acc)
        down_acc[...] = jnp.zeros_like(down_acc)

    low = low_lanes(CH)
    arrived = sum(start_ref[0].astype(f32) for start_ref in start_refs[size:])
    here = heads // size
    for d in range(size):
        part = slice(here * d, here * d + here)
        state[part] = start_refs[d][0].astype(f32) + arrived[part]
    for c in range(chunks):
        rows = slice(CH * c, CH * c + CH)
        for pair in range(pairs):
            both = (2 * pair, 2 * pair + 1)
            held = [state[h].astype(bf16) for h in both]
            carries = [
                dot_nt(phiq_ref[rows, FW * h : FW * h + FW], expand(held[i], i))
                for i, h in enumerate(both)
            ]
            for i, h in enumerate(both):
                states_ref[0, c, h] = held[i]
                last = jnp.exp2(row_ref[c, h : h + 1, CH - 1 : CH])
                state[h] = last * state[h] + u_ref[0, c, h]
            both = [
                intra_ref[rows, 128 * h : 128 * h + 128]
                + col_ref[rows, 4 * GR + h : 4 * GR + h + 1] * carry
                for h, carry in zip(both, carries)
            ]
            lanes = slice(128 * pair, 128 * pair + 128)
            numer = jnp.where(low, both[0], both[1])
            inner = pltpu.roll(jnp.where(low, both[1], both[0]), HD, 1)
            numer_all[rows, lanes] = numer
            inner_all[rows, lanes] = inner
            heads_low[rows, lanes] = (numer * lax.rsqrt(inner * inner + 1.0)).astype(bf16)
    for h in range(heads):
        states_ref[0, chunks, h] = state[h].astype(bf16)

    mix = mix_ref[...]
    rest = heads_low[...]
    mixing_bias, gain, shift, down_bias = (vec_ref[i : i + 1, :] for i in range(4))
    residual = x_ref[...].astype(f32) + dot(rest, mix) + mixing_bias
    center = residual - jnp.mean(residual, -1, keepdims=True)
    scale = lax.rsqrt(jnp.mean(center * center, -1, keepdims=True) + 1e-05)
    normal = center * scale
    normal_low = (normal * gain + shift).astype(bf16)
    normal_t = normal_low.T
    upstream = c_ref[...]
    upstream_t = upstream.T
    result = residual + down_bias
    grad_normal = jnp.zeros_like(residual)
    for j in range(up_ref.shape[1] // TILE):
        part = slice(TILE * j, TILE * j + TILE)
        up = up_ref[:, part]
        down = down_ref[part, :]
        hidden = dot(normal_low, up) + upb_ref[:, part]
        square = hidden * hidden
        th = jnp.tanh(hidden * (GELU_A + (GELU_A * GELU_B) * square))
        half = 0.5 + 0.5 * th
        active = (hidden * half).astype(bf16)
        slope = half + hidden * (0.5 - 0.5 * th * th) * (
            GELU_A + (3.0 * GELU_A * GELU_B) * square
        )
        result += dot(active, down)
        grad_hidden = slope * dot_nt(upstream, down)
        grad_hidden = grad_hidden.astype(bf16)
        vec_acc[4 + j : 5 + j, :] += jnp.sum(grad_hidden.astype(f32), 0, keepdims=True)
        grad_normal += dot_nt(grad_hidden, up)
        up_acc[:, part] += dot(normal_t, grad_hidden)
        down_acc[:, part] += dot(upstream_t, active)
    out_ref[...] = result.astype(bf16)
    upstream = upstream.astype(f32)
    dn = grad_normal * gain
    grad_residual = upstream + scale * (
        dn
        - jnp.mean(dn, -1, keepdims=True)
        - normal * jnp.mean(dn * normal, -1, keepdims=True)
    )
    dr_ref[...] = grad_residual
    for i, value in enumerate((grad_residual, grad_normal * normal, grad_normal, upstream)):
        vec_acc[i : i + 1, :] += jnp.sum(value, 0, keepdims=True)
    grad_low = grad_residual.astype(bf16)
    mix_acc[...] += dot_tn(rest, grad_low)
    grad_heads = dot_nt(grad_low, mix)

    ones2 = ones_ref[...]
    following = [None] * heads
    for c in reversed(range(chunks)):
        rows = slice(CH * c, CH * c + CH)
        grad_numers, squares, query_sides = [], [], []
        for pair in range(pairs):
            lanes = slice(128 * pair, 128 * pair + 128)
            inner = inner_all[rows, lanes]
            squares.append(1.0 / (inner * inner + 1.0))
            grad_numers.append(grad_heads[rows, lanes] * lax.rsqrt(inner * inner + 1.0))
            query_sides.append(
                dot(split2_cat(grad_numers[pair] * numer_all[rows, lanes]), ones2)
            )
        query_sides = [side * square for side, square in zip(query_sides, squares)]
        for pair in range(pairs):
            inner = inner_all[rows, 128 * pair : 128 * pair + 128]
            grad_inner = pltpu.roll(query_sides[pair] * inner * (-1.0 / HD), HD, 1)
            low_part = jnp.where(low, grad_numers[pair], grad_inner)
            high_part = jnp.where(low, grad_inner, grad_numers[pair])
            sent = []
            for h, together in ((2 * pair, low_part), (2 * pair + 1, high_part)):
                dn_ref[rows, 128 * h : 128 * h + 128] = together.astype(bf16)
                carried = col_ref[rows, 4 * GR + h : 4 * GR + h + 1]
                sent.append((carried * together).T.astype(bf16))
            for i, h in enumerate((2 * pair, 2 * pair + 1)):
                own = shrink(dot(sent[i], phiq_ref[rows, FW * h : FW * h + FW]), i)
                vloc_ref[0, c, h] = own
                if following[h] is not None:
                    last = jnp.exp2(row_ref[c, h : h + 1, CH - 1 : CH])
                    own = own + last * following[h]
                following[h] = own
        qside_ref[rows, :] = dot(
            split2_cat(jnp.concatenate(query_sides, 1)), select_ref[...]
        )
    for h in range(heads):
        sent_ref[0, h] = following[h].astype(bf16)

    @pl.when(b == pl.num_programs(0) - 1)
    def _():
        width, ff = up_acc.shape
        up_rows, down_rows, mix_rows = width // size, ff // size, mix_acc.shape[0] // size
        group = size // 2
        slab = keep_ref.shape[0] // group

        def write(ref, d):
            at = d % group * slab
            for j in range(ff // TILE):
                ref[at : at + up_rows, :] = up_acc[
                    up_rows * d : up_rows * d + up_rows, TILE * j : TILE * j + TILE
                ].astype(bf16)
                at += up_rows
            ref[at : at + down_rows, :] = (
                down_acc[:, down_rows * d : down_rows * d + down_rows].T.astype(bf16)
            )
            at += down_rows
            ref[at : at + mix_rows, :] = mix_acc[
                mix_rows * d : mix_rows * d + mix_rows, :
            ].astype(bf16)

        for d in range(size):
            kept = index_ref[0] % 2 == d // group

            @pl.when(kept)
            def _(d=d):
                write(keep_ref, d)

            @pl.when(jnp.logical_not(kept))
            def _(d=d):
                write(send_ref, d)


def query_back_body(
    x_ref,
    wq_ref,
    maps_back_ref,
    ones_ref,
    phiq_ref,
    phik_ref,
    v_ref,
    dn_ref,
    row_ref,
    col_ref,
    states_ref,
    *refs,
):
    dq_ref, dphik_ref, dv_ref, wqg_ref, *ticks = refs[-7:]
    clear(ticks)
    first = jnp.logical_and(pl.program_id(0) == 0, pl.program_id(1) == 0)

    @pl.when(first)
    def _():
        wqg_ref[...] = jnp.zeros_like(wqg_ref)

    x = x_ref[...]
    query = dot(x, wq_ref[...])
    width = query.shape[1]
    ones2 = ones_ref[...]
    mask = lower_mask(True)
    low = low_lanes(CH)
    pairs = width // 128
    units = [unit(query[:, 128 * pair : 128 * pair + 128], ones2) for pair in range(pairs)]
    angle_grads = []
    for pair in range(pairs):
        heads = (2 * pair, 2 * pair + 1)
        augmented = both_augmented(v_ref[:, 128 * pair : 128 * pair + 128], low)
        phiqs = [phiq_ref[:, FW * h : FW * h + FW] for h in heads]
        phiks = [phik_ref[:, FW * h : FW * h + FW] for h in heads]
        grads = [dn_ref[:, 128 * h : 128 * h + 128] for h in heads]
        raws = [dot_nt(phik, phiq) for phik, phiq in zip(phiks, phiqs)]
        raw_grads = [dot_nt(values, grad) for values, grad in zip(augmented, grads)]
        decays = [
            jnp.exp2(
                jnp.where(
                    mask,
                    row_ref[h : h + 1, :] - col_ref[:, GR + h : GR + h + 1],
                    -jnp.inf,
                )
            )
            for h in heads
        ]
        scores = [(raw * decay).astype(bf16) for raw, decay in zip(raws, decays)]
        raw_grads = [(grad * decay).astype(bf16) for grad, decay in zip(raw_grads, decays)]
        for i, h in enumerate(heads):
            dv_ref[:, 128 * h : 128 * h + 128] = dot(scores[i], grads[i]).astype(bf16)
        for i, h in enumerate(heads):
            dphik_ref[:, FW * h : FW * h + FW] = dot(raw_grads[i], phiqs[i]).astype(bf16)
        dphis = [
            dot_tn(raw_grads[i], phiks[i])
            + col_ref[:, 4 * GR + h : 4 * GR + h + 1]
            * dot(grads[i], expand(states_ref[0, 0, h], i))
            for i, h in enumerate(heads)
        ]
        angle_grads.append(
            jnp.concatenate([angle_gradient(dphi, phi) for dphi, phi in zip(dphis, phiqs)], 1)
        )
    for pair, dq in enumerate(feature_back(units, angle_grads, maps_back_ref, ones2)):
        dq_ref[:, 128 * pair : 128 * pair + 128] = dq.astype(bf16)
    wqg_ref[...] += dot_tn(x, dq_ref[...])


def key_back_body(
    end_refs,
    x_ref,
    wq_ref,
    wkv_ref,
    maps_back_ref,
    gw_ref,
    ones_ref,
    all_ref,
    tri_ref,
    phik_ref,
    v_ref,
    dq_ref,
    dphik_ref,
    dv_ref,
    qside_ref,
    row_ref,
    col_ref,
    states_ref,
    vloc_ref,
    dr_ref,
    factor_ref,
    *refs,
):
    dx_ref, wkvg_ref, gwg_ref, gbg_ref, *ticks, grads, state_grad, sides = refs[-10:]
    clear(ticks)
    first = jnp.logical_and(pl.program_id(0) == 0, pl.program_id(1) == 0)

    @pl.when(first)
    def _():
        wkvg_ref[...] = jnp.zeros_like(wkvg_ref)
        gwg_ref[...] = jnp.zeros_like(gwg_ref)
        gbg_ref[...] = jnp.zeros_like(gbg_ref)

    @pl.when(pl.program_id(1) == 0)
    def _():
        state_grad[...] = sum(end_ref[0].astype(f32) for end_ref in end_refs)

    x = x_ref[...]
    heads = state_grad.shape[0]
    keys = dot(x, wkv_ref[:, : wq_ref.shape[1]])
    width = wq_ref.shape[1]
    ones2 = ones_ref[...]
    low = low_lanes(CH)
    weigh = jnp.where(lax.broadcasted_iota(jnp.int32, (SR, FW), 0) < HD, 1.0, 4.0)
    bounds = []
    units = [unit(keys[:, 128 * pair : 128 * pair + 128], ones2) for pair in range(heads // 2)]
    angle_grads = []
    for pair in range(heads // 2):
        lanes = slice(128 * pair, 128 * pair + 128)
        both = (2 * pair, 2 * pair + 1)
        augmented = both_augmented(v_ref[:, lanes], low)
        phiks = [phik_ref[:, FW * h : FW * h + FW] for h in both]
        tails = [col_ref[:, 2 * GR + h : 2 * GR + h + 1] for h in both]
        spreads = [expand(state_grad[h].astype(bf16), i) for i, h in enumerate(both)]
        dvs = [dot_nt(phik, spread) for phik, spread in zip(phiks, spreads)]
        dphis = [dot(values, spread) for values, spread in zip(augmented, spreads)]
        dvs = [
            dv_ref[:, 128 * h : 128 * h + 128] + tails[i] * dvs[i] for i, h in enumerate(both)
        ]
        for i, h in enumerate(both):
            sides[:, 128 * h : 128 * h + 128] = dvs[i] * augmented[i].astype(f32)
        angle_grads.append(
            jnp.concatenate(
                [
                    angle_gradient(
                        dphik_ref[:, FW * h : FW * h + FW].astype(f32) + tails[i] * dphis[i],
                        phiks[i],
                    )
                    for i, h in enumerate(both)
                ],
                1,
            )
        )
        grads[:, width + 128 * pair : width + 128 * pair + 128] = jnp.where(
            low, dvs[0], dvs[1]
        ).astype(bf16)
        for h in both:
            grad_end = state_grad[h]
            bounds.append(
                jnp.sum(grad_end * weigh * states_ref[0, 0, h].astype(f32), 0, keepdims=True)
            )
            last = jnp.exp2(row_ref[h : h + 1, CH - 1 : CH])
            state_grad[h] = last * grad_end + vloc_ref[0, 0, h]
    key_side = dot(split2_cat(sides[...]), all_ref[...])
    key_row = key_side.T[:GR]
    differ = qside_ref[...].T[:GR] - key_row
    for pair, dk in enumerate(feature_back(units, angle_grads, maps_back_ref, ones2)):
        grads[:, 128 * pair : 128 * pair + 128] = dk.astype(bf16)
    bound = jnp.sum(jnp.concatenate(bounds, 0), 1, keepdims=True)
    bound = jnp.concatenate([bound, jnp.zeros((GR - heads, 1), f32)], 0)
    grad_log = dot(split3_cat(differ), tri_ref[...]) + bound
    gate, keep = row_ref[2 * GR : 3 * GR, :], row_ref[3 * GR : 4 * GR, :]
    grad_pre = (
        grad_log * keep - gate * key_row + factor_ref[...] * gate * keep
    ).astype(bf16)
    gbg_ref[...] += grad_pre.astype(f32)
    gwg_ref[...] += dot(grad_pre, x)
    together = grads[...]
    wkvg_ref[...] += dot_tn(x, together)
    dx_ref[...] = (
        dr_ref[...]
        + dot_nt(dq_ref[...], wq_ref[...])
        + dot_nt(together, wkv_ref[...])
        + dot_tn(grad_pre, gw_ref[...])
    )


def unpack_body(index_ref, every_ref, _, up_ref, down_ref, mix_ref, tick_ref, *, places):
    rows, ff = up_ref.shape
    width = down_ref.shape[1]
    depth = every_ref.shape[1]
    slab = depth * every_ref.shape[0] // pl.num_programs(0)
    tick_ref[...] = jnp.zeros_like(tick_ref)

    def copy(first, count, ref, lanes):
        done = 0
        while done < count:
            piece, at = divmod(first + done, depth)
            number = min(count - done, depth - at)
            ref[done : done + number, lanes] = every_ref[
                places[piece], at : at + number, :
            ].astype(f32)
            done += number

    for d in range(pl.num_programs(0)):

        @pl.when(pl.program_id(0) == d)
        def _(d=d):
            first = slab * d
            for j in range(ff // TILE):
                copy(first, rows, up_ref, slice(TILE * j, TILE * j + TILE))
                first += rows
            copy(first, down_ref.shape[0], down_ref, slice(0, width))
            first += down_ref.shape[0]

            @pl.when(index_ref[0] == d)
            def _():
                copy(first, mix_ref.shape[0], mix_ref, slice(0, width))


def pack_body(key_ref, value_ref, query_ref, mix_ref, maps_ref, tail_ref, first_ref, second_ref):
    width, own = key_ref.shape
    if own == 128:
        first_ref[:width] = key_ref[...]
        first_ref[width : 2 * width] = value_ref[...]
        second_ref[:width] = query_ref[...]
        at, then = 2 * width, width
    else:
        half = width // 2
        first_ref[:width] = jnp.concatenate([key_ref[...], value_ref[...]], 1)
        second_ref[:half] = jnp.concatenate([query_ref[:half], query_ref[half:]], 1)
        at, then = width, half
    high, rest = split2(maps_ref[...] * (0.5 / math.pi))
    first_ref[at : at + own] = high
    first_ref[at + own : at + 2 * own] = rest
    first_ref[at + 2 * own :] = tail_ref[...]
    for j in range(width // 128):
        second_ref[then + own * j : then + own * j + own] = mix_ref[:, 128 * j : 128 * j + 128]


def group_body(*refs, queries, keys, order):
    query_refs, refs = refs[:queries], refs[queries:]
    key_refs, refs = refs[:keys], refs[keys:]
    gate_refs, refs = refs[:keys], refs[keys:]
    bias_refs, (vector_ref, index_ref, keep_ref, send_ref) = refs[:keys], refs[keys:]
    width = query_refs[0].shape[0]
    half, rows_all, own = keep_ref.shape
    inner = query_refs[0].shape[1]
    here = own // HD
    cuts = width // own

    def total(parts, lanes):
        value = parts[0][:, lanes]
        for part in parts[1:]:
            value = value + part[:, lanes]
        return value

    every = slice(None)
    gates = total(gate_refs, every)
    biases = jnp.sum(total(bias_refs, every), 1, keepdims=True)
    vectors = vector_ref[...]
    vectors = jnp.concatenate(
        [vectors[r : r + 1, own * j : own * j + own] for r in range(8) for j in range(cuts)], 0
    )
    at = 3 * width + GR
    used = at + 8 * cuts
    lane = lax.broadcasted_iota(jnp.int32, (1, own), 1)

    def write(out_ref, d, place):
        lanes = slice(own * d, own * d + own)
        out_ref[place, :width] = total(query_refs, lanes).astype(bf16)
        out_ref[place, width : 2 * width] = total(key_refs, lanes).astype(bf16)
        lanes = slice(inner + own * d, inner + own * d + own)
        out_ref[place, 2 * width : 3 * width] = total(key_refs, lanes).astype(bf16)
        rows = [
            gates[h : h + 1, own * j : own * j + own]
            for h in range(here * d, here * d + here)
            for j in range(cuts)
        ]
        bias = jnp.zeros((1, own), f32)
        for i in range(here):
            bias = jnp.where(lane == i, biases[here * d + i : here * d + i + 1], bias)
        rows += [bias, jnp.zeros((GR - 1 - here * cuts, own), f32)]
        out_ref[place, 3 * width : at] = jnp.concatenate(rows, 0).astype(bf16)
        out_ref[place, at:used] = vectors.astype(bf16)
        if used < rows_all:
            out_ref[place, used:] = jnp.zeros((rows_all - used, own), bf16)

    for d, place in enumerate(order):
        kept = index_ref[0] % 2 == place // half

        @pl.when(kept)
        def _(d=d, place=place):
            write(keep_ref, d, place % half)

        @pl.when(jnp.logical_not(kept))
        def _(d=d, place=place):
            write(send_ref, d, place % half)


def tokens_entry(*refs, starts, **named):
    tokens_body(refs[:starts], *refs[starts:], **named)


def key_back_entry(*refs, arrivals):
    key_back_body(refs[:arrivals], *refs[arrivals:])


def whole(array):
    zeros = (0,) * len(array.shape)
    return pl.BlockSpec(array.shape, lambda *_: zeros, pipeline_mode=pl.Buffered(1))


def fixed(shape):
    zeros = (0,) * len(shape)
    return pl.BlockSpec(shape, lambda *_: zeros)


def call(body, grid, ins, outs, previous=(), after=(), scratch=(), name=None, flops=0, room=48):
    extra = list(previous) + list(after)
    specs = [spec for _, spec in ins] + [pl.BlockSpec(memory_space=pl.ANY)] * len(extra)
    return pl.pallas_call(
        body,
        grid=grid,
        in_specs=specs,
        out_specs=[spec for _, _, spec in outs],
        out_shape=[jax.ShapeDtypeStruct(shape, kind) for shape, kind, _ in outs],
        scratch_shapes=list(scratch),
        input_output_aliases={len(ins) + i: i for i in range(len(previous))},
        compiler_params=pltpu.CompilerParams(
            dimension_semantics=("arbitrary",) * len(grid), vmem_limit_bytes=room * 1024 * 1024
        ),
        cost_estimate=pl.CostEstimate(flops=flops, bytes_accessed=4 << 20, transcendentals=0),
        name=name,
    )(*[array for array, _ in ins], *extra)


def swap(x, axis, bit):
    size = lax.axis_size(axis)
    return lax.ppermute(x, axis, [(i, i ^ bit) for i in range(size)])


def spread_head(part):
    parts = [part]
    for k in range(1, lax.axis_size("head")):
        parts.append(swap(parts[k - 1], "head", 1) if k % 2 else swap(part, "head", k))
    return parts


def place_in(axis, bit, number):
    return (lax.axis_index(axis) // bit) % number


class HalvingSum:
    def __init__(self, array):
        self.terms = [(array, 0)]
        self.length = array.shape[0]

    @classmethod
    def begun(cls, keep, send):
        sums = cls(keep)
        sums.terms.append((swap(send, "head", 1), 0))
        return sums

    def part(self, offset, tick=0.0):
        total = tick
        for array, start in self.terms:
            piece = lax.dynamic_slice_in_dim(array, start + offset, self.length, 0)
            total = total + piece.astype(f32)
        return total.astype(bf16)

    def step(self, axis, bit, number=2, tick=0.0):
        self.length //= number
        mine = place_in(axis, bit, number)
        sends = [self.part((mine ^ k) * self.length, tick) for k in range(1, number)]
        self.terms = [(array, start + mine * self.length) for array, start in self.terms]
        for k, send in enumerate(sends):
            self.terms.append((swap(send, axis, (k + 1) * bit), 0))
        return sends


def open_join(array, axis, bit, number):
    return [array] + [swap(array, axis, k * bit) for k in range(1, number)]


def close_join(parts, axis, bit):
    number = len(parts)
    mine = place_in(axis, bit, number).astype(jnp.int32)
    if number == 2:
        own, other = parts
        return jnp.where(
            mine == 0, jnp.concatenate([own, other], 0), jnp.concatenate([other, own], 0)
        )
    return jnp.concatenate(
        [
            lax.select_n(mine, *[parts[j ^ place] for place in range(number)])
            if number <= 4
            else jnp.take(jnp.stack(parts), mine ^ j, axis=0)
            for j in range(number)
        ],
        0,
    )


def gather_all(piece, stages):
    every = lax.all_gather(piece, ("dp", "head"), axis=0, tiled=False)
    names = [
        (axis, 1 << i)
        for axis in ("dp", "head")
        for i in reversed(range(lax.axis_size(axis).bit_length() - 1))
    ]
    places = np.arange(1 << len(names)).reshape((2,) * len(names))
    singles = []
    for axis, bit, number in stages:
        while number > 1:
            number //= 2
            singles.append((axis, bit * number))
    places = places.transpose([names.index(single) for single in singles]).reshape(-1)
    if piece.shape[0] % GR:
        every = every[places].reshape(1, -1, piece.shape[1])
        places = places[:1] * 0
    return every, tuple(int(place) for place in places)


def high_rest(x):
    high = lax.reduce_precision(x, 8, 7)
    return high, x - high


def per_device(
    tokens,
    cotangent,
    carry_state,
    carry_norm,
    random_maps,
    query_weight,
    key_weight,
    value_weight,
    gate_weight,
    gate_bias,
    mixing_weight,
    mixing_bias,
    norm_gain,
    norm_bias,
    up_weight,
    up_bias,
    down_weight,
    down_bias,
):
    seqs, length, width = tokens.shape
    here = gate_weight.shape[1]
    size = lax.axis_size("head")
    replicas = lax.axis_size("dp")
    index = lax.axis_index("head")
    heads = here * size
    chunks = length // CH
    blocks = seqs * chunks
    count = seqs * length
    inner_width = heads * HD
    own = here * HD
    ff = up_weight.shape[1]
    pairs = heads // 2
    head_bits = [1 << i for i in range(size.bit_length() - 1)]
    stages = (
        [("head", 1, 2), ("dp", 1, min(2, replicas))]
        + [("head", bit, 2) for bit in head_bits[1:]]
        + [("dp", 2, replicas // 2)]
    )
    index_array = index.astype(jnp.int32).reshape(1)
    smem = pl.BlockSpec(memory_space=pltpu.SMEM)

    bias_high, bias_rest = high_rest(gate_bias)
    bias_mid, bias_rest = high_rest(bias_rest)
    biases = jnp.pad(jnp.stack([bias_high, bias_mid, bias_rest]), ((0, 0), (0, 128 - here)))
    tail = jnp.concatenate([gate_weight.T.reshape(-1, 128).astype(f32), biases])
    tail = jnp.pad(tail, ((0, GR - tail.shape[0]), (0, 0)))
    tail = tail.astype(bf16)
    packing = (key_weight, value_weight, query_weight, mixing_weight, random_maps.reshape(own, NF), tail)
    first_rows = (width * here + 2 * own + GR, 128)
    second_rows = (width * here, 128)
    first_part, second_part = call(
        pack_body,
        (1,),
        [(array, fixed(array.shape)) for array in packing],
        [(first_rows, bf16, fixed(first_rows)), (second_rows, bf16, fixed(second_rows))],
        name="pack",
        room=62,
        flops=1_000_000,
    )
    first_parts = spread_head(first_part)

    begin = jnp.concatenate(
        [
            carry_state.transpose(0, 1, 3, 2),
            jnp.broadcast_to(carry_norm[:, :, None, :], (seqs, here, SR - HD, FW)),
        ],
        2,
    ).astype(bf16)

    half = np.arange(128) // HD
    ones2 = np.tile((half[:, None] == half[None, :]).astype(np.float32), (2, 1))
    ones2 = jnp.asarray(ones2, bf16)
    place = np.arange(CH)
    upto = jnp.asarray(np.tile((place[:, None] <= place[None, :]).astype(np.float32), (3, 1)), bf16)
    onward = jnp.asarray(np.tile((place[:, None] >= place[None, :]).astype(np.float32), (3, 1)), bf16)
    lane = np.arange(128)
    one_lane = np.zeros((inner_width, 128), np.float32)
    one_lane[np.arange(heads) * HD, np.arange(heads)] = 1.0
    select = jnp.asarray(np.tile(one_lane, (2, 1)), bf16)
    all_lanes = (np.arange(heads * 128) // 128)[:, None] == lane[None, :]
    all_lanes = jnp.asarray(np.tile(all_lanes.astype(np.float32), (2, 1)), bf16)

    x = tokens.reshape(count, width)
    c = cotangent.reshape(count, width)
    state_shape = (heads, SR, FW)
    tick_outs = [((1, lanes), f32, fixed((1, lanes))) for lanes in (128, FW, width)]

    def rows_of(columns, base=0, reverse=False):
        def at(b, t):
            return ((base + b) * chunks + (chunks - 1 - t if reverse else t), 0)

        return pl.BlockSpec((CH, columns), at)

    def row_spec(base=0, reverse=False):
        return pl.BlockSpec((4 * GR, CH), rows_of(0, base, reverse).index_map)

    def per_block(shape, base=0, offset=0, reverse=False):
        zeros = (0,) * len(shape)

        def at(b, t):
            return (base + b, offset + (chunks - 1 - t if reverse else t)) + zeros

        return pl.BlockSpec((1, 1) + shape, at)

    def per_seq(base=0):
        return pl.BlockSpec((1,) + state_shape, lambda b, t: (base + b, 0, 0, 0))

    weights = [
        ((width, 2 * inner_width), bf16),
        ((pairs, 3 * 128, FW), bf16),
        ((pairs, 3 * FW, 128), bf16),
        ((GR, width), bf16),
        ((inner_width, width), bf16),
        ((GR, CH), f32),
    ]
    weights = [(shape, kind, fixed(shape)) for shape, kind in weights]

    def keys_ins(base):
        return [(x, rows_of(width, base)), (ones2, whole(ones2)), (upto, whole(upto))]

    def keys_outs(base):
        total_spec = pl.BlockSpec((1, GR, 128), lambda b, t: (base + b, 0, 0))
        return [
            ((count, heads * FW), bf16, rows_of(heads * FW, base)),
            ((count, inner_width), bf16, rows_of(inner_width, base)),
            ((blocks * 4 * GR, CH), f32, row_spec(base)),
            ((count, 128), f32, rows_of(128, base)),
            ((seqs, chunks) + state_shape, f32, per_block(state_shape, base)),
            ((seqs,) + state_shape, bf16, per_seq(base)),
            ((seqs, GR, 128), f32, total_spec),
            ((GR, CH), f32, fixed((GR, CH))),
            ((1, FW), f32, fixed((1, FW))),
        ]

    *previous, gate_sums, tick, wkv, maps_front, maps_back, gw, wvt, gb = call(
        functools.partial(keys_body, size=size, here=here, skipped=2),
        (2, chunks),
        [(part, whole(part)) for part in first_parts] + [(index_array, smem)] + keys_ins(0),
        keys_outs(0) + weights,
        after=[second_part, begin],
        scratch=[
            pltpu.VMEM(state_shape, f32),
            pltpu.VMEM((size,) + first_part.shape, bf16),
        ],
        name="keys",
        flops=10_000_000_000,
    )
    second_parts = [second_part] + [swap(second_part, "head", k) for k in range(1, size)]
    begins = [jnp.where(index == 0, begin, jnp.zeros_like(begin))] + [
        lax.ppermute(begin, "head", [(k, 0)]) for k in range(1, size)
    ]
    phik, v, row, col, update, end, total, more_sums, tick = call(
        functools.partial(keys_body, size=0, here=here, skipped=2 * size - 2 + len(previous)),
        (seqs - 2, chunks),
        [(part, whole(part)) for part in (wkv, maps_front, gw, wvt, gb)] + keys_ins(2),
        keys_outs(2),
        previous=previous,
        after=second_parts[1:] + begins[1:],
        scratch=[pltpu.VMEM(state_shape, f32)],
        name="keys",
        flops=10_000_000_000,
    )
    gate_sums = lax.all_gather(
        jnp.concatenate([gate_sums, more_sums]), ("dp", "head"), axis=0, tiled=True
    )
    last = jnp.exp2(total[:, :heads, 0])[:, :, None, None]
    begin = jnp.concatenate(begins, 1)

    sent = (end.astype(f32) + last * begin.astype(f32)).astype(bf16)
    starts = []
    ticks = (0.0, 0.0, 0.0)
    phiq = intra = wq = mix = None
    previous = ()
    for step, (base, number) in enumerate(((0, 1), (1, 2), (3, 1))):
        arrived = None
        if step < size - 1:
            arrived = lax.ppermute(sent, "head", [(step, step + 1)])
            starts.append(arrived)
        main = [
            (x, rows_of(width, base)),
            (maps_front, whole(maps_front)),
            (ones2, whole(ones2)),
            (phik, rows_of(heads * FW, base)),
            (v, rows_of(inner_width, base)),
            (row, row_spec(base)),
            (col, rows_of(128, base)),
        ]
        outs = [
            ((count, heads * FW), bf16, rows_of(heads * FW, base)),
            ((count, heads * 128), f32, rows_of(heads * 128, base)),
        ] + tick_outs
        if step == 0:
            phiq, intra, *ticks, wq, mix = call(
                functools.partial(queries_body, size=size, here=here, skipped=1),
                (number, chunks),
                [(part, whole(part)) for part in second_parts] + [(index_array, smem)] + main,
                outs
                + [
                    ((width, inner_width), bf16, fixed((width, inner_width))),
                    ((inner_width, width), bf16, fixed((inner_width, width))),
                ],
                after=[sent],
                scratch=[pltpu.VMEM((size,) + second_part.shape, bf16)],
                name="queries",
                flops=5_000_000_000,
            )
        else:
            phiq, intra, *ticks = call(
                functools.partial(queries_body, size=0, here=here, skipped=3),
                (number, chunks),
                [(wq, whole(wq))] + main,
                outs,
                previous=[phiq, intra],
                after=[sent],
                name="queries",
                flops=5_000_000_000 * number,
            )
        if step < size - 2:
            sent = (last * arrived.astype(f32) + end.astype(f32) + ticks[1][0]).astype(bf16)
    for step in range(3, size - 1):
        arrived = lax.ppermute(sent, "head", [(step, step + 1)])
        starts.append(arrived)
        sent = (last * arrived.astype(f32) + end.astype(f32)).astype(bf16)

    vectors = jnp.stack([mixing_bias, norm_gain, norm_bias, down_bias] * 2)

    def seq_rows(columns):
        return pl.BlockSpec((length, columns), lambda b: (b, 0))

    def seq_block(*shape):
        zeros = (0,) * len(shape)
        return pl.BlockSpec((1,) + shape, lambda b: (b,) + zeros)

    up_bias2 = up_bias.reshape(1, ff)
    slab = (width // size) * (ff // TILE) + ff // size + own
    layer_out, dr, dn, qside, states, vloc, vdev, keep, send, vector_grads = call(
        functools.partial(
            tokens_entry, starts=len(begins) + len(starts), chunks=chunks, size=size
        ),
        (seqs,),
        [(start, seq_block(*start.shape[1:])) for start in begins + starts]
        + [
            (index_array, smem),
            (x, seq_rows(width)),
            (c, seq_rows(width)),
            (phiq, seq_rows(heads * FW)),
            (intra, seq_rows(heads * 128)),
            (
                row.reshape(blocks, 4 * GR, CH),
                pl.BlockSpec((chunks, 4 * GR, CH), lambda b: (b, 0, 0)),
            ),
            (col, seq_rows(128)),
            (update, seq_block(chunks, *state_shape)),
            (mix, whole(mix)),
            (up_weight, whole(up_weight)),
            (down_weight, whole(down_weight)),
            (vectors, whole(vectors)),
            (up_bias2, whole(up_bias2)),
            (ones2, whole(ones2)),
            (select, whole(select)),
        ],
        [
            ((count, width), bf16, seq_rows(width)),
            ((count, width), f32, seq_rows(width)),
            ((count, heads * 128), bf16, seq_rows(heads * 128)),
            ((count, 128), f32, seq_rows(128)),
            ((seqs, chunks + 1) + state_shape, bf16, seq_block(chunks + 1, *state_shape)),
            ((seqs, chunks) + state_shape, f32, seq_block(chunks, *state_shape)),
            ((seqs,) + state_shape, bf16, seq_block(*state_shape)),
            ((size // 2 * slab, width), bf16, fixed((size // 2 * slab, width))),
            ((size // 2 * slab, width), bf16, fixed((size // 2 * slab, width))),
            ((8, width), f32, fixed((8, width))),
        ],
        scratch=[
            pltpu.VMEM(state_shape, f32),
            pltpu.VMEM((length, inner_width), bf16),
            pltpu.VMEM((length, inner_width), f32),
            pltpu.VMEM((length, inner_width), f32),
            pltpu.VMEM((width, ff), f32),
            pltpu.VMEM((width, ff), f32),
            pltpu.VMEM((inner_width, width), f32),
        ],
        name="tokens",
        room=62,
        flops=50_000_000_000,
    )

    sent = vdev
    waiting = list(stages)
    sums = HalvingSum.begun(keep, send)
    ticks = (0.0, [0.0], 0.0)
    finishes = []
    dq = dphik = dv = None
    previous = []
    query_grads = []
    for step, (base, number) in enumerate(((0, 1), (1, 2), (3, 1))):
        stage = waiting.pop(0)
        after = sums.step(*stage, ticks[2]) if step else [send]
        if step < size - 1:
            arrived = lax.ppermute(sent, "head", [(size - 1 - step, size - 2 - step)])
            finishes.append(arrived)
            after.append(sent)
        dq, dphik, dv, query_grad, *ticks = call(
            query_back_body,
            (number, chunks),
            [
                (x, rows_of(width, base)),
                (wq, whole(wq)),
                (maps_back, whole(maps_back)),
                (ones2, whole(ones2)),
                (phiq, rows_of(heads * FW, base)),
                (phik, rows_of(heads * FW, base)),
                (v, rows_of(inner_width, base)),
                (dn, rows_of(heads * 128, base)),
                (row, row_spec(base)),
                (col, rows_of(128, base)),
                (states, per_block(state_shape, base)),
            ],
            [
                ((count, inner_width), bf16, rows_of(inner_width, base)),
                ((count, heads * FW), bf16, rows_of(heads * FW, base)),
                ((count, heads * 128), bf16, rows_of(heads * 128, base)),
                ((width, inner_width), f32, fixed((width, inner_width))),
            ] + tick_outs,
            previous=previous,
            after=after,
            name="query_back",
            room=48 if step else 60,
            flops=8_000_000_000 * number,
        )
        previous = [dq, dphik, dv]
        query_grads.append(query_grad)
        if step < size - 2:
            sent = (last * arrived.astype(f32) + vdev.astype(f32) + ticks[1][0]).astype(bf16)
    for step in range(3, size - 1):
        arrived = lax.ppermute(sent, "head", [(size - 1 - step, size - 2 - step)])
        finishes.append(arrived)
        sent = (last * arrived.astype(f32) + vdev.astype(f32)).astype(bf16)

    gate_total = jnp.sum(gate_sums.reshape(-1, GR, CH)[:, :heads] + ticks[1][0])
    gate_count = replicas * heads * size * count
    mean_gate = gate_total / gate_count
    factor = 2.0 * penalty_weight * (mean_gate - target_gate) / heads
    factor = jnp.broadcast_to(factor, (1, CH))

    tokens_grad = None
    previous = []
    key_value_grads, gate_grads, gate_bias_grads = [], [], []
    for base, number in ((0, 2), (2, 2)):
        after = []
        if base == 0:
            while waiting:
                after = sums.step(*waiting.pop(0), ticks[2])
        else:
            piece = sums.part(0, ticks[2])
            after = [piece]
            every, places = gather_all(piece, stages)
        tokens_grad, key_value_grad, gate_grad, gate_bias_grad, *ticks = call(
            functools.partial(key_back_entry, arrivals=len(finishes)),
            (number, chunks),
            [(finish, per_seq(base)) for finish in finishes]
            + [
                (x, rows_of(width, base, True)),
                (wq, whole(wq)),
                (wkv, whole(wkv)),
                (maps_back, whole(maps_back)),
                (gw, whole(gw)),
                (ones2, whole(ones2)),
                (all_lanes, whole(all_lanes)),
                (onward, whole(onward)),
                (phik, rows_of(heads * FW, base, True)),
                (v, rows_of(inner_width, base, True)),
                (dq, rows_of(inner_width, base, True)),
                (dphik, rows_of(heads * FW, base, True)),
                (dv, rows_of(heads * 128, base, True)),
                (qside, rows_of(128, base, True)),
                (row, row_spec(base, True)),
                (col, rows_of(128, base, True)),
                (states, per_block(state_shape, base, 1, True)),
                (vloc, per_block(state_shape, base, 0, True)),
                (dr, rows_of(width, base, True)),
                (factor, whole(factor)),
            ],
            [
                ((count, width), f32, rows_of(width, base, True)),
                ((width, 2 * inner_width), f32, fixed((width, 2 * inner_width))),
                ((GR, width), f32, fixed((GR, width))),
                ((GR, CH), f32, fixed((GR, CH))),
            ] + tick_outs,
            previous=previous,
            after=after,
            scratch=[
                pltpu.VMEM((CH, 2 * inner_width), bf16),
                pltpu.VMEM(state_shape, f32),
                pltpu.VMEM((CH, heads * 128), f32),
            ],
            name="key_back",
            room=58,
            flops=8_000_000_000 * number,
        )
        previous = [tokens_grad]
        key_value_grads.append(key_value_grad)
        gate_grads.append(gate_grad)
        gate_bias_grads.append(gate_bias_grad)
    rows = 3 * width + GR + 8 * width // own
    rows += -rows % replicas
    order = [
        sum(((d >> i) & 1) << (len(head_bits) - 1 - i) for i in range(len(head_bits)))
        for d in range(size)
    ]
    parts = query_grads + key_value_grads + gate_grads + gate_bias_grads + [vector_grads]
    group = call(
        functools.partial(
            group_body, queries=len(query_grads), keys=len(key_value_grads), order=order
        ),
        (1,),
        [(part, fixed(part.shape)) for part in parts] + [(index_array, smem)],
        [((size // 2, rows, own), bf16, fixed((size // 2, rows, own)))] * 2,
        name="group",
        room=62,
        flops=1_000_000,
    )
    group_sums = HalvingSum.begun(*[half.reshape(-1, own) for half in group])
    for bit in head_bits[1:]:
        group_sums.step("head", bit)
    across = [stage for stage in stages if stage[0] == "dp"]
    for stage in across:
        group_sums.step(*stage)
    group = group_sums.part(0)
    for axis, bit, number in reversed(across[1:]):
        group = close_join(open_join(group, axis, bit, number), axis, bit)
    group, other = open_join(group, *across[0])
    up_grad, down_grad, mixing_grad, tick = call(
        functools.partial(unpack_body, places=places),
        (size,),
        [(index_array, smem), (every, whole(every))],
        [
            ((width, ff), f32, pl.BlockSpec((width // size, ff), lambda d: (d, 0))),
            ((ff, width), f32, pl.BlockSpec((ff // size, width), lambda d: (d, 0))),
            ((own, width), f32, fixed((own, width))),
            ((1, own), f32, fixed((1, own))),
        ],
        after=[group],
        name="unpack",
        flops=1_000_000_000,
    )
    group = close_join([group + tick.astype(bf16), other], *across[0][:2])
    group = group.astype(f32)
    gate_rows = here * width // own
    gate_grad = group[3 * width : 3 * width + gate_rows].reshape(here, width).T
    at = 3 * width + GR
    vector_grads = group[at : at + 8 * width // own].reshape(8, width)
    penalty = penalty_weight * (mean_gate - target_gate) * (mean_gate - target_gate)
    return (
        layer_out.reshape(seqs, length, width),
        tokens_grad.reshape(seqs, length, width),
        penalty,
        group[:width],
        group[width : 2 * width],
        group[2 * width : 3 * width],
        gate_grad,
        group[3 * width + gate_rows, :here],
        mixing_grad,
        vector_grads[0],
        vector_grads[1],
        vector_grads[2],
        up_grad,
        vector_grads[4:].reshape(ff),
        down_grad,
        vector_grads[3],
    )


def solution(mesh):
    placed = (
        P("dp", "head", None),
        P("dp", "head", None),
        P("dp", "head", None, None),
        P("dp", "head", None),
        P("head", None, None),
        P(None, "head"),
        P(None, "head"),
        P(None, "head"),
        P(None, "head"),
        P("head"),
        P("head", None),
        P(),
        P(),
        P(),
        P(),
        P(),
        P(),
        P(),
    )
    return jax.shard_map(
        per_device,
        mesh=mesh,
        in_specs=placed,
        out_specs=(
            P("dp", "head", None),
            P("dp", "head", None),
            P(),
            P(None, "head"),
            P(None, "head"),
            P(None, "head"),
            P(None, "head"),
            P("head"),
            P("head", None),
            P(),
            P(),
            P(),
            P(),
            P(),
            P(),
            P(),
        ),
        check_vma=False,
    )
```
